32 devices in a mesh: ctx: 8 (over z, x), fsdp: 4 (over y, core).
Axes of the slice: x: 2, y: 2, z: 4, core: 2. Of those that a mesh axis runs over, the one named last changes fastest.
Arguments:
- streams: bfloat16 [4, 1024, 8192], P('fsdp', 'ctx'), may hold values from -6 to 6
- cotangent: bfloat16 [4, 1024, 8192], P('fsdp', 'ctx'), may hold values from -6 to 6
- w_qkv: bfloat16 [2048, 6144], P(('ctx', 'fsdp')), may hold values from -0.125 to 0.125
- w_out: bfloat16 [2048, 2048], P(('ctx', 'fsdp')), may hold values from -0.5 to 0.5
- w_gate_up: bfloat16 [2048, 16384], P(('ctx', 'fsdp')), may hold values from -0.125 to 0.125
- w_down: bfloat16 [8192, 2048], P(('ctx', 'fsdp')), may hold values from -0.0625 to 0.0625
- hc_weight: float32 [2, 2048, 6], replicated, may hold values from -0.125 to 0.125
- hc_static: float32 [2, 4, 6], replicated, may hold values from 0.2 to 0.8
- seq_lengths: int32 [4, 4], replicated, may hold values from 1 to 960, 1024 in all within a row
- pair_perm: int32 [4, 8], replicated, may hold values from 0 to 7, each once within a row
Outputs:
- out_streams: bfloat16 [4, 1024, 8192], P('fsdp', 'ctx')
- grad_streams: bfloat16 [4, 1024, 8192], P('fsdp', 'ctx')
- grad_qkv: float32 [2048, 6144], P(('ctx', 'fsdp'))
- grad_out: float32 [2048, 2048], P(('ctx', 'fsdp'))
- grad_gate_up: float32 [2048, 16384], P(('ctx', 'fsdp'))
- grad_down: float32 [8192, 2048], P(('ctx', 'fsdp'))
- grad_hc_weight: float32 [2, 2048, 6], replicated
- grad_hc_static: float32 [2, 4, 6], replicated
The draws below stay inside these ranges and needn't reach their ends.
Inputs may be any that keep to these rules, and one draw needn't show every extreme that they name: `seq_lengths`: the lengths of a group sum to 1024; the longest is 960. `pair_perm`: each row is a permutation.
All inputs are finite; a program needn't handle non-finite values.
Results may differ from the reference program's by a relative error of at most 0.039.
Values may be sent and summed in bfloat16 or wider, within the bound.
No kernel may reach another device: no remote copies, remote signals or barrier semaphores. Data moves between devices by JAX's collectives and lax.ppermute only.
A program may use at most 512 MiB of HBM per device.

```python
import math
import jax
import jax.numpy as jnp
import numpy as np
from jax import lax

D = 2048
HEADS = 16
HEAD_DIM = 128
FF = 8192
STREAMS = 4
SEQS = 4
TOK_DEV = 128
BLOCK = 64
GROUP_TOK = 1024
N_CTX = 8
N_FSDP = 4


def steps_of(rng, dims, pieces, low, top_value):
    loudness = 1.0
    for axis_at, blocks in pieces:
        draws = jax.random.uniform(jax.random.fold_in(jax.random.fold_in(rng, 6), axis_at), (blocks,), jnp.float32, low / len(pieces), top_value / len(pieces))
        loudness = loudness * jnp.repeat(jnp.exp(draws), dims[axis_at] // blocks).reshape((-1,) + (1,) * (len(dims) - 1 - axis_at))
    return loudness


def profile(amount, total, most, lean):
    loads = [(1 << 20) // math.isqrt(standing ** lean) + 1 for standing in range(2, amount + 1)]
    spare, holding = total - most - (amount - 1), [1] * (amount - 1)
    while spare > 0:
        movable = [i for i in range(amount - 1) if holding[i] < most]
        pool, remaining = sum([loads[i] for i in movable]), spare
        for i in movable:
            more = min(most - holding[i], max(1, remaining * loads[i] // pool), spare)
            holding[i] = holding[i] + more
            spare = spare - more
    return np.array([most] + holding)


def uneven(own_key, count, total, bound, lean):
    if count == 2:
        one = jax.random.randint(own_key, (), max(1, total - bound), min(bound, total - 1) + 1)
        return jnp.stack([one, total - one])
    tallies = jnp.asarray(profile(count, total, bound, lean), jnp.int32)
    pairs = (count - 1) // 2
    giver, receiver = tallies[1:1 + 2 * pairs:2], tallies[2:2 + 2 * pairs:2]
    margin = jnp.minimum(giver - 1, bound - receiver)
    moved = jax.random.randint(jax.random.fold_in(own_key, 1), (pairs,), 0, 1 << 20) % (margin + 1)
    tallies = tallies.at[1:1 + 2 * pairs:2].set(giver - moved).at[2:2 + 2 * pairs:2].set(receiver + moved)
    return tallies[jax.random.permutation(jax.random.fold_in(own_key, 2), count)]


def centred(own_key, dims, width, bound, shards=(), held_as=jnp.bfloat16):
    values = width * jax.random.normal(own_key, dims, jnp.float32)
    if shards:
        values = values * steps_of(own_key, dims, shards, -0.22, 0.18)
    return jnp.clip(values, -bound, bound).astype(held_as)


def setup_inputs(seed: int = 0) -> dict:
    arg_keys = jax.random.split(jax.random.key(seed), 11)
    return {
        "streams": centred(arg_keys[0], (N_FSDP, GROUP_TOK, STREAMS * D), 1.0, 6.0, ((0, 4), (1, 8))),
        "cotangent": centred(arg_keys[1], (N_FSDP, GROUP_TOK, STREAMS * D), 1.0, 6.0, ((0, 4), (1, 8))),
        "w_qkv": centred(arg_keys[2], (D, 3 * D), D ** -0.5, 0.125, ((0, 32),)),
        "w_out": centred(arg_keys[3], (D, D), (D // 16) ** -0.5, 0.5, ((0, 32),)),
        "w_gate_up": centred(arg_keys[4], (D, 2 * FF), D ** -0.5, 0.125, ((0, 32),)),
        "w_down": centred(arg_keys[5], (FF, D), FF ** -0.5, 0.0625, ((0, 32),)),
        "hc_weight": centred(arg_keys[6], (2, D, 6), D ** -0.5, 0.125, (), jnp.float32),
        "hc_static": jnp.clip(jax.random.uniform(arg_keys[7], (2, STREAMS, 6), jnp.float32, 0.2, 0.8), 0.2, 0.8),
        "seq_lengths": jax.vmap(lambda own: uneven(own, SEQS, GROUP_TOK, GROUP_TOK - BLOCK, 0))(jax.random.split(arg_keys[8], N_FSDP)).reshape((N_FSDP, SEQS)).astype(jnp.int32),
        "pair_perm": jax.vmap(lambda own: jax.random.permutation(own, N_CTX))(jax.random.split(arg_keys[9], N_FSDP)).reshape((N_FSDP, N_CTX)).astype(jnp.int32),
    }


@jax.custom_vjp
def low(v):
    return lax.optimization_barrier(v.astype(jnp.bfloat16)).astype(jnp.float32)

@jax.custom_vjp
def low_back(v):
    return v

def low_keep(v):
    return (low(v), None)

def low_pass(kept, grad):
    return (grad,)

def back_keep(v):
    return (v, None)

def back_low(kept, grad):
    return (low(grad),)
low.defvjp(low_keep, low_pass)
low_back.defvjp(back_keep, back_low)
eps = 1e-05
highest = lax.Precision.HIGHEST

def places(pair_row, length_row, rows):
    count = pair_row.shape[0]
    half = rows // 2
    index = jnp.arange(count * rows, dtype=jnp.int32)
    owner = index // rows
    slot = index % rows // half
    offset = index % half
    pair = lax.optimization_barrier(jnp.sum(jnp.where(owner[:, None] == jnp.arange(count, dtype=jnp.int32)[None, :], pair_row[None, :], 0), axis=1)).astype(jnp.int32)
    block = jnp.where(slot == 0, pair, 2 * count - 1 - pair)
    position = (block * half + offset).astype(jnp.int32)
    ends = jnp.cumsum(length_row).astype(jnp.int32)
    starts = (ends - length_row).astype(jnp.int32)
    doc = lax.optimization_barrier(jnp.sum((position[:, None] >= ends[None, :]).astype(jnp.int32), axis=1)).astype(jnp.int32)
    seq_ids = jnp.arange(length_row.shape[0], dtype=jnp.int32)
    inside = (position - lax.optimization_barrier(jnp.sum(jnp.where(doc[:, None] == seq_ids[None, :], starts[None, :], 0), axis=1))).astype(jnp.int32)
    return (position, doc, inside)

def norm_rows(v):
    mean = lax.optimization_barrier(jnp.mean(v, axis=-1, keepdims=True))
    cent = v - mean
    return cent * lax.rsqrt(lax.optimization_barrier(jnp.mean(cent * cent, axis=-1, keepdims=True)) + eps)

def mix_in(state, weight, static):
    normed = norm_rows(state)
    coef = static[None] + jnp.tanh(jnp.einsum('tnd,dk->tnk', normed, weight, precision=highest))
    layer_in = lax.optimization_barrier(jnp.sum(coef[:, :, 0:1] * state, axis=1))
    return (norm_rows(layer_in), coef[:, :, 1:5], coef[:, :, 5])

def mix_out(state, mixing, beta, branch):
    return jnp.einsum('tij,tid->tjd', mixing, state, precision=highest) + beta[:, :, None] * branch[:, None, :]

def rotate(v, inside, sign):
    half = v.shape[-1] // 2
    freq = 10000.0 ** (-jnp.arange(half, dtype=jnp.float32) / half)
    angle = inside.astype(jnp.float32)[:, None] * freq[None, :]
    cosine = jnp.cos(angle)[:, None, :]
    sine = sign * jnp.sin(angle)[:, None, :]
    first, second = (v[..., :half], v[..., half:])
    return jnp.concatenate([first * cosine - second * sine, second * cosine + first * sine], axis=-1)

def attend_block(query, keys, values, qpos, qdoc, kpos, kdoc):
    scores = jnp.einsum('qhe,khe->hqk', query, keys, precision=highest) * HEAD_DIM ** (-0.5)
    scores = low_back(scores)
    keep = (kpos[None, :] <= qpos[:, None]) & (kdoc[None, :] == qdoc[:, None])
    scores = jnp.where(keep[None], scores, -1e+30)
    probs = low(jax.nn.softmax(scores, axis=-1))
    return jnp.einsum('hqk,khe->qhe', probs, values, precision=highest)

def group_attend(args):
    query, keys, values, position, doc = args
    total = query.shape[0]
    rows_blk = min(512, total)
    count = total // rows_blk

    def one(piece):
        qs, qp, qd = piece
        return attend_block(qs, keys, values, qp, qd, position, doc)
    out = lax.map(jax.checkpoint(one), (query.reshape(count, rows_blk, HEADS, HEAD_DIM), position.reshape(count, rows_blk), doc.reshape(count, rows_blk)))
    return out.reshape(total, HEADS, HEAD_DIM)

def layer(state, w_qkv, w_out, w_gate_up, w_down, hc_weight, hc_static, position, doc, inside):
    groups, total = (state.shape[0], state.shape[1])
    flat = state.reshape(groups * total, STREAMS, D)
    inflat = inside.reshape(-1)
    normed, mixing, beta = mix_in(flat, hc_weight[0], hc_static[0])
    u = low(normed)
    qkv = low_back(jnp.dot(u, w_qkv, precision=highest))
    query = low(rotate(qkv[:, :D].reshape(-1, HEADS, HEAD_DIM), inflat, 1.0))
    keys = low(rotate(qkv[:, D:2 * D].reshape(-1, HEADS, HEAD_DIM), inflat, 1.0))
    values = low(qkv[:, 2 * D:].reshape(-1, HEADS, HEAD_DIM))
    shape4 = (groups, total, HEADS, HEAD_DIM)
    att = lax.map(group_attend, (query.reshape(shape4), keys.reshape(shape4), values.reshape(shape4), position, doc))
    attn_out = low(low_back(att.reshape(groups * total, D)))
    branch = low_back(jnp.dot(attn_out, w_out, precision=highest))
    mid = mix_out(flat, mixing, beta, branch)
    normed2, mixing2, beta2 = mix_in(mid, hc_weight[1], hc_static[1])
    u2 = low(normed2)
    gate_up = low_back(jnp.dot(u2, w_gate_up, precision=highest))
    hidden = low(low_back(jax.nn.silu(gate_up[:, :FF]) * gate_up[:, FF:]))
    branch2 = low_back(jnp.dot(hidden, w_down, precision=highest))
    final = mix_out(mid, mixing2, beta2, branch2)
    return final.reshape(groups, total, STREAMS * D)

def reference(streams, cotangent, w_qkv, w_out, w_gate_up, w_down, hc_weight, hc_static, seq_lengths, pair_perm):
    position, doc, inside = jax.vmap(lambda pr, lr: places(pr, lr, TOK_DEV))(pair_perm, seq_lengths)
    state = streams.astype(jnp.float32).reshape(streams.shape[0], streams.shape[1], STREAMS, D)

    def forward(st, wq, wo, wg, wd, hw, hs):
        return layer(st, wq, wo, wg, wd, hw, hs, position, doc, inside)
    out, pull = jax.vjp(forward, state, w_qkv.astype(jnp.float32), w_out.astype(jnp.float32), w_gate_up.astype(jnp.float32), w_down.astype(jnp.float32), hc_weight, hc_static)
    grads = pull(cotangent.astype(jnp.float32))
    grad_streams = grads[0].reshape(streams.shape).astype(jnp.bfloat16)
    return (out.astype(jnp.bfloat16), grad_streams, grads[1], grads[2], grads[3], grads[4], grads[5], grads[6])
```

```python
import functools

import jax
import jax.numpy as jnp
from jax import lax
from jax.experimental import pallas as pl
from jax.experimental.pallas import tpu as pltpu
from jax.sharding import PartitionSpec as P

D = 2048
HEADS = 16
HEAD_DIM = 128
FF = 8192
STREAMS = 4
SCALE = HEAD_DIM ** (-0.5)

eps = 1e-05
F32 = jnp.float32
BF16 = jnp.bfloat16
MIB = 1 << 20


def doc_of(position, length_row):
    ends = jnp.cumsum(length_row)
    starts = ends - length_row
    doc = jnp.sum((position[:, None] >= ends[None, :]).astype(jnp.int32), axis=1)
    seq_ids = jnp.arange(length_row.shape[0], dtype=jnp.int32)
    start = jnp.sum(jnp.where(doc[:, None] == seq_ids[None, :], starts[None, :], 0), axis=1)
    return (doc, start)


def places(pair_row, length_row, rows, owners):
    count = pair_row.shape[0]
    half = rows // 2
    ids = jnp.arange(count, dtype=jnp.int32)
    pair = jnp.sum(jnp.where(owners[:, None] == ids[None, :], pair_row[None, :], 0), axis=1)
    block = jnp.stack([pair, 2 * count - 1 - pair], axis=1)
    offset = jnp.arange(half, dtype=jnp.int32)
    position = (block[:, :, None] * half + offset[None, None, :]).reshape(-1)
    doc, start = doc_of(position, length_row)
    return (position, doc, start)


def ring_order(n):
    return list(range(0, n, 2)) + list(range(n - 1, 0, -2)) if n % 2 == 0 else list(range(n))


def ring_perms(n):
    order = ring_order(n)
    ahead = [(order[i], order[(i + 1) % n]) for i in range(n)]
    return (ahead, [(b, a) for a, b in ahead])


def ring_offsets(n):
    offsets = [0]
    for k in range(1, n // 2):
        offsets += [-k, k]
    return offsets + [-(n // 2)]


def ring_owners(n, place):
    order = jnp.array(ring_order(n), dtype=jnp.int32)
    ids = jnp.arange(n, dtype=jnp.int32)
    mine = jnp.sum(jnp.where(order == place, ids, 0))
    at = (mine + jnp.array(ring_offsets(n), dtype=jnp.int32)) % n
    return jnp.sum(jnp.where(at[:, None] == ids[None, :], order[None, :], 0), axis=1)


def ring_gather(block):
    n = lax.axis_size("ctx")
    ahead, back = ring_perms(n)
    one = other = block
    blocks = [block]
    for k in range(1, n // 2 + 1):
        if 2 * k == n:
            half = block.shape[0] // 2
            one = lax.ppermute(one[:half], "ctx", ahead)
            other = lax.ppermute(other[half:], "ctx", back)
        else:
            one = lax.ppermute(one, "ctx", ahead)
            other = lax.ppermute(other, "ctx", back)
        blocks += [one, other]
    return jnp.concatenate(blocks, axis=0)


def ring_scatter(partial, rows):
    n = lax.axis_size("ctx")
    ahead, back = ring_perms(n)
    offsets = ring_offsets(n)

    def part(offset):
        at = offsets.index(offset)
        return partial[at * rows : (at + 1) * rows]

    def add(moving, offset, first, last):
        own = part(offset)
        sent = [own[:first], own[first:last], own[last:]]
        sent[1] = (moving.astype(F32) + sent[1].astype(F32)).astype(BF16)
        return jnp.concatenate(sent, axis=0)

    half = n // 2
    mid = rows // 2
    one, other = part(-half)[:mid], part(-half)[mid:]
    span_one, span_other = (0, mid), (mid, rows)
    for k in range(half - 1, 0, -1):
        one = add(lax.ppermute(one, "ctx", ahead), k, *span_one)
        other = add(lax.ppermute(other, "ctx", back), -k, *span_other)
        span_one = span_other = (0, rows)
    one = lax.ppermute(one, "ctx", ahead).astype(F32)
    other = lax.ppermute(other, "ctx", back).astype(F32)
    if half == 1:
        return part(0).astype(F32) + jnp.concatenate([one, other], axis=0)
    return part(0).astype(F32) + one + other


def to_columns(weight, parts):
    n = lax.axis_size("ctx")
    place = lax.axis_index("ctx")
    rows = weight.shape[0]
    width = weight.shape[1] // parts // n
    if n <= 8:

        def piece(dest):
            return jnp.concatenate(
                [
                    lax.dynamic_slice_in_dim(weight, (p * n + dest) * width, width, 1)
                    for p in range(parts)
                ],
                axis=1,
            )

        held = jnp.zeros((n, rows, parts * width), weight.dtype)
        for k in range(n):
            got = piece((place + k) % n)
            if k:
                got = lax.ppermute(got, "ctx", [(i, (i + k) % n) for i in range(n)])
            held = lax.dynamic_update_slice_in_dim(held, got[None], (place - k) % n, 0)
    else:
        cut = weight.reshape(rows, parts, n, width).transpose(2, 0, 1, 3)
        held = lax.all_to_all(cut.reshape(n, rows, parts * width), "ctx", 0, 0, tiled=True)
    full = lax.all_gather(held.reshape(n * rows, parts * width), "fsdp", axis=0, tiled=True)
    return full


def to_rows(gradient, parts):
    n = lax.axis_size("ctx")
    place = lax.axis_index("ctx")
    mine = lax.psum_scatter(gradient.astype(BF16), "fsdp", scatter_dimension=0, tiled=True)
    rows = mine.shape[0] // n
    width = mine.shape[1] // parts
    if n <= 8:
        out = jnp.zeros((rows, parts * n * width), F32)
        for k in range(n):
            got = lax.dynamic_slice_in_dim(mine, (place + k) % n * rows, rows, 0)
            if k:
                got = lax.ppermute(got, "ctx", [(i, (i + k) % n) for i in range(n)])
            got = got.astype(F32)
            source = (place - k) % n
            for p in range(parts):
                out = lax.dynamic_update_slice_in_dim(
                    out, got[:, p * width : (p + 1) * width], (p * n + source) * width, 1
                )
        return out
    got = lax.all_to_all(mine.reshape(n, rows, parts * width), "ctx", 0, 0, tiled=True)
    got = got.reshape(n, rows, parts, width).transpose(1, 2, 0, 3)
    return got.reshape(rows, parts * n * width).astype(F32)


def share_rows(gradient):
    mine = lax.psum_scatter(gradient.astype(BF16), "fsdp", scatter_dimension=0, tiled=True)
    return mine.astype(F32)


def weight_share(gradient, shard_rows):
    partial_rows = lax.psum_scatter(
        gradient.astype(BF16), "ctx", scatter_dimension=0, tiled=True
    )
    return lax.psum_scatter(partial_rows, "fsdp", scatter_dimension=0, tiled=True).astype(F32)


def spread_columns(v):
    n, m = lax.axis_size("ctx"), lax.axis_size("fsdp")
    rows = v.shape[0]
    return v.reshape(rows, n, m, D // (n * m)).transpose(0, 2, 1, 3).reshape(rows, D)


def unspread_columns(v):
    n, m = lax.axis_size("ctx"), lax.axis_size("fsdp")
    rows = v.shape[0]
    return v.reshape(rows, m, n, D // (n * m)).transpose(0, 2, 1, 3).reshape(rows, D)


def sum_all(v):
    for axis in ("ctx", "fsdp"):
        n = lax.axis_size(axis)
        if n & (n - 1):
            v = lax.psum(v, axis)
            continue
        step = 1
        while step < n:
            v = v + lax.ppermute(v, axis, [(i, i ^ step) for i in range(n)])
            step *= 2
    return v


LANES = 128
HC_ROWS = 32


def lanes_of(rows):
    return lax.broadcasted_iota(jnp.int32, (rows, LANES), 1)


def put(held, lane, at, column):
    return jnp.where(lane == at, column, held)


def mean_of(v):
    return jnp.sum(v, axis=1, keepdims=True) * (1.0 / D)


def stream_parts(ref):
    return [ref[:, i * D : (i + 1) * D].astype(F32) for i in range(STREAMS)]


def mixed(parts, coef, branch):
    outs = []
    for j in range(STREAMS):
        total = coef[:, 8 * j + 5 : 8 * j + 6] * branch
        for i in range(STREAMS):
            total = total + coef[:, 8 * i + 1 + j : 8 * i + 2 + j] * parts[i]
        outs.append(total)
    return outs


def branch_grad(parts, coef):
    return sum(coef[:, 8 * j + 5 : 8 * j + 6] * parts[j] for j in range(STREAMS))


def layer_in(parts, coef):
    return sum(coef[:, 8 * i : 8 * i + 1] * parts[i] for i in range(STREAMS))


def enter(parts, wpack, static):
    rows = parts[0].shape[0]
    lane = lanes_of(rows)
    aux = jnp.zeros((rows, LANES), F32)
    pieces = ([], [], [])
    for i in range(STREAMS):
        mean = mean_of(parts[i])
        cent = parts[i] - mean
        rstd = lax.rsqrt(mean_of(cent * cent) + eps)
        left = cent * rstd
        for piece in pieces:
            piece.append(left.astype(BF16))
            left = left - piece[-1].astype(F32)
        aux = put(aux, lane, 8 * i + 6, mean)
        aux = put(aux, lane, 8 * i + 7, rstd)
    dims = (((1,), (1,)), ((), ()))
    proj = sum(
        lax.dot_general(jnp.concatenate(p, axis=0), wpack, dims, preferred_element_type=F32)
        for p in pieces[::-1]
    )
    proj = proj + pltpu.roll(proj, LANES - 32, 1) + pltpu.roll(proj, LANES - 64, 1)
    for i in range(STREAMS):
        own = jnp.where(lane < 6, proj[i * rows : (i + 1) * rows], 0.0)
        aux += own if i == 0 else pltpu.roll(own, 8 * i, 1)
    coef = static + jnp.tanh(aux)
    x = layer_in(parts, coef)
    mean = mean_of(x)
    cent = x - mean
    rstd = lax.rsqrt(mean_of(cent * cent) + eps)
    aux = put(aux, lane, 32, mean)
    aux = put(aux, lane, 33, rstd)
    return (aux, coef, cent * rstd)


def leave_grads(parts, grads, branch):
    rows = parts[0].shape[0]
    lane = lanes_of(rows)
    red = jnp.zeros((rows, LANES), F32)
    for j in range(STREAMS):
        red = put(red, lane, 8 * j + 5, jnp.sum(grads[j] * branch, axis=1, keepdims=True))
        for i in range(STREAMS):
            red = put(
                red, lane, 8 * i + 1 + j, jnp.sum(parts[i] * grads[j], axis=1, keepdims=True)
            )
    return red


def enter_back(parts, grads, aux, coef, red, du, wpack, normed_ref, dz_ref, stat_ref, step):
    rows = parts[0].shape[0]
    lane = lanes_of(rows)
    x = layer_in(parts, coef)
    rx = aux[:, 33:34]
    nx = (x - aux[:, 32:33]) * rx
    dx = rx * (du - mean_of(du) - nx * mean_of(du * nx))
    for i in range(STREAMS):
        red = put(red, lane, 8 * i, jnp.sum(parts[i] * dx, axis=1, keepdims=True))
    used = (lane < 8 * STREAMS) & (lane % 8 < 6)
    slope = jnp.tanh(aux)
    dz = jnp.where(used, red * (1.0 - slope * slope), 0.0)
    stat_ref[0:1, :] += jnp.sum(red, axis=0, keepdims=True)
    dz_ref[pl.ds(step * rows, rows), :] = dz
    both = dz * aux
    packed = []
    for i in range(STREAMS):
        own = dz if i == 0 else pltpu.roll(dz, LANES - 8 * i, 1)
        own = jnp.where(lane < 6, own, 0.0)
        top = own.astype(BF16).astype(F32)
        packed.append((top + pltpu.roll(top, 32, 1) + pltpu.roll(own - top, 96, 1)).astype(BF16))
    dn_all = lax.dot_general(
        jnp.concatenate(packed, axis=0), wpack, (((1,), (0,)), ((), ())), preferred_element_type=F32
    )
    outs = []
    total_rows = dz_ref.shape[0]
    for i in range(STREAMS):
        mean, rstd = aux[:, 8 * i + 6 : 8 * i + 7], aux[:, 8 * i + 7 : 8 * i + 8]
        normed = (parts[i] - mean) * rstd
        normed_ref[pl.ds(i * total_rows + step * rows, rows), :] = normed.astype(BF16)
        dn = dn_all[i * rows : (i + 1) * rows]
        own = (lane >= 8 * i) & (lane < 8 * i + 6)
        along = jnp.sum(jnp.where(own, both, 0.0), axis=1, keepdims=True) * (1.0 / D)
        total = coef[:, 8 * i : 8 * i + 1] * dx + rstd * (dn - mean_of(dn) - normed * along)
        for j in range(STREAMS):
            total = total + coef[:, 8 * i + 1 + j : 8 * i + 2 + j] * grads[j]
        outs.append(total)
    return outs


def finish_hc(normed_ref, dz_ref, stat_ref, hc_ref):
    across = dz_ref[...].T
    left = jnp.concatenate([across[8 * i : 8 * i + 8] for i in range(STREAMS)], axis=1)
    top = left.astype(BF16)
    low = (left - top.astype(F32)).astype(BF16)
    both = lax.dot_general(
        jnp.concatenate([top, low], axis=0),
        normed_ref[...],
        (((1,), (0,)), ((), ())),
        preferred_element_type=F32,
    )
    hc_ref[0:8, :] = both[0:8] + both[8:16]
    hc_ref[8:16, :] = jnp.zeros((8, D), F32)
    hc_ref[8:9, 0:LANES] = stat_ref[0:1, :]


def first_kernel(s_ref, w_ref, static_ref, u_ref, aux_ref):
    aux, _, u = enter(stream_parts(s_ref), w_ref[...], static_ref[0:1, :])
    u_ref[...] = u.astype(BF16)
    aux_ref[...] = aux


def middle_kernel(s_ref, c_ref, y_ref, aux0_ref, w_ref, static_ref, u_ref, dy_ref, aux_ref):
    coef0 = static_ref[0:1, :] + jnp.tanh(aux0_ref[...])
    mid = mixed(stream_parts(s_ref), coef0, y_ref[...])
    aux, coef, u = enter(mid, w_ref[...], static_ref[1:2, :])
    u_ref[...] = u.astype(BF16)
    aux_ref[...] = aux
    dy_ref[...] = branch_grad(stream_parts(c_ref), coef).astype(BF16)


def out_kernel(
    s_ref, c_ref, y_ref, y2_ref, aux0_ref, aux1_ref, static_ref, out_ref, red_ref
):
    coef0 = static_ref[0:1, :] + jnp.tanh(aux0_ref[...])
    coef1 = static_ref[1:2, :] + jnp.tanh(aux1_ref[...])
    mid = mixed(stream_parts(s_ref), coef0, y_ref[...])
    y2 = y2_ref[...]
    for j, total in enumerate(mixed(mid, coef1, y2)):
        out_ref[:, j * D : (j + 1) * D] = total.astype(BF16)
    red_ref[...] = leave_grads(mid, stream_parts(c_ref), y2)


def back_kernel(
    s_ref, c_ref, y_ref, du_ref, red_ref, aux0_ref, aux1_ref, w_ref, static_ref,
    dmid_ref, dy_ref, hc_ref, normed_ref, dz_ref, stat_ref,
):
    step = pl.program_id(0)

    @pl.when(step == 0)
    def _():
        stat_ref[...] = jnp.zeros_like(stat_ref)

    coef0 = static_ref[0:1, :] + jnp.tanh(aux0_ref[...])
    aux1 = aux1_ref[...]
    coef1 = static_ref[1:2, :] + jnp.tanh(aux1)
    mid = mixed(stream_parts(s_ref), coef0, y_ref[...])
    dmid = enter_back(
        mid, stream_parts(c_ref), aux1, coef1, red_ref[...], du_ref[...], w_ref[...],
        normed_ref, dz_ref, stat_ref, step,
    )
    for j in range(STREAMS):
        dmid_ref[:, j * D : (j + 1) * D] = dmid[j]
    dy_ref[...] = branch_grad(dmid, coef0).astype(BF16)

    @pl.when(step == pl.num_programs(0) - 1)
    def _():
        finish_hc(normed_ref, dz_ref, stat_ref, hc_ref)


def last_kernel(
    s_ref, dmid_ref, y_ref, du_ref, aux0_ref, w_ref, static_ref,
    ds_ref, hc_ref, normed_ref, dz_ref, stat_ref,
):
    step = pl.program_id(0)

    @pl.when(step == 0)
    def _():
        stat_ref[...] = jnp.zeros_like(stat_ref)

    aux0 = aux0_ref[...]
    coef0 = static_ref[0:1, :] + jnp.tanh(aux0)
    parts, grads = stream_parts(s_ref), stream_parts(dmid_ref)
    red = leave_grads(parts, grads, y_ref[...])
    ds = enter_back(
        parts, grads, aux0, coef0, red, du_ref[...], w_ref[...],
        normed_ref, dz_ref, stat_ref, step,
    )
    for j in range(STREAMS):
        ds_ref[:, j * D : (j + 1) * D] = ds[j].astype(BF16)

    @pl.when(step == pl.num_programs(0) - 1)
    def _():
        finish_hc(normed_ref, dz_ref, stat_ref, hc_ref)


def row_call(kernel, rows, ins, outs, hc=False):
    tile = HC_ROWS

    def cut(columns):
        return pl.BlockSpec((tile, columns), lambda i: (i, 0))

    def whole(shape):
        return pl.BlockSpec(shape, lambda i: (0, 0))

    in_specs = [cut(a.shape[1]) if by_rows else whole(a.shape) for a, by_rows in ins]
    out_specs = [cut(columns) for columns, _ in outs]
    out_shape = [jax.ShapeDtypeStruct((rows, columns), dtype) for columns, dtype in outs]
    scratch = []
    if hc:
        out_specs.append(whole((16, D)))
        out_shape.append(jax.ShapeDtypeStruct((16, D), F32))
        scratch = [
            pltpu.VMEM((STREAMS * rows, D), BF16),
            pltpu.VMEM((rows, LANES), F32),
            pltpu.VMEM((8, LANES), F32),
        ]
    return pl.pallas_call(
        kernel,
        grid=(rows // tile,),
        in_specs=in_specs,
        out_specs=out_specs,
        out_shape=out_shape,
        scratch_shapes=scratch,
        compiler_params=pltpu.CompilerParams(vmem_limit_bytes=40 * MIB),
    )(*[a for a, _ in ins])


def pack_weight(weight):
    across = jnp.pad(weight.T, ((0, 26), (0, 0)))
    top = lax.reduce_precision(across, 8, 7)
    mid = lax.reduce_precision(across - top, 8, 7)
    return jnp.concatenate([top, mid, across - top - mid, top], axis=0).astype(BF16)


Q_ROWS = 256


def turn(v, cosine, sine):
    return v * cosine + pltpu.roll(v, HEAD_DIM // 2, 1) * sine


def attend_kernel(
    q_ref, k_ref, v_ref, cos_ref, sin_ref, qpos_ref, qstart_ref, kpos_ref,
    o_ref, lse_ref, qr_ref, kr_ref, vb_ref,
):
    at = pl.program_id(1)

    @pl.when(at == 0)
    def _():
        kr_ref[...] = turn(k_ref[...], cos_ref[...], sin_ref[...]).astype(BF16)
        vb_ref[...] = v_ref[...].astype(BF16)

    here = pl.ds(at * Q_ROWS, Q_ROWS)
    query = turn(q_ref[...], cos_ref[here, :], sin_ref[here, :]).astype(BF16)
    qr_ref[...] = query
    scores = (
        lax.dot_general(query, kr_ref[...], (((1,), (1,)), ((), ())), preferred_element_type=F32)
        * SCALE
    )
    kpos = kpos_ref[0:1, :]
    keep = (kpos <= qpos_ref[...]) & (kpos >= qstart_ref[...])
    scores = jnp.where(keep, scores, -1e30)
    top = jnp.max(scores, axis=1, keepdims=True)
    grown = jnp.exp(scores - top)
    total = jnp.sum(grown, axis=1, keepdims=True)
    out = jnp.dot((grown / total).astype(BF16), vb_ref[...], preferred_element_type=F32)
    o_ref[...] = out.astype(BF16)
    lse_ref[...] = jnp.broadcast_to(top + jnp.log(total), lse_ref.shape)


def attend_back_kernel(
    q_ref, k_ref, v_ref, do_ref, lse_ref, cos_ref, sin_ref, qpos_ref, qstart_ref, kpos_ref,
    dq_ref, dk_ref, dv_ref, dk_sum, dv_sum,
):
    at = pl.program_id(1)

    @pl.when(at == 0)
    def _():
        dk_sum[...] = jnp.zeros_like(dk_sum)
        dv_sum[...] = jnp.zeros_like(dv_sum)

    here = pl.ds(at * Q_ROWS, Q_ROWS)
    query, keys, d_out = q_ref[...], k_ref[...], do_ref[...]
    nt = (((1,), (1,)), ((), ()))
    tn = (((0,), (0,)), ((), ()))
    scores = lax.dot_general(query, keys, nt, preferred_element_type=F32) * SCALE
    kpos = kpos_ref[0:1, :]
    keep = (kpos <= qpos_ref[...]) & (kpos >= qstart_ref[...])
    probs = jnp.where(keep, jnp.exp(scores - lse_ref[:, 0:1]), 0.0)
    d_probs = lax.dot_general(d_out, v_ref[...], nt, preferred_element_type=F32)
    delta = jnp.sum(probs * d_probs, axis=1, keepdims=True)
    ds = (probs * (d_probs - delta)).astype(BF16)
    dq = jnp.dot(ds, keys, preferred_element_type=F32) * SCALE
    dq_ref[...] = turn(dq, cos_ref[here, :], -sin_ref[here, :]).astype(BF16)
    dk_sum[...] += lax.dot_general(ds, query, tn, preferred_element_type=F32)
    dv_sum[...] += lax.dot_general(probs.astype(BF16), d_out, tn, preferred_element_type=F32)

    @pl.when(at == pl.num_programs(1) - 1)
    def _():
        dk_ref[...] = turn(dk_sum[...] * SCALE, cos_ref[...], -sin_ref[...]).astype(BF16)
        dv_ref[...] = dv_sum[...].astype(BF16)


def attention_specs(total):
    by_query = pl.BlockSpec((Q_ROWS, HEAD_DIM), lambda h, i: (i, h))
    by_head = pl.BlockSpec((total, HEAD_DIM), lambda h, i: (0, h))
    table = pl.BlockSpec((total, HEAD_DIM), lambda h, i: (0, 0))
    row = pl.BlockSpec((Q_ROWS, 1), lambda h, i: (i, 0))
    keys = pl.BlockSpec((8, total), lambda h, i: (0, 0))
    return (by_query, by_head, [table, table, row, row, keys])


def attend(qkv, heads, marks):
    total = qkv.shape[0]
    by_query, by_head, shared = attention_specs(total)

    def of(kind):
        return pl.BlockSpec((total, HEAD_DIM), lambda h, i: (0, kind * heads + h))

    low = jax.ShapeDtypeStruct((total, heads * HEAD_DIM), BF16)
    wide = jax.ShapeDtypeStruct((total, heads * HEAD_DIM), F32)
    return pl.pallas_call(
        attend_kernel,
        grid=(heads, total // Q_ROWS),
        in_specs=[by_query, of(1), of(2)] + shared,
        out_specs=[by_query, by_query, by_query, by_head, by_head],
        out_shape=[low, wide, low, low, low],
        compiler_params=pltpu.CompilerParams(vmem_limit_bytes=40 * MIB),
    )(qkv, qkv, qkv, *marks)


def attend_back(query, keys, values, d_out, lse, heads, marks):
    total = query.shape[0]
    by_query, by_head, shared = attention_specs(total)
    low = jax.ShapeDtypeStruct((total, heads * HEAD_DIM), BF16)
    return pl.pallas_call(
        attend_back_kernel,
        grid=(heads, total // Q_ROWS),
        in_specs=[by_query, by_head, by_head, by_query, by_query] + shared,
        out_specs=[by_query, by_head, by_head],
        out_shape=[low, low, low],
        scratch_shapes=[pltpu.VMEM((total, HEAD_DIM), F32)] * 2,
        compiler_params=pltpu.CompilerParams(vmem_limit_bytes=40 * MIB),
    )(query, keys, values, d_out, lse, *marks)


def angles(inside):
    half = HEAD_DIM // 2
    freq = 10000.0 ** (-jnp.arange(half, dtype=F32) / half)
    angle = inside.astype(F32)[:, None] * freq[None, :]
    cosine, sine = jnp.cos(angle), jnp.sin(angle)
    return (jnp.concatenate([cosine, cosine], axis=1), jnp.concatenate([-sine, sine], axis=1))


class HeadAttention:
    def __init__(self, rows, w_qkv, w_out, pair_row, length_row):
        n = lax.axis_size("ctx")
        self.place = lax.axis_index("ctx")
        self.rows, self.heads = rows, HEADS // n
        self.owners = ring_owners(n, self.place)
        position, _, start = places(pair_row, length_row, rows, self.owners)
        cosine, sine = angles(position - start)
        kpos = jnp.broadcast_to(position[None, :], (8, position.shape[0]))
        self.marks = (cosine, sine, position[:, None], start[:, None], kpos)
        self.qkv_cols = to_columns(w_qkv, 3)
        self.out_all = lax.all_gather(w_out, ("ctx", "fsdp"), axis=0, tiled=True)

    def to_tokens(self, heads_out):
        n = lax.axis_size("ctx")
        order, offsets = ring_order(n), ring_offsets(n)
        width = heads_out.shape[1]
        mine = jnp.zeros((self.rows, n * width), heads_out.dtype)
        for at, offset in enumerate(offsets):
            got = heads_out[at * self.rows : (at + 1) * self.rows]
            back = -offset if offset != -(n // 2) else offset
            if offset:
                pairs = [(order[i], order[(i + offset) % n]) for i in range(n)]
                got = lax.ppermute(got, "ctx", pairs)
            source = self.owners[offsets.index(back)]
            mine = lax.dynamic_update_slice_in_dim(mine, got, source * width, 1)
        return mine

    def forward(self, u):
        self.u_all = ring_gather(spread_columns(u))
        qkv = jnp.dot(self.u_all, self.qkv_cols, preferred_element_type=F32)
        self.o, self.lse, self.q, self.k, self.v = attend(qkv, self.heads, self.marks)
        return jnp.dot(self.to_tokens(self.o), self.out_all, preferred_element_type=F32)

    def backward(self, dy):
        dy_all = ring_gather(dy)
        width = self.heads * HEAD_DIM
        out_rows = lax.dynamic_slice_in_dim(self.out_all, self.place * width, width, 0)
        d_out = jnp.einsum("td,ed->te", dy_all, out_rows, preferred_element_type=F32).astype(BF16)
        grad_out = jnp.einsum("te,td->ed", self.o, dy_all, preferred_element_type=F32)
        dq, dk, dv = attend_back(self.q, self.k, self.v, d_out, self.lse, self.heads, self.marks)
        d_qkv = jnp.concatenate([dq, dk, dv], axis=1)
        partial = jnp.einsum(
            "tc,dc->td", d_qkv, self.qkv_cols, preferred_element_type=F32
        ).astype(BF16)
        grad_qkv = jnp.einsum("td,tc->dc", self.u_all, d_qkv, preferred_element_type=F32)
        du = unspread_columns(ring_scatter(partial, self.rows))
        return (du, to_rows(grad_qkv, 3), share_rows(grad_out))


def rotate(v, inside, sign):
    half = v.shape[-1] // 2
    freq = 10000.0 ** (-jnp.arange(half, dtype=F32) / half)
    angle = inside.astype(F32)[:, None] * freq[None, :]
    cosine = jnp.cos(angle)[:, None, :]
    sine = sign * jnp.sin(angle)[:, None, :]
    first, second = (v[..., :half], v[..., half:])
    return jnp.concatenate(
        [first * cosine - second * sine, second * cosine + first * sine], axis=-1
    )


class TokenAttention:
    def __init__(self, rows, w_qkv, w_out, pair_row, length_row):
        n = lax.axis_size("ctx")
        place = lax.axis_index("ctx")
        self.rows = rows
        owners = jnp.arange(n, dtype=jnp.int32)
        kpos, kdoc, kstart = places(pair_row, length_row, rows, owners)

        def own(v):
            return lax.dynamic_slice_in_dim(v, place * rows, rows)

        self.inside = own(kpos - kstart)
        self.keep = (kpos[None, :] <= own(kpos)[:, None]) & (kdoc[None, :] == own(kdoc)[:, None])
        self.w_qkv, self.w_out = w_qkv, w_out

    def gathered(self, weight):
        return lax.all_gather(weight, ("ctx", "fsdp"), axis=0, tiled=True)

    def scores(self):
        scores = jnp.einsum("qhe,hke->hqk", self.q, self.k, preferred_element_type=F32) * SCALE
        return jnp.where(self.keep[None], scores, -1e30)

    def forward(self, u):
        rows, shape = self.rows, (self.rows, HEADS, HEAD_DIM)
        self.u = u
        qkv = jnp.dot(u, self.gathered(self.w_qkv), preferred_element_type=F32)
        self.q = rotate(qkv[:, :D].reshape(shape), self.inside, 1.0).astype(BF16)
        key = rotate(qkv[:, D : 2 * D].reshape(shape), self.inside, 1.0).astype(BF16)
        value = qkv[:, 2 * D :].reshape(shape).astype(BF16)
        self.k = lax.all_gather(key.transpose(1, 0, 2), "ctx", axis=1, tiled=True)
        self.v = lax.all_gather(value.transpose(1, 0, 2), "ctx", axis=1, tiled=True)
        scores = self.scores()
        top = jnp.max(scores, axis=-1, keepdims=True)
        self.lse = top + jnp.log(jnp.sum(jnp.exp(scores - top), axis=-1, keepdims=True))
        probs = jnp.exp(scores - self.lse).astype(BF16)
        attended = jnp.einsum("hqk,hke->qhe", probs, self.v, preferred_element_type=F32)
        self.o = attended.reshape(rows, D).astype(BF16)
        return jnp.dot(self.o, self.gathered(self.w_out), preferred_element_type=F32)

    def backward(self, dy):
        rows = self.rows
        d_out = jnp.einsum(
            "td,ed->te", dy, self.gathered(self.w_out), preferred_element_type=F32
        )
        d_out = d_out.astype(BF16).reshape(rows, HEADS, HEAD_DIM)
        grad_out = jnp.einsum("te,td->ed", self.o, dy, preferred_element_type=F32)
        again = jnp.exp(self.scores() - self.lse)
        d_probs = jnp.einsum("qhe,hke->hqk", d_out, self.v, preferred_element_type=F32)
        delta = jnp.sum(again * d_probs, axis=-1, keepdims=True)
        ds = (again * (d_probs - delta)).astype(BF16)
        dq = jnp.einsum("hqk,hke->qhe", ds, self.k, preferred_element_type=F32) * SCALE
        dk_all = jnp.einsum("hqk,qhe->hke", ds, self.q, preferred_element_type=F32) * SCALE
        dv_all = jnp.einsum(
            "hqk,qhe->hke", again.astype(BF16), d_out, preferred_element_type=F32
        )

        def shared(v):
            mine = lax.psum_scatter(v.astype(BF16), "ctx", scatter_dimension=1, tiled=True)
            return mine.astype(F32).transpose(1, 0, 2)

        dk, dv = shared(dk_all), shared(dv_all)
        d_qkv = jnp.concatenate(
            [
                rotate(dq, self.inside, -1.0).reshape(rows, D),
                rotate(dk, self.inside, -1.0).reshape(rows, D),
                dv.reshape(rows, D),
            ],
            axis=1,
        ).astype(BF16)
        du = jnp.einsum("tc,dc->td", d_qkv, self.gathered(self.w_qkv), preferred_element_type=F32)
        grad_qkv = jnp.einsum("td,tc->dc", self.u, d_qkv, preferred_element_type=F32)
        return (
            du,
            weight_share(grad_qkv, self.w_qkv.shape[0]),
            weight_share(grad_out, self.w_out.shape[0]),
        )


def on_device(
    streams,
    cotangent,
    w_qkv,
    w_out,
    w_gate_up,
    w_down,
    hc_weight,
    hc_static,
    seq_lengths,
    pair_perm,
):
    n = lax.axis_size("ctx")
    group = lax.axis_index("fsdp")
    rows = streams.shape[1]
    pair_row = lax.dynamic_index_in_dim(pair_perm, group, 0, keepdims=False)
    length_row = lax.dynamic_index_in_dim(seq_lengths, group, 0, keepdims=False)
    state, cot = streams[0], cotangent[0]
    wpack0, wpack1 = pack_weight(hc_weight[0]), pack_weight(hc_weight[1])
    static = jnp.pad(hc_static, ((0, 0), (0, 0), (0, 2))).reshape(2, 8 * STREAMS)
    static = jnp.pad(static, ((0, 6), (0, LANES - 8 * STREAMS)))

    plan = HeadAttention if HEADS % n == 0 else TokenAttention
    attention = plan(rows, w_qkv, w_out, pair_row, length_row)
    u, aux0 = row_call(
        first_kernel,
        rows,
        [(state, True), (wpack0, False), (static, False)],
        [(D, BF16), (LANES, F32)],
    )
    gate_up_cols = to_columns(w_gate_up, 2)
    down_rows = lax.all_gather(w_down, "fsdp", axis=0, tiled=True)
    y = attention.forward(u)
    u2, dy2, aux1 = row_call(
        middle_kernel,
        rows,
        [(state, True), (cot, True), (y, True), (aux0, True), (wpack1, False), (static, False)],
        [(D, BF16), (D, BF16), (LANES, F32)],
    )
    u2_all = ring_gather(spread_columns(u2))
    dy2_all = ring_gather(dy2)
    width = FF // n
    gate_up = jnp.dot(u2_all, gate_up_cols, preferred_element_type=F32)
    gate, up = gate_up[:, :width], gate_up[:, width:]
    hidden = (jax.nn.silu(gate) * up).astype(BF16)
    y2_partial = jnp.dot(hidden, down_rows, preferred_element_type=F32).astype(BF16)
    y2 = ring_scatter(y2_partial, rows)
    d_hidden = jnp.einsum("td,fd->tf", dy2_all, down_rows, preferred_element_type=F32)
    d_hidden = lax.reduce_precision(d_hidden, 8, 7)
    grad_down = share_rows(
        jnp.einsum("tf,td->fd", hidden, dy2_all, preferred_element_type=F32)
    )
    open_gate = jax.nn.sigmoid(gate)
    d_up = d_hidden * gate * open_gate
    d_gate = d_hidden * up * open_gate * (1.0 + gate * (1.0 - open_gate))
    dgu = jnp.concatenate([d_gate, d_up], axis=1).astype(BF16)
    du2_partial = jnp.einsum("tg,dg->td", dgu, gate_up_cols, preferred_element_type=F32)
    du2 = unspread_columns(ring_scatter(du2_partial.astype(BF16), rows))
    grad_gate_up = to_rows(
        jnp.einsum("td,tg->dg", u2_all, dgu, preferred_element_type=F32), 2
    )
    out, red1 = row_call(
        out_kernel,
        rows,
        [
            (state, True), (cot, True), (y, True), (y2, True), (aux0, True), (aux1, True),
            (static, False),
        ],
        [(STREAMS * D, BF16), (LANES, F32)],
    )
    dmid, dy, hc1 = row_call(
        back_kernel,
        rows,
        [
            (state, True), (cot, True), (y, True), (du2, True), (red1, True), (aux0, True),
            (aux1, True), (wpack1, False), (static, False),
        ],
        [(STREAMS * D, F32), (D, BF16)],
        hc=True,
    )
    du, grad_qkv, grad_out = attention.backward(dy)
    grad_state, hc0 = row_call(
        last_kernel,
        rows,
        [
            (state, True), (dmid, True), (y, True), (du, True), (aux0, True), (wpack0, False),
            (static, False),
        ],
        [(STREAMS * D, BF16)],
        hc=True,
    )
    hc = jnp.stack([sum_all(hc0), sum_all(hc1)])
    grad_hc_weight = hc[:, 0:6].transpose(0, 2, 1)
    grad_hc_static = hc[:, 8, : 8 * STREAMS].reshape(2, STREAMS, 8)[:, :, 0:6]
    return (
        out[None],
        grad_state[None],
        grad_qkv,
        grad_out,
        grad_gate_up,
        grad_down,
        grad_hc_weight,
        grad_hc_static,
    )


def solution(mesh):
    return jax.shard_map(
        on_device,
        mesh=mesh,
        in_specs=(
            P("fsdp", "ctx", None),
            P("fsdp", "ctx", None),
            P(("ctx", "fsdp"), None),
            P(("ctx", "fsdp"), None),
            P(("ctx", "fsdp"), None),
            P(("ctx", "fsdp"), None),
            P(),
            P(),
            P(),
            P(),
        ),
        out_specs=(
            P("fsdp", "ctx", None),
            P("fsdp", "ctx", None),
            P(("ctx", "fsdp"), None),
            P(("ctx", "fsdp"), None),
            P(("ctx", "fsdp"), None),
            P(("ctx", "fsdp"), None),
            P(),
            P(),
        ),
        check_vma=False,
    )
```

```python
import functools

import jax
import jax.numpy as jnp
from jax import lax
from jax.experimental import pallas as pl
from jax.experimental.pallas import tpu as pltpu
from jax.sharding import PartitionSpec as P

D = 2048
HEADS = 16
HEAD_DIM = 128
FF = 8192
STREAMS = 4
SCALE = HEAD_DIM ** (-0.5)

eps = 1e-05
F32 = jnp.float32
BF16 = jnp.bfloat16
MIB = 1 << 20


def doc_of(position, length_row):
    ends = jnp.cumsum(length_row)
    starts = ends - length_row
    doc = jnp.sum((position[:, None] >= ends[None, :]).astype(jnp.int32), axis=1)
    seq_ids = jnp.arange(length_row.shape[0], dtype=jnp.int32)
    start = jnp.sum(jnp.where(doc[:, None] == seq_ids[None, :], starts[None, :], 0), axis=1)
    return (doc, start)


def places(pair_row, length_row, rows, owners):
    count = pair_row.shape[0]
    half = rows // 2
    ids = jnp.arange(count, dtype=jnp.int32)
    pair = jnp.sum(jnp.where(owners[:, None] == ids[None, :], pair_row[None, :], 0), axis=1)
    block = jnp.stack([pair, 2 * count - 1 - pair], axis=1)
    offset = jnp.arange(half, dtype=jnp.int32)
    position = (block[:, :, None] * half + offset[None, None, :]).reshape(-1)
    doc, start = doc_of(position, length_row)
    return (position, doc, start)


def ring_order(n):
    return list(range(0, n, 2)) + list(range(n - 1, 0, -2)) if n % 2 == 0 else list(range(n))


def ring_perms(n):
    order = ring_order(n)
    ahead = [(order[i], order[(i + 1) % n]) for i in range(n)]
    return (ahead, [(b, a) for a, b in ahead])


def ring_offsets(n):
    offsets = [0]
    for k in range(1, n // 2):
        offsets += [-k, k]
    return offsets + [-(n // 2)]


def ring_owners(n, place):
    order = jnp.array(ring_order(n), dtype=jnp.int32)
    ids = jnp.arange(n, dtype=jnp.int32)
    mine = jnp.sum(jnp.where(order == place, ids, 0))
    at = (mine + jnp.array(ring_offsets(n), dtype=jnp.int32)) % n
    return jnp.sum(jnp.where(at[:, None] == ids[None, :], order[None, :], 0), axis=1)


def ring_gather(block, early=None):
    n = lax.axis_size("ctx")
    ahead, back = ring_perms(n)
    moving = [block, block]
    blocks = [block]
    for step in range(n // 2):
        if 2 * (step + 1) == n:
            half = block.shape[0] // 2
            moving = [moving[0][:half], moving[1][half:]]
        moving = [lax.ppermute(moving[0], "ctx", ahead), lax.ppermute(moving[1], "ctx", back)]
        if early:
            moving = early(step, moving)
        blocks += moving
    return blocks


def add_pair(moving, partial, rows, slots, spans):
    def kernel(one_ref, other_ref, one_own, other_own, one_out, other_out):
        for ref, own, out, (first, last) in (
            (one_ref, one_own, one_out, spans[0]),
            (other_ref, other_own, other_out, spans[1]),
        ):
            if last - first < rows:
                out[...] = own[...]
            here = slice(first, last)
            out[here, :] = (ref[...].astype(F32) + own[here, :].astype(F32)).astype(BF16)

    def whole(shape, at):
        return pl.BlockSpec(shape, lambda i: (at, 0))

    shape = (rows, partial.shape[1])
    return pl.pallas_call(
        kernel,
        grid=(1,),
        in_specs=[whole(v.shape, 0) for v in moving] + [whole(shape, at) for at in slots],
        out_specs=[whole(shape, 0)] * 2,
        out_shape=[jax.ShapeDtypeStruct(shape, BF16)] * 2,
        cost_estimate=cost(moving, [jax.ShapeDtypeStruct(shape, BF16)] * 4),
        compiler_params=room(12 * rows * partial.shape[1] * 2),
    )(*moving, partial, partial)


def ring_scatter(partial, rows, early=None):
    n = lax.axis_size("ctx")
    ahead, back = ring_perms(n)
    offsets = ring_offsets(n)
    half = n // 2
    mid = rows // 2
    last = offsets.index(-half) * rows
    moving = [partial[last : last + mid], partial[last + mid : last + rows]]
    spans = [(0, mid), (mid, rows)]
    for step in range(half):
        moving = [lax.ppermute(moving[0], "ctx", ahead), lax.ppermute(moving[1], "ctx", back)]
        if early:
            moving = early(step, moving)
        k = half - 1 - step
        if k:
            slots = [offsets.index(k), offsets.index(-k)]
            moving = add_pair(moving, partial, rows, slots, spans)
            spans = [(0, rows), (0, rows)]
    if half == 1:
        moving = [jnp.concatenate(moving, axis=0), jnp.zeros((rows, partial.shape[1]), BF16)]
    return (partial, *moving)


def joined_dot(blocks, weight, nt=False, tile=256, dtype=F32):
    total, depth = sum(v.shape[0] for v in blocks), blocks[0].shape[1]
    columns = weight.shape[0] if nt else weight.shape[1]
    tile = min(tile, columns)
    count = len(blocks)

    def kernel(*refs):
        w_ref, joined, out = refs[count:]

        @pl.when(pl.program_id(0) == 0)
        def _():
            at = 0
            for ref in refs[:count]:
                joined[at : at + ref.shape[0], :] = ref[...]
                at += ref.shape[0]

        dims = (((1,), (1 if nt else 0,)), ((), ()))
        out[...] = lax.dot_general(
            joined[...], w_ref[...], dims, preferred_element_type=F32
        ).astype(dtype)

    once = pl.Buffered(1)
    outs = [
        jax.ShapeDtypeStruct((total, depth), BF16),
        jax.ShapeDtypeStruct((total, columns), dtype),
    ]
    w_spec = (
        pl.BlockSpec((tile, depth), lambda j: (j, 0))
        if nt
        else pl.BlockSpec((depth, tile), lambda j: (0, j))
    )
    return pl.pallas_call(
        kernel,
        grid=(columns // tile,),
        in_specs=[
            pl.BlockSpec(v.shape, lambda j: (0, 0), pipeline_mode=once) for v in blocks
        ]
        + [w_spec],
        out_specs=[
            pl.BlockSpec((total, depth), lambda j: (0, 0), pipeline_mode=once),
            pl.BlockSpec((total, tile), lambda j: (0, j)),
        ],
        out_shape=outs,
        cost_estimate=cost((*blocks, weight), outs, 2 * total * depth * columns),
        compiler_params=room(4 * total * depth, 4 * tile * depth, 12 * total * tile),
    )(*blocks, weight)


def ffn_specs(blocks, width):
    total, depth = sum(v.shape[0] for v in blocks), blocks[0].shape[1]
    tile = min(256 if total <= 1024 else 128, width)
    once = pl.Buffered(1)
    whole = [pl.BlockSpec(v.shape, lambda j: (0, 0), pipeline_mode=once) for v in blocks]
    joined = pl.BlockSpec((total, depth), lambda j: (0, 0), pipeline_mode=once)
    return (total, depth, tile, whole, joined, pl.BlockSpec((total, tile), lambda j: (0, j)))


def join_once(refs, joined):
    @pl.when(pl.program_id(0) == 0)
    def _():
        at = 0
        for ref in refs:
            joined[at : at + ref.shape[0], :] = ref[...]
            at += ref.shape[0]


def ffn_enter(blocks, weight):
    width = weight.shape[1] // 2
    total, depth, tile, whole, joined_spec, cut = ffn_specs(blocks, width)
    count, steps = len(blocks), width // tile

    def kernel(*refs):
        wg_ref, wu_ref, joined, gate_ref, up_ref, hidden_ref = refs[count:]
        join_once(refs[:count], joined)
        gate = jnp.dot(joined[...], wg_ref[...], preferred_element_type=F32)
        up = jnp.dot(joined[...], wu_ref[...], preferred_element_type=F32)
        gate_ref[...] = gate
        up_ref[...] = up
        hidden_ref[...] = (gate * jax.nn.sigmoid(gate) * up).astype(BF16)

    outs = [
        jax.ShapeDtypeStruct((total, depth), BF16),
        jax.ShapeDtypeStruct((total, width), F32),
        jax.ShapeDtypeStruct((total, width), F32),
        jax.ShapeDtypeStruct((total, width), BF16),
    ]
    w_specs = [
        pl.BlockSpec((depth, tile), lambda j: (0, j)),
        pl.BlockSpec((depth, tile), lambda j: (0, steps + j)),
    ]
    return pl.pallas_call(
        kernel,
        grid=(steps,),
        in_specs=whole + w_specs,
        out_specs=[joined_spec, cut, cut, cut],
        out_shape=outs,
        cost_estimate=cost((*blocks, weight), outs, 4 * total * depth * width),
        compiler_params=room(4 * total * depth, 8 * tile * depth, 36 * total * tile),
    )(*blocks, weight, weight)


def ffn_back(blocks, weight, gate, up):
    width = weight.shape[0]
    total, depth, tile, whole, joined_spec, cut = ffn_specs(blocks, width)
    count = len(blocks)

    def kernel(*refs):
        w_ref, gate_ref, up_ref, joined, d_gate_ref, d_up_ref = refs[count:]
        join_once(refs[:count], joined)
        d_hidden = lax.dot_general(
            joined[...], w_ref[...], (((1,), (1,)), ((), ())), preferred_element_type=F32
        )
        d_hidden = d_hidden.astype(BF16).astype(F32)
        gate = gate_ref[...]
        open_gate = jax.nn.sigmoid(gate)
        part = d_hidden * open_gate
        d_up_ref[...] = (part * gate).astype(BF16)
        d_gate_ref[...] = (part * up_ref[...] * (1.0 + gate * (1.0 - open_gate))).astype(BF16)

    outs = [jax.ShapeDtypeStruct((total, depth), BF16)]
    outs += [jax.ShapeDtypeStruct((total, width), BF16)] * 2
    return pl.pallas_call(
        kernel,
        grid=(width // tile,),
        in_specs=whole + [pl.BlockSpec((tile, depth), lambda j: (j, 0)), cut, cut],
        out_specs=[joined_spec, cut, cut],
        out_shape=outs,
        cost_estimate=cost((*blocks, weight, gate, up), outs, 2 * total * depth * width),
        compiler_params=room(4 * total * depth, 4 * tile * depth, 40 * total * tile),
    )(*blocks, weight, gate, up)


def ffn_leave(d_gate, d_up, weight):
    total, width = d_gate.shape
    depth, tile = weight.shape[0], 256

    def kernel(g_ref, u_ref, w_ref, out_ref):
        nt = (((1,), (1,)), ((), ()))
        out = lax.dot_general(g_ref[...], w_ref[:, :width], nt, preferred_element_type=F32)
        out += lax.dot_general(u_ref[...], w_ref[:, width:], nt, preferred_element_type=F32)
        out_ref[...] = out.astype(BF16)

    out = jax.ShapeDtypeStruct((total, depth), BF16)
    resident = pl.BlockSpec((total, width), lambda j: (0, 0), pipeline_mode=pl.Buffered(1))
    return pl.pallas_call(
        kernel,
        grid=(depth // tile,),
        in_specs=[resident, resident, pl.BlockSpec((tile, 2 * width), lambda j: (j, 0))],
        out_specs=pl.BlockSpec((total, tile), lambda j: (0, j)),
        out_shape=out,
        cost_estimate=cost((d_gate, d_up, weight), [out], 4 * total * depth * width),
        compiler_params=room(4 * total * width, 8 * tile * width, 12 * total * tile),
    )(d_gate, d_up, weight)


def after(value, *others):
    return lax.optimization_barrier((value, *others))[0]


def cost(ins, outs, flops=0, exps=0):
    moved = sum(v.size * v.dtype.itemsize for v in (*ins, *outs))
    return pl.CostEstimate(flops=flops, bytes_accessed=moved, transcendentals=exps)


def room(*sizes):
    return pltpu.CompilerParams(vmem_limit_bytes=60 * MIB)


def bytes_of(*arrays):
    return sum(v.size * v.dtype.itemsize for v in arrays)


def place_call(kernel, place, ins, outs, scratch=()):
    vmem = pl.BlockSpec(memory_space=pltpu.VMEM)
    return pl.pallas_call(
        kernel,
        in_specs=[pl.BlockSpec(memory_space=pltpu.SMEM)] + [vmem] * len(ins),
        out_specs=[vmem] * len(outs),
        out_shape=outs,
        scratch_shapes=scratch,
        cost_estimate=cost(ins, outs),
        compiler_params=room(bytes_of(*ins, *outs) * 3 // 2),
    )(place.reshape(1), *ins)


def shifted(place_ref, k, n):
    return lax.rem(place_ref[0] + (k + n), n)


def lanes_at(index, width):
    return pl.ds(pl.multiple_of(index * width, width), width)


def cut_columns(weight, parts, place, n):
    rows = weight.shape[0]
    width = weight.shape[1] // parts // n

    def kernel(place_ref, w_ref, *outs):
        for k in range(n):
            dest = shifted(place_ref, k, n)
            for p in range(parts):
                outs[k][:, p * width : (p + 1) * width] = w_ref[:, lanes_at(p * n + dest, width)]

    piece = jax.ShapeDtypeStruct((rows, parts * width), weight.dtype)
    return place_call(kernel, place, [weight], [piece] * n)


def cut_rows(v, place, n):
    rows = v.shape[0] // n

    def kernel(place_ref, v_ref, *outs):
        for k in range(n):
            outs[k][...] = v_ref[lanes_at(shifted(place_ref, k, n), rows), :]

    piece = jax.ShapeDtypeStruct((rows, v.shape[1]), v.dtype)
    return place_call(kernel, place, [v], [piece] * n)


def join_rows(pieces, place, n):
    rows, width = pieces[0].shape

    def kernel(place_ref, *refs):
        for k in range(n):
            refs[n][lanes_at(shifted(place_ref, -k, n), rows), :] = refs[k][...]

    whole = jax.ShapeDtypeStruct((n * rows, width), pieces[0].dtype)
    return place_call(kernel, place, pieces, [whole])[0]


def join_columns(lists, parts, place, dtype):
    n = len(lists[0])
    rows, width = lists[0][0].shape[0], lists[0][0].shape[1] // parts

    def kernel(place_ref, *refs):
        for i in range(len(lists)):
            for k in range(n):
                source = shifted(place_ref, -k, n)
                for p in range(parts):
                    cut = refs[i * n + k][:, p * width : (p + 1) * width]
                    here = lanes_at((i * parts + p) * n + source, width)
                    refs[-1][:, here] = cut.astype(dtype)

    whole = jax.ShapeDtypeStruct((rows, len(lists) * parts * n * width), dtype)
    return place_call(kernel, place, [v for one in lists for v in one], [whole])[0]


def send_one(pieces, k, *ties):
    n = len(pieces)
    return lax.ppermute(after(pieces[k], *ties), "ctx", [(i, (i + k) % n) for i in range(n)])


def send_on(pieces):
    got = [pieces[0]]
    for k in range(1, len(pieces)):
        got.append(send_one(pieces, k, *got[max(k - 4, 0) : max(k - 3, 0)]))
    return got


def send_columns(weight, parts):
    n = lax.axis_size("ctx")
    rows = weight.shape[0]
    width = weight.shape[1] // parts // n
    if n <= 8:
        return send_on(cut_columns(weight, parts, lax.axis_index("ctx"), n))
    cut = weight.reshape(rows, parts, n, width).transpose(2, 0, 1, 3)
    return [lax.all_to_all(cut.reshape(n, rows, parts * width), "ctx", 0, 0, tiled=True)]


def take_columns(sent):
    if len(sent) == 1:
        return sent[0].reshape(-1, sent[0].shape[-1])
    return join_rows(sent, lax.axis_index("ctx"), len(sent))


def send_rows(mine):
    n = lax.axis_size("ctx")
    if n <= 8:
        return send_on(cut_rows(mine, lax.axis_index("ctx"), n))
    return [lax.all_to_all(mine.reshape(n, -1, mine.shape[1]), "ctx", 0, 0, tiled=True)]


def take_rows(lists, parts):
    if len(lists[0]) > 1:
        return join_columns(lists, parts, lax.axis_index("ctx"), F32)
    wholes = []
    for (sent,) in lists:
        n, rows = sent.shape[:2]
        got = sent.reshape(n, rows, parts, -1).transpose(1, 2, 0, 3)
        wholes.append(got.reshape(rows, -1).astype(F32))
    return jnp.concatenate(wholes, axis=1)


def gather_groups(v):
    return lax.all_gather(v, "fsdp", axis=0, tiled=True)


def scatter_groups(v):
    return lax.psum_scatter(v, "fsdp", scatter_dimension=0, tiled=True)


def far(v):
    return lax.ppermute(v, "fsdp", [(i, i ^ 2) for i in range(4)])


def near(v):
    return lax.ppermute(v, "fsdp", [(i, i ^ 1) for i in range(4)])


def in_order(held):
    me = lax.axis_index("fsdp")
    out = jnp.zeros((4,) + held[0].shape, held[0].dtype)
    for k, h in enumerate(held):
        out = lax.dynamic_update_slice_in_dim(out, h[None], me ^ k, 0)
    return out.reshape(4 * held[0].shape[0], held[0].shape[1])


def cut_groups(v):
    me = lax.axis_index("fsdp")
    rows = v.shape[0] // 4
    return [lax.dynamic_slice_in_dim(v, (me ^ k) * rows, rows, 0) for k in range(4)]


def add_low(got, own):
    return (got.astype(F32) + own.astype(F32)).astype(BF16)


def weight_share(gradient, shard_rows):
    partial_rows = lax.psum_scatter(
        gradient.astype(BF16), "ctx", scatter_dimension=0, tiled=True
    )
    return lax.psum_scatter(partial_rows, "fsdp", scatter_dimension=0, tiled=True).astype(F32)


def spread_lanes(v, n, m):
    w = D // (n * m)
    cuts = [v[:, (c * m + f) * w : (c * m + f + 1) * w] for f in range(m) for c in range(n)]
    return jnp.concatenate(cuts, axis=1)


def unspread_lanes(v, n, m):
    return spread_lanes(v, m, n)


def sum_all(v):
    for axis in ("ctx", "fsdp"):
        n = lax.axis_size(axis)
        if n & (n - 1):
            v = lax.psum(v, axis)
            continue
        step = 1
        while step < n:
            v = v + lax.ppermute(v, axis, [(i, i ^ step) for i in range(n)])
            step *= 2
    return v


LANES = 128
HC_ROWS = 32


def lanes_of(rows):
    return lax.broadcasted_iota(jnp.int32, (rows, LANES), 1)


def put(held, lane, at, column):
    return jnp.where(lane == at, column, held)


def mean_of(v):
    return jnp.sum(v, axis=1, keepdims=True) * (1.0 / D)


def stream_parts(ref):
    return [ref[:, i * D : (i + 1) * D].astype(F32) for i in range(STREAMS)]


def mixed(parts, coef, branch):
    outs = []
    for j in range(STREAMS):
        total = coef[:, 8 * j + 5 : 8 * j + 6] * branch
        for i in range(STREAMS):
            total = total + coef[:, 8 * i + 1 + j : 8 * i + 2 + j] * parts[i]
        outs.append(total)
    return outs


def branch_grad(parts, coef):
    return sum(coef[:, 8 * j + 5 : 8 * j + 6] * parts[j] for j in range(STREAMS))


def layer_in(parts, coef):
    return sum(coef[:, 8 * i : 8 * i + 1] * parts[i] for i in range(STREAMS))


def enter(parts, wpack, static):
    rows = parts[0].shape[0]
    lane = lanes_of(rows)
    aux = jnp.zeros((rows, LANES), F32)
    pieces = ([], [], [])
    for i in range(STREAMS):
        mean = mean_of(parts[i])
        cent = parts[i] - mean
        rstd = lax.rsqrt(mean_of(cent * cent) + eps)
        left = cent * rstd
        for piece in pieces:
            piece.append(left.astype(BF16))
            left = left - piece[-1].astype(F32)
        aux = put(aux, lane, 8 * i + 6, mean)
        aux = put(aux, lane, 8 * i + 7, rstd)
    dims = (((1,), (1,)), ((), ()))
    proj = sum(
        lax.dot_general(jnp.concatenate(p, axis=0), wpack, dims, preferred_element_type=F32)
        for p in pieces[::-1]
    )
    proj = proj + pltpu.roll(proj, LANES - 32, 1) + pltpu.roll(proj, LANES - 64, 1)
    for i in range(STREAMS):
        own = jnp.where(lane < 6, proj[i * rows : (i + 1) * rows], 0.0)
        aux += own if i == 0 else pltpu.roll(own, 8 * i, 1)
    coef = static + jnp.tanh(aux)
    x = layer_in(parts, coef)
    mean = mean_of(x)
    cent = x - mean
    rstd = lax.rsqrt(mean_of(cent * cent) + eps)
    aux = put(aux, lane, 32, mean)
    aux = put(aux, lane, 33, rstd)
    return (aux, coef, cent * rstd)


def leave_grads(parts, grads, branch):
    rows = parts[0].shape[0]
    lane = lanes_of(rows)
    red = jnp.zeros((rows, LANES), F32)
    for j in range(STREAMS):
        red = put(red, lane, 8 * j + 5, jnp.sum(grads[j] * branch, axis=1, keepdims=True))
        for i in range(STREAMS):
            red = put(
                red, lane, 8 * i + 1 + j, jnp.sum(parts[i] * grads[j], axis=1, keepdims=True)
            )
    return red


def enter_back(parts, grads, aux, coef, red, du, wpack, normed_ref, dz_ref, stat_ref, step):
    rows = parts[0].shape[0]
    lane = lanes_of(rows)
    x = layer_in(parts, coef)
    rx = aux[:, 33:34]
    nx = (x - aux[:, 32:33]) * rx
    dx = rx * (du - mean_of(du) - nx * mean_of(du * nx))
    for i in range(STREAMS):
        red = put(red, lane, 8 * i, jnp.sum(parts[i] * dx, axis=1, keepdims=True))
    used = (lane < 8 * STREAMS) & (lane % 8 < 6)
    slope = jnp.tanh(aux)
    dz = jnp.where(used, red * (1.0 - slope * slope), 0.0)
    stat_ref[0:1, :] += jnp.sum(red, axis=0, keepdims=True)
    dz_ref[pl.ds(step * rows, rows), :] = dz
    both = dz * aux
    packed = []
    for i in range(STREAMS):
        own = dz if i == 0 else pltpu.roll(dz, LANES - 8 * i, 1)
        own = jnp.where(lane < 6, own, 0.0)
        top = own.astype(BF16).astype(F32)
        packed.append((top + pltpu.roll(top, 32, 1) + pltpu.roll(own - top, 96, 1)).astype(BF16))
    dn_all = lax.dot_general(
        jnp.concatenate(packed, axis=0), wpack, (((1,), (0,)), ((), ())), preferred_element_type=F32
    )
    outs = []
    total_rows = dz_ref.shape[0]
    for i in range(STREAMS):
        mean, rstd = aux[:, 8 * i + 6 : 8 * i + 7], aux[:, 8 * i + 7 : 8 * i + 8]
        normed = (parts[i] - mean) * rstd
        normed_ref[pl.ds(i * total_rows + step * rows, rows), :] = normed.astype(BF16)
        dn = dn_all[i * rows : (i + 1) * rows]
        own = (lane >= 8 * i) & (lane < 8 * i + 6)
        along = jnp.sum(jnp.where(own, both, 0.0), axis=1, keepdims=True) * (1.0 / D)
        total = coef[:, 8 * i : 8 * i + 1] * dx + rstd * (dn - mean_of(dn) - normed * along)
        for j in range(STREAMS):
            total = total + coef[:, 8 * i + 1 + j : 8 * i + 2 + j] * grads[j]
        outs.append(total)
    return outs


def finish_hc(normed_ref, dz_ref, stat_ref, hc_ref):
    across = dz_ref[...].T
    left = jnp.concatenate([across[8 * i : 8 * i + 8] for i in range(STREAMS)], axis=1)
    top = left.astype(BF16)
    low = (left - top.astype(F32)).astype(BF16)
    both = lax.dot_general(
        jnp.concatenate([top, low], axis=0),
        normed_ref[...],
        (((1,), (0,)), ((), ())),
        preferred_element_type=F32,
    )
    hc_ref[...] = both[0:8] + both[8:16]
    hc_ref[6:7, 0:LANES] = stat_ref[0:1, :]


def sum_of(refs):
    return sum(ref[...].astype(F32) for ref in refs)


def first_kernel(order, s_ref, w_ref, static_ref, u_ref, aux_ref):
    aux, _, u = enter(stream_parts(s_ref), w_ref[...], static_ref[0:1, :])
    u = u.astype(BF16)
    u_ref[...] = spread_lanes(u, *order) if order else u
    aux_ref[...] = aux


def middle_kernel(order, s_ref, c_ref, y_ref, aux0_ref, w_ref, static_ref, u_ref, dy_ref, aux_ref):
    coef0 = static_ref[0:1, :] + jnp.tanh(aux0_ref[...])
    mid = mixed(stream_parts(s_ref), coef0, y_ref[...])
    aux, coef, u = enter(mid, w_ref[...], static_ref[1:2, :])
    u_ref[...] = spread_lanes(u.astype(BF16), *order)
    aux_ref[...] = aux
    dy_ref[...] = branch_grad(stream_parts(c_ref), coef).astype(BF16)


def out_kernel(
    s_ref, c_ref, y_ref, y2a_ref, y2b_ref, y2c_ref, aux0_ref, aux1_ref, static_ref,
    out_ref, red_ref,
):
    coef0 = static_ref[0:1, :] + jnp.tanh(aux0_ref[...])
    coef1 = static_ref[1:2, :] + jnp.tanh(aux1_ref[...])
    mid = mixed(stream_parts(s_ref), coef0, y_ref[...])
    y2 = sum_of((y2a_ref, y2b_ref, y2c_ref))
    for j, total in enumerate(mixed(mid, coef1, y2)):
        out_ref[:, j * D : (j + 1) * D] = total.astype(BF16)
    red_ref[...] = leave_grads(mid, stream_parts(c_ref), y2)


def back_kernel(
    order, s_ref, c_ref, y_ref, dua_ref, dub_ref, duc_ref, red_ref, aux0_ref, aux1_ref, w_ref,
    static_ref, dmid_ref, dy_ref, hc_ref, normed_ref, dz_ref, stat_ref,
):
    step = pl.program_id(0)

    @pl.when(step == 0)
    def _():
        stat_ref[...] = jnp.zeros_like(stat_ref)

    coef0 = static_ref[0:1, :] + jnp.tanh(aux0_ref[...])
    aux1 = aux1_ref[...]
    coef1 = static_ref[1:2, :] + jnp.tanh(aux1)
    mid = mixed(stream_parts(s_ref), coef0, y_ref[...])
    du = unspread_lanes(sum_of((dua_ref, dub_ref, duc_ref)), *order)
    dmid = enter_back(
        mid, stream_parts(c_ref), aux1, coef1, red_ref[...], du, w_ref[...],
        normed_ref, dz_ref, stat_ref, step,
    )
    for j in range(STREAMS):
        dmid_ref[:, j * D : (j + 1) * D] = dmid[j]
    dy_ref[...] = branch_grad(dmid, coef0).astype(BF16)

    @pl.when(step == pl.num_programs(0) - 1)
    def _():
        finish_hc(normed_ref, dz_ref, stat_ref, hc_ref)


def red_kernel(s_ref, dmid_ref, y_ref, red_ref):
    red_ref[...] = leave_grads(stream_parts(s_ref), stream_parts(dmid_ref), y_ref[...])


def last_kernel(
    order, s_ref, dmid_ref, *refs
):
    du_refs = refs[:-9]
    red_ref, aux0_ref, w_ref, static_ref, ds_ref, hc_ref, normed_ref, dz_ref, stat_ref = refs[-9:]
    step = pl.program_id(0)

    @pl.when(step == 0)
    def _():
        stat_ref[...] = jnp.zeros_like(stat_ref)

    aux0 = aux0_ref[...]
    coef0 = static_ref[0:1, :] + jnp.tanh(aux0)
    parts, grads = stream_parts(s_ref), stream_parts(dmid_ref)
    du = sum_of(du_refs)
    if order:
        du = unspread_lanes(du, *order)
    ds = enter_back(
        parts, grads, aux0, coef0, red_ref[...], du, w_ref[...],
        normed_ref, dz_ref, stat_ref, step,
    )
    for j in range(STREAMS):
        ds_ref[:, j * D : (j + 1) * D] = ds[j].astype(BF16)

    @pl.when(step == pl.num_programs(0) - 1)
    def _():
        finish_hc(normed_ref, dz_ref, stat_ref, hc_ref)


def row_call(kernel, rows, ins, outs, hc=False):
    tile = HC_ROWS

    def cut(columns):
        return pl.BlockSpec((tile, columns), lambda i: (i, 0))

    def whole(shape):
        return pl.BlockSpec(shape, lambda i: (0, 0))

    in_specs = [cut(a.shape[1]) if by_rows else whole(a.shape) for a, by_rows in ins]
    out_specs = [cut(columns) for columns, _ in outs]
    out_shape = [jax.ShapeDtypeStruct((rows, columns), dtype) for columns, dtype in outs]
    scratch = []
    if hc:
        out_specs.append(whole((8, D)))
        out_shape.append(jax.ShapeDtypeStruct((8, D), F32))
        scratch = [
            pltpu.VMEM((STREAMS * rows, D), BF16),
            pltpu.VMEM((rows, LANES), F32),
            pltpu.VMEM((8, LANES), F32),
        ]
    return pl.pallas_call(
        kernel,
        grid=(rows // tile,),
        in_specs=in_specs,
        out_specs=out_specs,
        out_shape=out_shape,
        scratch_shapes=scratch,
        cost_estimate=cost([a for a, _ in ins], out_shape, 100 * rows * STREAMS * D),
        compiler_params=pltpu.CompilerParams(vmem_limit_bytes=60 * MIB),
    )(*[a for a, _ in ins])


def pack_weight(weight):
    across = jnp.pad(weight.T, ((0, 26), (0, 0)))
    top = lax.reduce_precision(across, 8, 7)
    mid = lax.reduce_precision(across - top, 8, 7)
    return jnp.concatenate([top, mid, across - top - mid, top], axis=0).astype(BF16)


Q_ROWS = 256


def turn(v, cosine, sine):
    return v * cosine + pltpu.roll(v, HEAD_DIM // 2, 1) * sine


def attend_kernel(
    q_ref, k_ref, v_ref, cos_ref, sin_ref, qpos_ref, qstart_ref, kpos_ref,
    o_ref, lse_ref, qr_ref, kr_ref, vb_ref,
):
    at = pl.program_id(1)

    @pl.when(at == 0)
    def _():
        kr_ref[...] = turn(k_ref[...], cos_ref[...], sin_ref[...]).astype(BF16)
        vb_ref[...] = v_ref[...].astype(BF16)

    here = pl.ds(at * Q_ROWS, Q_ROWS)
    query = turn(q_ref[...], cos_ref[here, :], sin_ref[here, :]).astype(BF16)
    qr_ref[...] = query
    scores = (
        lax.dot_general(query, kr_ref[...], (((1,), (1,)), ((), ())), preferred_element_type=F32)
        * SCALE
    )
    kpos = kpos_ref[0:1, :]
    keep = (kpos <= qpos_ref[...]) & (kpos >= qstart_ref[...])
    scores = jnp.where(keep, scores, -1e30)
    top = jnp.max(scores, axis=1, keepdims=True)
    grown = jnp.exp(scores - top)
    total = jnp.sum(grown, axis=1, keepdims=True)
    out = jnp.dot((grown / total).astype(BF16), vb_ref[...], preferred_element_type=F32)
    o_ref[...] = out.astype(BF16)
    lse_ref[...] = jnp.broadcast_to(top + jnp.log(total), lse_ref.shape)


def attend_back_kernel(
    q_ref, k_ref, v_ref, do_ref, lse_ref, cos_ref, sin_ref, qpos_ref, qstart_ref, kpos_ref,
    dq_ref, dk_ref, dv_ref, dk_sum, dv_sum,
):
    at = pl.program_id(1)

    @pl.when(at == 0)
    def _():
        dk_sum[...] = jnp.zeros_like(dk_sum)
        dv_sum[...] = jnp.zeros_like(dv_sum)

    here = pl.ds(at * Q_ROWS, Q_ROWS)
    query, keys, d_out = q_ref[...], k_ref[...], do_ref[...]
    nt = (((1,), (1,)), ((), ()))
    tn = (((0,), (0,)), ((), ()))
    scores = lax.dot_general(query, keys, nt, preferred_element_type=F32) * SCALE
    kpos = kpos_ref[0:1, :]
    keep = (kpos <= qpos_ref[...]) & (kpos >= qstart_ref[...])
    probs = jnp.where(keep, jnp.exp(scores - lse_ref[:, 0:1]), 0.0)
    d_probs = lax.dot_general(d_out, v_ref[...], nt, preferred_element_type=F32)
    delta = jnp.sum(probs * d_probs, axis=1, keepdims=True)
    ds = (probs * (d_probs - delta)).astype(BF16)
    dq = jnp.dot(ds, keys, preferred_element_type=F32) * SCALE
    dq_ref[...] = turn(dq, cos_ref[here, :], -sin_ref[here, :]).astype(BF16)
    dk_sum[...] += lax.dot_general(ds, query, tn, preferred_element_type=F32)
    dv_sum[...] += lax.dot_general(probs.astype(BF16), d_out, tn, preferred_element_type=F32)

    @pl.when(at == pl.num_programs(1) - 1)
    def _():
        dk_ref[...] = turn(dk_sum[...] * SCALE, cos_ref[...], -sin_ref[...]).astype(BF16)
        dv_ref[...] = dv_sum[...].astype(BF16)


def attention_specs(total):
    by_query = pl.BlockSpec((Q_ROWS, HEAD_DIM), lambda h, i: (i, h))
    by_head = pl.BlockSpec((total, HEAD_DIM), lambda h, i: (0, h))
    table = pl.BlockSpec((total, HEAD_DIM), lambda h, i: (0, 0))
    row = pl.BlockSpec((Q_ROWS, 1), lambda h, i: (i, 0))
    keys = pl.BlockSpec((8, total), lambda h, i: (0, 0))
    return (by_query, by_head, [table, table, row, row, keys])


def attend(qkv, heads, marks):
    total = qkv.shape[0]
    by_query, by_head, shared = attention_specs(total)

    def of(kind):
        return pl.BlockSpec((total, HEAD_DIM), lambda h, i: (0, kind * heads + h))

    low = jax.ShapeDtypeStruct((total, heads * HEAD_DIM), BF16)
    wide = jax.ShapeDtypeStruct((total, heads * HEAD_DIM), F32)
    return pl.pallas_call(
        attend_kernel,
        grid=(heads, total // Q_ROWS),
        in_specs=[by_query, of(1), of(2)] + shared,
        out_specs=[by_query, by_query, by_query, by_head, by_head],
        out_shape=[low, wide, low, low, low],
        cost_estimate=cost([qkv], [low] * 4, 4 * heads * total**2 * HEAD_DIM, heads * total**2),
        compiler_params=room(20 * Q_ROWS * total, 40 * total * HEAD_DIM),
    )(qkv, qkv, qkv, *marks)


def attend_back(query, keys, values, d_out, lse, heads, marks):
    total = query.shape[0]
    by_query, by_head, shared = attention_specs(total)
    low = jax.ShapeDtypeStruct((total, heads * HEAD_DIM), BF16)
    return pl.pallas_call(
        attend_back_kernel,
        grid=(heads, total // Q_ROWS),
        in_specs=[by_query, by_head, by_head, by_query, by_query] + shared,
        out_specs=[by_query, by_head, by_head],
        out_shape=[low, low, low],
        scratch_shapes=[pltpu.VMEM((total, HEAD_DIM), F32)] * 2,
        cost_estimate=cost([lse], [low] * 7, 10 * heads * total**2 * HEAD_DIM, heads * total**2),
        compiler_params=room(32 * Q_ROWS * total, 48 * total * HEAD_DIM),
    )(query, keys, values, d_out, lse, *marks)


def angles(inside):
    half = HEAD_DIM // 2
    freq = 10000.0 ** (-jnp.arange(half, dtype=F32) / half)
    angle = inside.astype(F32)[:, None] * freq[None, :]
    cosine, sine = jnp.cos(angle), jnp.sin(angle)
    return (jnp.concatenate([cosine, cosine], axis=1), jnp.concatenate([-sine, sine], axis=1))


class HeadAttention:
    def __init__(self, rows, w_qkv, w_out, pair_row, length_row):
        n = lax.axis_size("ctx")
        self.group = lax.axis_index("fsdp")
        self.rows, self.heads = rows, HEADS // n
        owners = ring_owners(n, lax.axis_index("ctx"))
        position, _, start = places(pair_row, length_row, rows, owners)
        cosine, sine = angles(position - start)
        kpos = jnp.broadcast_to(position[None, :], (8, position.shape[0]))
        self.marks = (cosine, sine, position[:, None], start[:, None], kpos)
        self.sent_qkv = send_columns(w_qkv, 3)
        self.w_out = w_out

    def to_tokens(self, heads_out):
        n = lax.axis_size("ctx")
        order, offsets = ring_order(n), ring_offsets(n)
        got = []
        for offset in offsets:
            at = offsets.index(-offset if 2 * offset != -n else offset)
            own = heads_out[at * self.rows : (at + 1) * self.rows]
            pairs = [(order[i], order[(i - offset) % n]) for i in range(n)]
            got.append(lax.ppermute(own, "ctx", pairs) if offset else own)
        return got

    def join_tokens(self, got):
        n, m = lax.axis_size("ctx"), lax.axis_size("fsdp")
        offsets, width = ring_offsets(n), got[0].shape[1]

        def kernel(place_ref, *refs):
            place = place_ref[0]
            mine = jnp.where(place % 2 == 0, place // 2, n - 1 - place // 2)
            held = refs[-1]
            for k, offset in enumerate(offsets):
                at = lax.rem(mine + offset + n, n)
                owner = jnp.where(at < n // 2, 2 * at, 2 * (n - 1 - at) + 1)
                held[:, lanes_at(owner, width)] = refs[k][...]
            refs[n][...] = spread_lanes(held[...], n, m)

        whole = jax.ShapeDtypeStruct((self.rows, n * width), got[0].dtype)
        scratch = [pltpu.VMEM(whole.shape, whole.dtype)]
        return place_call(kernel, lax.axis_index("ctx"), got, [whole], scratch)[0]

    def forward(self, u, w_gate_up, w_down):
        n, m = lax.axis_size("ctx"), lax.axis_size("fsdp")
        got = {}

        out_ctx = lax.all_gather(self.w_out, "ctx", axis=0, tiled=True)
        u, sent_qkv = lax.optimization_barrier((u, self.sent_qkv))

        def early(step, arrived):
            if step == 0:
                got["own"] = take_columns(sent_qkv)
                got["far"] = far(got["own"])
            if step == 1:
                arrived, got["far"] = lax.optimization_barrier((arrived, got["far"]))
                got["near"] = [near(got["own"]), near(got["far"])]
            if step == 2:
                arrived, got["near"], got["out"] = lax.optimization_barrier(
                    (arrived, got["near"], out_ctx)
                )
                held = [got["own"], got["near"][0], got["far"], got["near"][1]]
                got["cols"] = in_order(held)
            if step == 3:
                arrived, got["cols"] = lax.optimization_barrier((arrived, got["cols"]))
            return arrived

        blocks = ring_gather(u, early)
        self.qkv_cols = got["cols"]
        out_all = lax.all_gather(got["out"], "fsdp", axis=0, tiled=True)
        down_rows = gather_groups(after(w_down, *blocks))
        cut = cut_columns(after(w_gate_up, *blocks), 2, lax.axis_index("ctx"), n)
        self.u_all, qkv = joined_dot(blocks, self.qkv_cols)
        sent = [cut[0]] + [send_one(cut, k) for k in range(1, 4)]
        self.o, self.lse, self.q, self.k, self.v = attend(qkv, self.heads, self.marks)
        o, *sent = lax.optimization_barrier((self.o, *sent))
        sent_o = self.to_tokens(o)
        sent += [send_one(cut, k, o) for k in range(4, n)]
        held = out_all.reshape(m, n, -1, D)
        held = lax.dynamic_slice_in_dim(held, lax.axis_index("ctx"), 1, 1)
        self.out_rows = held.reshape(-1, D)
        y = jnp.dot(self.join_tokens(sent_o), out_all, preferred_element_type=F32)
        y, *sent[:6] = lax.optimization_barrier((y, *sent[:6]))
        return (y, sent, down_rows)

    def backward(self, dy, grad_gate, grad_up):
        got = {}

        def early_dy(step, arrived):
            if step == 2:
                arrived, got["gate"] = lax.optimization_barrier((arrived, grad_gate))
            return arrived

        blocks = ring_gather(dy, early_dy)
        dy_all, d_out = joined_dot(blocks, self.out_rows, nt=True, dtype=BF16)
        sent_gate = send_rows(after(got["gate"], dy_all))
        d_out, grad_up = lax.optimization_barrier((d_out, grad_up))
        dq, dk, dv = attend_back(self.q, self.k, self.v, d_out, self.lse, self.heads, self.marks)
        d_qkv = jnp.concatenate([dq, dk, dv], axis=1)
        partial = jnp.einsum(
            "tc,dc->td", d_qkv, self.qkv_cols, preferred_element_type=F32
        ).astype(BF16)


        def early(step, arrived):
            if step == 0:
                u_all = after(self.u_all, partial)
                g = jnp.einsum("td,tc->dc", u_all, d_qkv, preferred_element_type=F32)
                got["qkv"] = scatter_groups(g.astype(BF16))
            if step == 1:
                o, dy_now = after([self.o, dy_all], arrived)
                g = jnp.einsum("te,td->ed", o, dy_now, preferred_element_type=F32)
                got["out"] = scatter_groups(g.astype(BF16)).astype(F32)
            return arrived

        du = ring_scatter(partial, self.rows, early)
        du, sent_gate = lax.optimization_barrier((du, sent_gate))
        sent_up = send_rows(after(grad_up, du[1]))
        sent_qkv = send_rows(after(got["qkv"], du[1]))
        return (
            du,
            lambda tie: take_rows([after(sent_qkv, tie)], 3),
            got["out"],
            take_rows([sent_gate, sent_up], 1),
        )


def rotate(v, inside, sign):
    half = v.shape[-1] // 2
    freq = 10000.0 ** (-jnp.arange(half, dtype=F32) / half)
    angle = inside.astype(F32)[:, None] * freq[None, :]
    cosine = jnp.cos(angle)[:, None, :]
    sine = sign * jnp.sin(angle)[:, None, :]
    first, second = (v[..., :half], v[..., half:])
    return jnp.concatenate(
        [first * cosine - second * sine, second * cosine + first * sine], axis=-1
    )


class TokenAttention:
    def __init__(self, rows, w_qkv, w_out, pair_row, length_row):
        n = lax.axis_size("ctx")
        place = lax.axis_index("ctx")
        self.rows = rows
        owners = jnp.arange(n, dtype=jnp.int32)
        kpos, kdoc, kstart = places(pair_row, length_row, rows, owners)

        def own(v):
            return lax.dynamic_slice_in_dim(v, place * rows, rows)

        self.inside = own(kpos - kstart)
        self.keep = (kpos[None, :] <= own(kpos)[:, None]) & (kdoc[None, :] == own(kdoc)[:, None])
        self.w_qkv, self.w_out = w_qkv, w_out

    def gathered(self, weight):
        return lax.all_gather(weight, ("ctx", "fsdp"), axis=0, tiled=True)

    def scores(self):
        scores = jnp.einsum("qhe,hke->hqk", self.q, self.k, preferred_element_type=F32) * SCALE
        return jnp.where(self.keep[None], scores, -1e30)

    def forward(self, u, w_gate_up, w_down):
        rows, shape = self.rows, (self.rows, HEADS, HEAD_DIM)
        self.u = u
        qkv = jnp.dot(u, self.gathered(self.w_qkv), preferred_element_type=F32)
        self.q = rotate(qkv[:, :D].reshape(shape), self.inside, 1.0).astype(BF16)
        key = rotate(qkv[:, D : 2 * D].reshape(shape), self.inside, 1.0).astype(BF16)
        value = qkv[:, 2 * D :].reshape(shape).astype(BF16)
        self.k = lax.all_gather(key.transpose(1, 0, 2), "ctx", axis=1, tiled=True)
        self.v = lax.all_gather(value.transpose(1, 0, 2), "ctx", axis=1, tiled=True)
        scores = self.scores()
        top = jnp.max(scores, axis=-1, keepdims=True)
        self.lse = top + jnp.log(jnp.sum(jnp.exp(scores - top), axis=-1, keepdims=True))
        probs = jnp.exp(scores - self.lse).astype(BF16)
        attended = jnp.einsum("hqk,hke->qhe", probs, self.v, preferred_element_type=F32)
        self.o = attended.reshape(rows, D).astype(BF16)
        y = jnp.dot(self.o, self.gathered(self.w_out), preferred_element_type=F32)
        return (y, send_columns(w_gate_up, 2), gather_groups(w_down))

    def backward(self, dy, grad_gate, grad_up):
        rows = self.rows
        d_out = jnp.einsum(
            "td,ed->te", dy, self.gathered(self.w_out), preferred_element_type=F32
        )
        d_out = d_out.astype(BF16).reshape(rows, HEADS, HEAD_DIM)
        grad_out = jnp.einsum("te,td->ed", self.o, dy, preferred_element_type=F32)
        again = jnp.exp(self.scores() - self.lse)
        d_probs = jnp.einsum("qhe,hke->hqk", d_out, self.v, preferred_element_type=F32)
        delta = jnp.sum(again * d_probs, axis=-1, keepdims=True)
        ds = (again * (d_probs - delta)).astype(BF16)
        dq = jnp.einsum("hqk,hke->qhe", ds, self.k, preferred_element_type=F32) * SCALE
        dk_all = jnp.einsum("hqk,qhe->hke", ds, self.q, preferred_element_type=F32) * SCALE
        dv_all = jnp.einsum(
            "hqk,qhe->hke", again.astype(BF16), d_out, preferred_element_type=F32
        )

        def shared(v):
            mine = lax.psum_scatter(v.astype(BF16), "ctx", scatter_dimension=1, tiled=True)
            return mine.astype(F32).transpose(1, 0, 2)

        dk, dv = shared(dk_all), shared(dv_all)
        d_qkv = jnp.concatenate(
            [
                rotate(dq, self.inside, -1.0).reshape(rows, D),
                rotate(dk, self.inside, -1.0).reshape(rows, D),
                dv.reshape(rows, D),
            ],
            axis=1,
        ).astype(BF16)
        du = jnp.einsum("tc,dc->td", d_qkv, self.gathered(self.w_qkv), preferred_element_type=F32)
        grad_qkv = jnp.einsum("td,tc->dc", self.u, d_qkv, preferred_element_type=F32)
        grad_qkv = weight_share(grad_qkv, self.w_qkv.shape[0])
        return (
            (du,),
            lambda tie: grad_qkv,
            weight_share(grad_out, self.w_out.shape[0]),
            take_rows([send_rows(g) for g in (grad_gate, grad_up)], 1),
        )


def on_device(
    streams,
    cotangent,
    w_qkv,
    w_out,
    w_gate_up,
    w_down,
    hc_weight,
    hc_static,
    seq_lengths,
    pair_perm,
):
    n = lax.axis_size("ctx")
    group = lax.axis_index("fsdp")
    rows = streams.shape[1]
    pair_row = lax.dynamic_index_in_dim(pair_perm, group, 0, keepdims=False)
    length_row = lax.dynamic_index_in_dim(seq_lengths, group, 0, keepdims=False)
    state, cot = streams[0], cotangent[0]
    wpack0, wpack1 = pack_weight(hc_weight[0]), pack_weight(hc_weight[1])
    static = jnp.pad(hc_static, ((0, 0), (0, 0), (0, 2))).reshape(2, 8 * STREAMS)
    static = jnp.pad(static, ((0, 6), (0, LANES - 8 * STREAMS)))

    by_heads = HEADS % n == 0 and n % 2 == 0 and n > 2 and lax.axis_size("fsdp") == 4
    plan = HeadAttention if by_heads else TokenAttention
    attention = plan(rows, w_qkv, w_out, pair_row, length_row)
    order = (n, lax.axis_size("fsdp"))
    own_order = order if by_heads else None
    u, aux0 = row_call(
        functools.partial(first_kernel, own_order),
        rows,
        [(state, True), (wpack0, False), (static, False)],
        [(D, BF16), (LANES, F32)],
    )
    y, sent_gate_up, down_rows = attention.forward(u, w_gate_up, w_down)
    u2, dy2, aux1 = row_call(
        functools.partial(middle_kernel, order),
        rows,
        [(state, True), (cot, True), (y, True), (aux0, True), (wpack1, False), (static, False)],
        [(D, BF16), (D, BF16), (LANES, F32)],
    )
    got = {}

    def early_u2(step, arrived):
        if step == 0:
            got["own"] = take_columns(sent_gate_up)
            arrived, got["own"], got["down"] = lax.optimization_barrier(
                (arrived, got["own"], down_rows)
            )
        return arrived

    u2_blocks = ring_gather(u2, early_u2)
    gate_up_cols, down_rows = gather_groups(got["own"]), got["down"]
    width = FF // n
    u2_all, gate, up, hidden = ffn_enter(u2_blocks, gate_up_cols)

    def early_dy2(step, arrived):
        return after(arrived, gate) if step == 2 else arrived

    dy2_blocks = ring_gather(after(dy2, *u2_blocks[-2:]), early_dy2)
    y2_partial = jnp.dot(hidden, down_rows, preferred_element_type=F32).astype(BF16)
    y2_partial, dy2_blocks = lax.optimization_barrier((y2_partial, dy2_blocks))

    def early_y2(step, arrived):
        if step == 0:
            got["dy2_all"], got["d_gate"], got["d_up"] = ffn_back(
                after(dy2_blocks, arrived), down_rows, gate, up
            )
        if step == 1:
            d_gate, d_up = after([got["d_gate"], got["d_up"]], arrived)
            got["du2"] = ffn_leave(d_gate, d_up, gate_up_cols)
        return arrived

    y2 = ring_scatter(y2_partial, rows, early_y2)
    for name in ("gate", "up", "down"):
        if name == "down":
            left, right = hidden, got["dy2_all"]
        else:
            left, right = u2_all, got["d_" + name]
        left = after(left, got["du2"], *[v for k, v in got.items() if k.startswith("grad_")])
        g = jnp.einsum("td,tg->dg", left, right, preferred_element_type=F32)
        got["grad_" + name] = g.astype(BF16)

    def leave(terms):
        return row_call(
            out_kernel,
            rows,
            [
                (state, True), (cot, True), (y, True), *[(v, True) for v in terms],
                (aux0, True), (aux1, True), (static, False),
            ],
            [(STREAMS * D, BF16), (LANES, F32)],
        )

    def early_du2(step, arrived):
        if step == 1:
            arrived, y2_all = lax.optimization_barrier((arrived, tuple(y2)))
            got["y2"] = y2_all
        if step == 2:
            arrived, got["grad_gate"], got["grad_up"] = lax.optimization_barrier(
                (arrived, got["grad_gate"], got["grad_up"])
            )
            got["out"] = leave(got["y2"])
        if step == 3:
            arrived, got["out"], got["grad_down"] = lax.optimization_barrier(
                (arrived, got["out"], got["grad_down"])
            )
        return arrived

    du2 = ring_scatter(got["du2"], rows, early_du2)
    if "out" not in got:
        got["out"] = leave(y2)
    out, red1 = got["out"]
    grad_gate, grad_up = [scatter_groups(got[k]) for k in ("grad_gate", "grad_up")]
    grad_down = scatter_groups(got["grad_down"]).astype(F32)
    dmid, dy, hc1 = row_call(
        functools.partial(back_kernel, order),
        rows,
        [
            (state, True), (cot, True), (y, True), *[(v, True) for v in du2], (red1, True),
            (aux0, True), (aux1, True), (wpack1, False), (static, False),
        ],
        [(STREAMS * D, F32), (D, BF16)],
        hc=True,
    )
    red0 = row_call(red_kernel, rows, [(state, True), (dmid, True), (y, True)], [(LANES, F32)])[0]
    du, take_grad_qkv, grad_out, grad_gate_up = attention.backward(dy, grad_gate, grad_up)
    du, grad_down = lax.optimization_barrier((du, grad_down))
    grad_state, hc0 = row_call(
        functools.partial(last_kernel, own_order),
        rows,
        [
            (state, True), (dmid, True), *[(v, True) for v in du], (red0, True), (aux0, True),
            (wpack0, False), (static, False),
        ],
        [(STREAMS * D, BF16)],
        hc=True,
    )
    grad_qkv = take_grad_qkv(hc0)
    hc = sum_all(jnp.concatenate([hc0, hc1], axis=0)).reshape(2, 8, D)
    grad_hc_weight = hc[:, 0:6].transpose(0, 2, 1)
    grad_hc_static = hc[:, 6, : 8 * STREAMS].reshape(2, STREAMS, 8)[:, :, 0:6]
    return (
        out[None],
        grad_state[None],
        grad_qkv,
        grad_out,
        grad_gate_up,
        grad_down,
        grad_hc_weight,
        grad_hc_static,
    )


def solution(mesh):
    return jax.shard_map(
        on_device,
        mesh=mesh,
        in_specs=(
            P("fsdp", "ctx", None),
            P("fsdp", "ctx", None),
            P(("ctx", "fsdp"), None),
            P(("ctx", "fsdp"), None),
            P(("ctx", "fsdp"), None),
            P(("ctx", "fsdp"), None),
            P(),
            P(),
            P(),
            P(),
        ),
        out_specs=(
            P("fsdp", "ctx", None),
            P("fsdp", "ctx", None),
            P(("ctx", "fsdp"), None),
            P(("ctx", "fsdp"), None),
            P(("ctx", "fsdp"), None),
            P(("ctx", "fsdp"), None),
            P(),
            P(),
        ),
        check_vma=False,
    )
```

```python
import functools

import jax
import jax.numpy as jnp
from jax import lax
from jax.experimental import pallas as pl
from jax.experimental.pallas import tpu as pltpu
from jax.sharding import PartitionSpec as P

D = 2048
HEADS = 16
HEAD_DIM = 128
FF = 8192
STREAMS = 4
SCALE = HEAD_DIM ** (-0.5)

eps = 1e-05
F32 = jnp.float32
BF16 = jnp.bfloat16
MIB = 1 << 20


def doc_of(position, length_row):
    ends = jnp.cumsum(length_row)
    starts = ends - length_row
    doc = jnp.sum((position[:, None] >= ends[None, :]).astype(jnp.int32), axis=1)
    seq_ids = jnp.arange(length_row.shape[0], dtype=jnp.int32)
    start = jnp.sum(jnp.where(doc[:, None] == seq_ids[None, :], starts[None, :], 0), axis=1)
    return (doc, start)


def places(pair_row, length_row, rows, owners):
    count = pair_row.shape[0]
    half = rows // 2
    ids = jnp.arange(count, dtype=jnp.int32)
    pair = jnp.sum(jnp.where(owners[:, None] == ids[None, :], pair_row[None, :], 0), axis=1)
    block = jnp.stack([pair, 2 * count - 1 - pair], axis=1)
    offset = jnp.arange(half, dtype=jnp.int32)
    position = (block[:, :, None] * half + offset[None, None, :]).reshape(-1)
    doc, start = doc_of(position, length_row)
    return (position, doc, start)


def ring_order(n):
    return list(range(0, n, 2)) + list(range(n - 1, 0, -2)) if n % 2 == 0 else list(range(n))


def ring_perms(n):
    order = ring_order(n)
    ahead = [(order[i], order[(i + 1) % n]) for i in range(n)]
    return (ahead, [(b, a) for a, b in ahead])


def ring_offsets(n):
    offsets = [0]
    for k in range(1, n // 2):
        offsets += [-k, k]
    return offsets + [-(n // 2)]


def ring_owners(n, place):
    order = jnp.array(ring_order(n), dtype=jnp.int32)
    ids = jnp.arange(n, dtype=jnp.int32)
    mine = jnp.sum(jnp.where(order == place, ids, 0))
    at = (mine + jnp.array(ring_offsets(n), dtype=jnp.int32)) % n
    return jnp.sum(jnp.where(at[:, None] == ids[None, :], order[None, :], 0), axis=1)


def ring_gather(block, early=None):
    n = lax.axis_size("ctx")
    ahead, back = ring_perms(n)
    moving = [block, block]
    blocks = [block]
    for step in range(n // 2):
        if 2 * (step + 1) == n:
            half = block.shape[0] // 2
            moving = [moving[0][:half], moving[1][half:]]
        moving = [lax.ppermute(moving[0], "ctx", ahead), lax.ppermute(moving[1], "ctx", back)]
        if early:
            moving = early(step, moving)
        blocks += moving
    return blocks


def add_pair(moving, partial, rows, slots, spans):
    def kernel(one_ref, other_ref, one_own, other_own, one_out, other_out):
        for ref, own, out, (first, last) in (
            (one_ref, one_own, one_out, spans[0]),
            (other_ref, other_own, other_out, spans[1]),
        ):
            if last - first < rows:
                out[...] = own[...]
            here = slice(first, last)
            out[here, :] = (ref[...].astype(F32) + own[here, :].astype(F32)).astype(BF16)

    def whole(shape, at):
        return pl.BlockSpec(shape, lambda i: (at, 0))

    shape = (rows, partial.shape[1])
    return pl.pallas_call(
        kernel,
        grid=(1,),
        in_specs=[whole(v.shape, 0) for v in moving] + [whole(shape, at) for at in slots],
        out_specs=[whole(shape, 0)] * 2,
        out_shape=[jax.ShapeDtypeStruct(shape, BF16)] * 2,
        cost_estimate=cost(moving, [jax.ShapeDtypeStruct(shape, BF16)] * 4),
        compiler_params=room(),
    )(*moving, partial, partial)


def ring_scatter(partial, rows, early=None):
    n = lax.axis_size("ctx")
    ahead, back = ring_perms(n)
    offsets = ring_offsets(n)
    half = n // 2
    mid = rows // 2
    last = offsets.index(-half) * rows
    moving = [partial[last : last + mid], partial[last + mid : last + rows]]
    spans = [(0, mid), (mid, rows)]
    for step in range(half):
        moving = [lax.ppermute(moving[0], "ctx", ahead), lax.ppermute(moving[1], "ctx", back)]
        if early:
            moving = early(step, moving)
        k = half - 1 - step
        if k:
            slots = [offsets.index(k), offsets.index(-k)]
            moving = add_pair(moving, partial, rows, slots, spans)
            spans = [(0, rows), (0, rows)]
    if half == 1:
        moving = [jnp.concatenate(moving, axis=0), jnp.zeros((rows, partial.shape[1]), BF16)]
    return (partial, *moving)


def joined_dot(blocks, weight, nt=False, tile=256, dtype=F32):
    total, depth = sum(v.shape[0] for v in blocks), blocks[0].shape[1]
    columns = weight.shape[0] if nt else weight.shape[1]
    tile = min(tile, columns)
    count = len(blocks)

    def kernel(*refs):
        w_ref, joined, out = refs[count:]

        @pl.when(pl.program_id(0) == 0)
        def _():
            at = 0
            for ref in refs[:count]:
                joined[at : at + ref.shape[0], :] = ref[...]
                at += ref.shape[0]

        dims = (((1,), (1 if nt else 0,)), ((), ()))
        out[...] = lax.dot_general(
            joined[...], w_ref[...], dims, preferred_element_type=F32
        ).astype(dtype)

    once = pl.Buffered(1)
    outs = [
        jax.ShapeDtypeStruct((total, depth), BF16),
        jax.ShapeDtypeStruct((total, columns), dtype),
    ]
    w_spec = (
        pl.BlockSpec((tile, depth), lambda j: (j, 0))
        if nt
        else pl.BlockSpec((depth, tile), lambda j: (0, j))
    )
    return pl.pallas_call(
        kernel,
        grid=(columns // tile,),
        in_specs=[
            pl.BlockSpec(v.shape, lambda j: (0, 0), pipeline_mode=once) for v in blocks
        ]
        + [w_spec],
        out_specs=[
            pl.BlockSpec((total, depth), lambda j: (0, 0), pipeline_mode=once),
            pl.BlockSpec((total, tile), lambda j: (0, j)),
        ],
        out_shape=outs,
        cost_estimate=cost((*blocks, weight), outs, 2 * total * depth * columns),
        compiler_params=room(),
    )(*blocks, weight)


def ffn_specs(blocks, width):
    total, depth = sum(v.shape[0] for v in blocks), blocks[0].shape[1]
    tile = run_of(width, 2)
    once = pl.Buffered(1)
    whole = [pl.BlockSpec(v.shape, lambda j: (0, 0), pipeline_mode=once) for v in blocks]
    joined = pl.BlockSpec((total, depth), lambda j: (0, 0), pipeline_mode=once)
    return (total, depth, tile, whole, joined, lambda c: pl.BlockSpec((total, c), lambda j: (0, j)))


def join_once(refs, joined):
    @pl.when(pl.program_id(0) == 0)
    def _():
        at = 0
        for ref in refs:
            joined[at : at + ref.shape[0], :] = ref[...]
            at += ref.shape[0]


def ffn_enter(blocks, weight):
    width = weight.shape[1] // 2
    total, depth, tile, whole, joined_spec, cut = ffn_specs(blocks, width)
    count = len(blocks)

    def kernel(*refs):
        w_ref, joined, both_ref, hidden_ref = refs[count:]
        join_once(refs[:count], joined)
        both = jnp.dot(joined[...], w_ref[...], preferred_element_type=F32)
        gate, up = both[:, :tile], both[:, tile:]
        both_ref[...] = both
        hidden_ref[...] = (gate * jax.nn.sigmoid(gate) * up).astype(BF16)

    outs = [
        jax.ShapeDtypeStruct((total, depth), BF16),
        jax.ShapeDtypeStruct((total, 2 * width), F32),
        jax.ShapeDtypeStruct((total, width), BF16),
    ]
    return pl.pallas_call(
        kernel,
        grid=(width // tile,),
        in_specs=whole + [pl.BlockSpec((depth, 2 * tile), lambda j: (0, j))],
        out_specs=[joined_spec, cut(2 * tile), cut(tile)],
        out_shape=outs,
        cost_estimate=cost((*blocks, weight), outs, 4 * total * depth * width),
        compiler_params=room(),
    )(*blocks, weight)


def ffn_back(blocks, weight, both):
    width = weight.shape[0]
    total, depth, tile, whole, joined_spec, cut = ffn_specs(blocks, width)
    count = len(blocks)

    def kernel(*refs):
        w_ref, both_ref, joined, grad_ref = refs[count:]
        join_once(refs[:count], joined)
        d_hidden = lax.dot_general(
            joined[...], w_ref[...], (((1,), (1,)), ((), ())), preferred_element_type=F32
        )
        d_hidden = d_hidden.astype(BF16).astype(F32)
        gate, up = both_ref[:, :tile], both_ref[:, tile:]
        open_gate = jax.nn.sigmoid(gate)
        part = d_hidden * open_gate
        grad_ref[:, :tile] = (part * up * (1.0 + gate * (1.0 - open_gate))).astype(BF16)
        grad_ref[:, tile:] = (part * gate).astype(BF16)

    outs = [
        jax.ShapeDtypeStruct((total, depth), BF16),
        jax.ShapeDtypeStruct((total, 2 * width), BF16),
    ]
    return pl.pallas_call(
        kernel,
        grid=(width // tile,),
        in_specs=whole + [pl.BlockSpec((tile, depth), lambda j: (j, 0)), cut(2 * tile)],
        out_specs=[joined_spec, cut(2 * tile)],
        out_shape=outs,
        cost_estimate=cost((*blocks, weight, both), outs, 2 * total * depth * width),
        compiler_params=room(),
    )(*blocks, weight, both)


def after(value, *others):
    return lax.optimization_barrier((value, *others))[0]


def cost(ins, outs, flops=0, exps=0):
    moved = sum(v.size * v.dtype.itemsize for v in (*ins, *outs))
    return pl.CostEstimate(flops=flops, bytes_accessed=moved, transcendentals=exps)


def room():
    return pltpu.CompilerParams(vmem_limit_bytes=60 * MIB)


def place_call(kernel, place, ins, outs, scratch=()):
    vmem = pl.BlockSpec(memory_space=pltpu.VMEM)
    return pl.pallas_call(
        kernel,
        in_specs=[pl.BlockSpec(memory_space=pltpu.SMEM)] + [vmem] * len(ins),
        out_specs=[vmem] * len(outs),
        out_shape=outs,
        scratch_shapes=scratch,
        cost_estimate=cost(ins, outs),
        compiler_params=room(),
    )(place.reshape(1), *ins)


def shifted(place_ref, k, n):
    return lax.rem(place_ref[0] + (k + n), n)


def lanes_at(index, width):
    return pl.ds(pl.multiple_of(index * width, width), width)


def run_of(width, parts):
    return min(256, max(128, width // 4)) if parts == 2 else width


def cut_columns(weight, parts, place, n):
    rows = weight.shape[0]
    width = weight.shape[1] // parts // n
    run = run_of(width, parts)

    def kernel(place_ref, w_ref, *outs):
        for k in range(n):
            dest = shifted(place_ref, k, n)
            for at in range(width // run):
                for p in range(parts):
                    to = (at * parts + p) * run
                    start = pl.multiple_of((p * n + dest) * width + at * run, run)
                    outs[k][:, to : to + run] = w_ref[:, pl.ds(start, run)]

    piece = jax.ShapeDtypeStruct((rows, parts * width), weight.dtype)
    return place_call(kernel, place, [weight], [piece] * n)


def cut_rows(v, place, n):
    rows = v.shape[0] // n

    def kernel(place_ref, v_ref, *outs):
        for k in range(n):
            outs[k][...] = v_ref[lanes_at(shifted(place_ref, k, n), rows), :]

    piece = jax.ShapeDtypeStruct((rows, v.shape[1]), v.dtype)
    return place_call(kernel, place, [v], [piece] * n)


def join_rows(pieces, place, n):
    rows, width = pieces[0].shape

    def kernel(place_ref, *refs):
        for k in range(n):
            refs[n][lanes_at(shifted(place_ref, -k, n), rows), :] = refs[k][...]

    whole = jax.ShapeDtypeStruct((n * rows, width), pieces[0].dtype)
    return place_call(kernel, place, pieces, [whole])[0]


def join_columns(pieces, parts, place, dtype):
    n = len(pieces)
    rows, width = pieces[0].shape[0], pieces[0].shape[1] // parts
    run = run_of(width, parts)

    def kernel(place_ref, *refs):
        for k in range(n):
            source = shifted(place_ref, -k, n)
            for at in range(width // run):
                for p in range(parts):
                    cut = refs[k][:, (at * parts + p) * run : (at * parts + p + 1) * run]
                    start = pl.multiple_of((p * n + source) * width + at * run, run)
                    refs[n][:, pl.ds(start, run)] = cut.astype(dtype)

    whole = jax.ShapeDtypeStruct((rows, parts * n * width), dtype)
    return place_call(kernel, place, pieces, [whole])[0]


def send_one(pieces, k, *ties):
    n = len(pieces)
    return lax.ppermute(after(pieces[k], *ties), "ctx", [(i, (i + k) % n) for i in range(n)])


def send_on(pieces):
    got = [pieces[0]]
    for k in range(1, len(pieces)):
        got.append(send_one(pieces, k, *got[max(k - 4, 0) : max(k - 3, 0)]))
    return got


def send_columns(weight, parts):
    n = lax.axis_size("ctx")
    rows = weight.shape[0]
    width = weight.shape[1] // parts // n
    if n <= 8:
        return send_on(cut_columns(weight, parts, lax.axis_index("ctx"), n))
    cut = weight.reshape(rows, parts, n, -1, run_of(width, parts)).transpose(2, 0, 3, 1, 4)
    return [lax.all_to_all(cut.reshape(n, rows, parts * width), "ctx", 0, 0, tiled=True)]


def take_columns(sent):
    if len(sent) == 1:
        return sent[0].reshape(-1, sent[0].shape[-1])
    return join_rows(sent, lax.axis_index("ctx"), len(sent))


def send_rows(mine):
    n = lax.axis_size("ctx")
    if n <= 8:
        return send_on(cut_rows(mine, lax.axis_index("ctx"), n))
    return [lax.all_to_all(mine.reshape(n, -1, mine.shape[1]), "ctx", 0, 0, tiled=True)]


def take_rows(sent, parts):
    if len(sent) > 1:
        return join_columns(sent, parts, lax.axis_index("ctx"), F32)
    n, rows, columns = sent[0].shape
    got = sent[0].reshape(n, rows, -1, parts, run_of(columns // parts, parts))
    return got.transpose(1, 3, 0, 2, 4).reshape(rows, -1).astype(F32)


def gather_groups(v):
    return lax.all_gather(v, "fsdp", axis=0, tiled=True)


def scatter_groups(v):
    return lax.psum_scatter(v, "fsdp", scatter_dimension=0, tiled=True)


def far(v):
    return lax.ppermute(v, "fsdp", [(i, i ^ 2) for i in range(4)])


def near(v):
    return lax.ppermute(v, "fsdp", [(i, i ^ 1) for i in range(4)])


def in_order(held):
    me = lax.axis_index("fsdp")
    out = jnp.zeros((4,) + held[0].shape, held[0].dtype)
    for k, h in enumerate(held):
        out = lax.dynamic_update_slice_in_dim(out, h[None], me ^ k, 0)
    return out.reshape(4 * held[0].shape[0], held[0].shape[1])


def cut_groups(v):
    me = lax.axis_index("fsdp")
    rows = v.shape[0] // 4
    return [lax.dynamic_slice_in_dim(v, (me ^ k) * rows, rows, 0) for k in range(4)]


def add_low(got, own):
    return (got.astype(F32) + own.astype(F32)).astype(BF16)


def weight_share(gradient, shard_rows):
    partial_rows = lax.psum_scatter(
        gradient.astype(BF16), "ctx", scatter_dimension=0, tiled=True
    )
    return lax.psum_scatter(partial_rows, "fsdp", scatter_dimension=0, tiled=True).astype(F32)


def spread_lanes(v, n, m):
    w = D // (n * m)
    cuts = [v[:, (c * m + f) * w : (c * m + f + 1) * w] for f in range(m) for c in range(n)]
    return jnp.concatenate(cuts, axis=1)


def unspread_lanes(v, n, m):
    return spread_lanes(v, m, n)


def sum_all(v, beside):
    beside, made = list(beside), []
    for axis in ("ctx", "fsdp"):
        n = lax.axis_size(axis)
        if n & (n - 1):
            v = lax.psum(v, axis)
            continue
        step = 1
        while step < n:
            got = lax.ppermute(v, axis, [(i, i ^ step) for i in range(n)])
            if beside:
                got, now = lax.optimization_barrier((got, beside.pop(0)))
                made.append(now)
            v = v + got
            step *= 2
    return (v, made + beside)


LANES = 128
HC_ROWS = 32


def lanes_of(rows):
    return lax.broadcasted_iota(jnp.int32, (rows, LANES), 1)


def put(held, lane, at, column):
    return jnp.where(lane == at, column, held)


def mean_of(v):
    return jnp.sum(v, axis=1, keepdims=True) * (1.0 / D)


def stream_parts(ref):
    return [ref[:, i * D : (i + 1) * D].astype(F32) for i in range(STREAMS)]


def mixed(parts, coef, branch):
    outs = []
    for j in range(STREAMS):
        total = coef[:, 8 * j + 5 : 8 * j + 6] * branch
        for i in range(STREAMS):
            total = total + coef[:, 8 * i + 1 + j : 8 * i + 2 + j] * parts[i]
        outs.append(total)
    return outs


def branch_grad(parts, coef):
    return sum(coef[:, 8 * j + 5 : 8 * j + 6] * parts[j] for j in range(STREAMS))


def layer_in(parts, coef):
    return sum(coef[:, 8 * i : 8 * i + 1] * parts[i] for i in range(STREAMS))


def enter(parts, wpack, static):
    rows = parts[0].shape[0]
    lane = lanes_of(rows)
    aux = jnp.zeros((rows, LANES), F32)
    pieces = ([], [], [])
    for i in range(STREAMS):
        mean = mean_of(parts[i])
        cent = parts[i] - mean
        rstd = lax.rsqrt(mean_of(cent * cent) + eps)
        left = cent * rstd
        for piece in pieces:
            piece.append(left.astype(BF16))
            left = left - piece[-1].astype(F32)
        aux = put(aux, lane, 8 * i + 6, mean)
        aux = put(aux, lane, 8 * i + 7, rstd)
    dims = (((1,), (1,)), ((), ()))
    proj = sum(
        lax.dot_general(jnp.concatenate(p, axis=0), wpack, dims, preferred_element_type=F32)
        for p in pieces[::-1]
    )
    proj = proj + pltpu.roll(proj, LANES - 32, 1) + pltpu.roll(proj, LANES - 64, 1)
    for i in range(STREAMS):
        own = jnp.where(lane < 6, proj[i * rows : (i + 1) * rows], 0.0)
        aux += own if i == 0 else pltpu.roll(own, 8 * i, 1)
    coef = static + jnp.tanh(aux)
    x = layer_in(parts, coef)
    mean = mean_of(x)
    cent = x - mean
    rstd = lax.rsqrt(mean_of(cent * cent) + eps)
    aux = put(aux, lane, 32, mean)
    aux = put(aux, lane, 33, rstd)
    return (aux, coef, cent * rstd)


def leave_grads(parts, grads, branch):
    rows = parts[0].shape[0]
    lane = lanes_of(rows)
    red = jnp.zeros((rows, LANES), F32)
    for j in range(STREAMS):
        red = put(red, lane, 8 * j + 5, jnp.sum(grads[j] * branch, axis=1, keepdims=True))
        for i in range(STREAMS):
            red = put(
                red, lane, 8 * i + 1 + j, jnp.sum(parts[i] * grads[j], axis=1, keepdims=True)
            )
    return red


def enter_back(parts, grads, aux, coef, red, du, wpack, normed_ref, dz_ref, stat_ref, step):
    rows = parts[0].shape[0]
    lane = lanes_of(rows)
    x = layer_in(parts, coef)
    rx = aux[:, 33:34]
    nx = (x - aux[:, 32:33]) * rx
    dx = rx * (du - mean_of(du) - nx * mean_of(du * nx))
    for i in range(STREAMS):
        red = put(red, lane, 8 * i, jnp.sum(parts[i] * dx, axis=1, keepdims=True))
    used = (lane < 8 * STREAMS) & (lane % 8 < 6)
    slope = jnp.tanh(aux)
    dz = jnp.where(used, red * (1.0 - slope * slope), 0.0)
    stat_ref[0:1, :] += jnp.sum(red, axis=0, keepdims=True)
    dz_ref[pl.ds(step * rows, rows), :] = dz
    both = dz * aux
    packed = []
    for i in range(STREAMS):
        own = dz if i == 0 else pltpu.roll(dz, LANES - 8 * i, 1)
        own = jnp.where(lane < 6, own, 0.0)
        top = own.astype(BF16).astype(F32)
        packed.append((top + pltpu.roll(top, 32, 1) + pltpu.roll(own - top, 96, 1)).astype(BF16))
    dn_all = lax.dot_general(
        jnp.concatenate(packed, axis=0), wpack, (((1,), (0,)), ((), ())), preferred_element_type=F32
    )
    outs = []
    total_rows = dz_ref.shape[0]
    for i in range(STREAMS):
        mean, rstd = aux[:, 8 * i + 6 : 8 * i + 7], aux[:, 8 * i + 7 : 8 * i + 8]
        normed = (parts[i] - mean) * rstd
        normed_ref[pl.ds(i * total_rows + step * rows, rows), :] = normed.astype(BF16)
        dn = dn_all[i * rows : (i + 1) * rows]
        own = (lane >= 8 * i) & (lane < 8 * i + 6)
        along = jnp.sum(jnp.where(own, both, 0.0), axis=1, keepdims=True) * (1.0 / D)
        total = coef[:, 8 * i : 8 * i + 1] * dx + rstd * (dn - mean_of(dn) - normed * along)
        for j in range(STREAMS):
            total = total + coef[:, 8 * i + 1 + j : 8 * i + 2 + j] * grads[j]
        outs.append(total)
    return outs


def finish_hc(normed_ref, dz_ref, stat_ref, hc_ref):
    across = dz_ref[...].T
    left = jnp.concatenate([across[8 * i : 8 * i + 8] for i in range(STREAMS)], axis=1)
    top = left.astype(BF16)
    low = (left - top.astype(F32)).astype(BF16)
    both = lax.dot_general(
        jnp.concatenate([top, low], axis=0),
        normed_ref[...],
        (((1,), (0,)), ((), ())),
        preferred_element_type=F32,
    )
    hc_ref[...] = both[0:8] + both[8:16]
    hc_ref[6:7, 0:LANES] = stat_ref[0:1, :]


def sum_of(refs):
    return sum(ref[...].astype(F32) for ref in refs)


def first_kernel(order, s_ref, w_ref, static_ref, u_ref, aux_ref):
    aux, _, u = enter(stream_parts(s_ref), w_ref[...], static_ref[0:1, :])
    u = u.astype(BF16)
    u_ref[...] = spread_lanes(u, *order) if order else u
    aux_ref[...] = aux


def middle_kernel(order, s_ref, c_ref, y_ref, aux0_ref, w_ref, static_ref, u_ref, dy_ref, aux_ref):
    coef0 = static_ref[0:1, :] + jnp.tanh(aux0_ref[...])
    mid = mixed(stream_parts(s_ref), coef0, y_ref[...])
    aux, coef, u = enter(mid, w_ref[...], static_ref[1:2, :])
    u_ref[...] = spread_lanes(u.astype(BF16), *order)
    aux_ref[...] = aux
    dy_ref[...] = branch_grad(stream_parts(c_ref), coef).astype(BF16)


def out_kernel(
    s_ref, y_ref, y2a_ref, y2b_ref, y2c_ref, aux0_ref, aux1_ref, static_ref, out_ref
):
    coef0 = static_ref[0:1, :] + jnp.tanh(aux0_ref[...])
    coef1 = static_ref[1:2, :] + jnp.tanh(aux1_ref[...])
    mid = mixed(stream_parts(s_ref), coef0, y_ref[...])
    y2 = sum_of((y2a_ref, y2b_ref, y2c_ref))
    for j, total in enumerate(mixed(mid, coef1, y2)):
        out_ref[:, j * D : (j + 1) * D] = total.astype(BF16)


def back_kernel(
    order, s_ref, c_ref, y_ref, y2a_ref, y2b_ref, y2c_ref, dua_ref, dub_ref, duc_ref, aux0_ref,
    aux1_ref, w_ref, static_ref, dmid_ref, dy_ref, hc_ref, normed_ref, dz_ref, stat_ref,
):
    step = pl.program_id(0)

    @pl.when(step == 0)
    def _():
        stat_ref[...] = jnp.zeros_like(stat_ref)

    coef0 = static_ref[0:1, :] + jnp.tanh(aux0_ref[...])
    aux1 = aux1_ref[...]
    coef1 = static_ref[1:2, :] + jnp.tanh(aux1)
    mid = mixed(stream_parts(s_ref), coef0, y_ref[...])
    du = unspread_lanes(sum_of((dua_ref, dub_ref, duc_ref)), *order)
    grads = stream_parts(c_ref)
    red = leave_grads(mid, grads, sum_of((y2a_ref, y2b_ref, y2c_ref)))
    dmid = enter_back(
        mid, grads, aux1, coef1, red, du, w_ref[...],
        normed_ref, dz_ref, stat_ref, step,
    )
    for j in range(STREAMS):
        dmid_ref[:, j * D : (j + 1) * D] = dmid[j]
    dy_ref[...] = branch_grad(dmid, coef0).astype(BF16)

    @pl.when(step == pl.num_programs(0) - 1)
    def _():
        finish_hc(normed_ref, dz_ref, stat_ref, hc_ref)


def red_kernel(s_ref, dmid_ref, y_ref, red_ref):
    red_ref[...] = leave_grads(stream_parts(s_ref), stream_parts(dmid_ref), y_ref[...])


def last_kernel(
    order, s_ref, dmid_ref, *refs
):
    du_refs = refs[:-9]
    red_ref, aux0_ref, w_ref, static_ref, ds_ref, hc_ref, normed_ref, dz_ref, stat_ref = refs[-9:]
    step = pl.program_id(0)

    @pl.when(step == 0)
    def _():
        stat_ref[...] = jnp.zeros_like(stat_ref)

    aux0 = aux0_ref[...]
    coef0 = static_ref[0:1, :] + jnp.tanh(aux0)
    parts, grads = stream_parts(s_ref), stream_parts(dmid_ref)
    du = sum_of(du_refs)
    if order:
        du = unspread_lanes(du, *order)
    ds = enter_back(
        parts, grads, aux0, coef0, red_ref[...], du, w_ref[...],
        normed_ref, dz_ref, stat_ref, step,
    )
    for j in range(STREAMS):
        ds_ref[:, j * D : (j + 1) * D] = ds[j].astype(BF16)

    @pl.when(step == pl.num_programs(0) - 1)
    def _():
        finish_hc(normed_ref, dz_ref, stat_ref, hc_ref)


def row_call(kernel, rows, ins, outs, hc=False):
    tile = HC_ROWS if hc else min(rows, 2 * HC_ROWS)

    def cut(columns):
        return pl.BlockSpec((tile, columns), lambda i: (i, 0))

    def whole(shape):
        return pl.BlockSpec(shape, lambda i: (0, 0))

    in_specs = [cut(a.shape[1]) if by_rows else whole(a.shape) for a, by_rows in ins]
    out_specs = [cut(columns) for columns, _ in outs]
    out_shape = [jax.ShapeDtypeStruct((rows, columns), dtype) for columns, dtype in outs]
    scratch = []
    if hc:
        out_specs.append(whole((8, D)))
        out_shape.append(jax.ShapeDtypeStruct((8, D), F32))
        scratch = [
            pltpu.VMEM((STREAMS * rows, D), BF16),
            pltpu.VMEM((rows, LANES), F32),
            pltpu.VMEM((8, LANES), F32),
        ]
    return pl.pallas_call(
        kernel,
        grid=(rows // tile,),
        in_specs=in_specs,
        out_specs=out_specs,
        out_shape=out_shape,
        scratch_shapes=scratch,
        cost_estimate=cost([a for a, _ in ins], out_shape, 100 * rows * STREAMS * D),
        compiler_params=room(),
    )(*[a for a, _ in ins])


def pack_weight(weight):
    across = jnp.pad(weight.T, ((0, 26), (0, 0)))
    top = lax.reduce_precision(across, 8, 7)
    mid = lax.reduce_precision(across - top, 8, 7)
    return jnp.concatenate([top, mid, across - top - mid, top], axis=0).astype(BF16)


Q_ROWS = 512


def turn(v, cosine, sine):
    return v * cosine + pltpu.roll(v, HEAD_DIM // 2, 1) * sine


def attend_kernel(
    q_ref, k_ref, v_ref, cos_ref, sin_ref, qpos_ref, qstart_ref, kpos_ref,
    o_ref, lse_ref, qr_ref, kr_ref, vb_ref,
):
    at = pl.program_id(1)

    @pl.when(at == 0)
    def _():
        kr_ref[...] = turn(k_ref[...], cos_ref[...], sin_ref[...]).astype(BF16)
        vb_ref[...] = v_ref[...].astype(BF16)

    here = pl.ds(at * Q_ROWS, Q_ROWS)
    query = turn(q_ref[...], cos_ref[here, :], sin_ref[here, :]).astype(BF16)
    qr_ref[...] = query
    scores = (
        lax.dot_general(query, kr_ref[...], (((1,), (1,)), ((), ())), preferred_element_type=F32)
        * SCALE
    )
    kpos = kpos_ref[0:1, :]
    keep = (kpos <= qpos_ref[...]) & (kpos >= qstart_ref[...])
    scores = jnp.where(keep, scores, -1e30)
    top = jnp.max(scores, axis=1, keepdims=True)
    grown = jnp.exp(scores - top)
    total = jnp.sum(grown, axis=1, keepdims=True)
    out = jnp.dot((grown / total).astype(BF16), vb_ref[...], preferred_element_type=F32)
    o_ref[...] = out.astype(BF16)
    lse_ref[...] = jnp.broadcast_to(top + jnp.log(total), lse_ref.shape)


def attend_back_kernel(
    q_ref, k_ref, v_ref, do_ref, lse_ref, cos_ref, sin_ref, qpos_ref, qstart_ref, kpos_ref,
    dq_ref, dk_ref, dv_ref, dk_sum, dv_sum,
):
    at = pl.program_id(1)

    @pl.when(at == 0)
    def _():
        dk_sum[...] = jnp.zeros_like(dk_sum)
        dv_sum[...] = jnp.zeros_like(dv_sum)

    here = pl.ds(at * Q_ROWS, Q_ROWS)
    query, keys, d_out = q_ref[...], k_ref[...], do_ref[...]
    nt = (((1,), (1,)), ((), ()))
    tn = (((0,), (0,)), ((), ()))
    scores = lax.dot_general(query, keys, nt, preferred_element_type=F32) * SCALE
    kpos = kpos_ref[0:1, :]
    keep = (kpos <= qpos_ref[...]) & (kpos >= qstart_ref[...])
    probs = jnp.where(keep, jnp.exp(scores - lse_ref[:, 0:1]), 0.0)
    d_probs = lax.dot_general(d_out, v_ref[...], nt, preferred_element_type=F32)
    delta = jnp.sum(probs * d_probs, axis=1, keepdims=True)
    ds = (probs * (d_probs - delta)).astype(BF16)
    dq = jnp.dot(ds, keys, preferred_element_type=F32) * SCALE
    dq_ref[...] = turn(dq, cos_ref[here, :], -sin_ref[here, :]).astype(BF16)
    dk_sum[...] += lax.dot_general(ds, query, tn, preferred_element_type=F32)
    dv_sum[...] += lax.dot_general(probs.astype(BF16), d_out, tn, preferred_element_type=F32)

    @pl.when(at == pl.num_programs(1) - 1)
    def _():
        dk_ref[...] = turn(dk_sum[...] * SCALE, cos_ref[...], -sin_ref[...]).astype(BF16)
        dv_ref[...] = dv_sum[...].astype(BF16)


def attention_specs(total):
    by_query = pl.BlockSpec((Q_ROWS, HEAD_DIM), lambda h, i: (i, h))
    by_head = pl.BlockSpec((total, HEAD_DIM), lambda h, i: (0, h))
    table = pl.BlockSpec((total, HEAD_DIM), lambda h, i: (0, 0))
    row = pl.BlockSpec((Q_ROWS, 1), lambda h, i: (i, 0))
    keys = pl.BlockSpec((8, total), lambda h, i: (0, 0))
    return (by_query, by_head, [table, table, row, row, keys])


def attend(qkv, heads, marks):
    total = qkv.shape[0]
    by_query, by_head, shared = attention_specs(total)

    def of(kind):
        return pl.BlockSpec((total, HEAD_DIM), lambda h, i: (0, kind * heads + h))

    low = jax.ShapeDtypeStruct((total, heads * HEAD_DIM), BF16)
    wide = jax.ShapeDtypeStruct((total, heads * HEAD_DIM), F32)
    return pl.pallas_call(
        attend_kernel,
        grid=(heads, total // Q_ROWS),
        in_specs=[by_query, of(1), of(2)] + shared,
        out_specs=[by_query, by_query, by_query, by_head, by_head],
        out_shape=[low, wide, low, low, low],
        cost_estimate=cost([qkv], [low] * 4, 4 * heads * total**2 * HEAD_DIM, heads * total**2),
        compiler_params=room(),
    )(qkv, qkv, qkv, *marks)


def attend_back(query, keys, values, d_out, lse, heads, marks):
    total = query.shape[0]
    by_query, by_head, shared = attention_specs(total)
    low = jax.ShapeDtypeStruct((total, heads * HEAD_DIM), BF16)
    return pl.pallas_call(
        attend_back_kernel,
        grid=(heads, total // Q_ROWS),
        in_specs=[by_query, by_head, by_head, by_query, by_query] + shared,
        out_specs=[by_query, by_head, by_head],
        out_shape=[low, low, low],
        scratch_shapes=[pltpu.VMEM((total, HEAD_DIM), F32)] * 2,
        cost_estimate=cost([lse], [low] * 7, 10 * heads * total**2 * HEAD_DIM, heads * total**2),
        compiler_params=room(),
    )(query, keys, values, d_out, lse, *marks)


def angles(inside):
    half = HEAD_DIM // 2
    freq = 10000.0 ** (-jnp.arange(half, dtype=F32) / half)
    angle = inside.astype(F32)[:, None] * freq[None, :]
    cosine, sine = jnp.cos(angle), jnp.sin(angle)
    return (jnp.concatenate([cosine, cosine], axis=1), jnp.concatenate([-sine, sine], axis=1))


class HeadAttention:
    def __init__(self, rows, w_qkv, w_out, pair_row, length_row):
        n = lax.axis_size("ctx")
        self.group = lax.axis_index("fsdp")
        self.rows, self.heads = rows, HEADS // n
        owners = ring_owners(n, lax.axis_index("ctx"))
        position, _, start = places(pair_row, length_row, rows, owners)
        cosine, sine = angles(position - start)
        kpos = jnp.broadcast_to(position[None, :], (8, position.shape[0]))
        self.marks = (cosine, sine, position[:, None], start[:, None], kpos)
        self.cut_qkv = cut_columns(w_qkv, 3, lax.axis_index("ctx"), n)
        self.w_out = w_out

    def to_tokens(self, heads_out):
        n = lax.axis_size("ctx")
        order, offsets = ring_order(n), ring_offsets(n)
        got = []
        for offset in offsets:
            at = offsets.index(-offset if 2 * offset != -n else offset)
            own = heads_out[at * self.rows : (at + 1) * self.rows]
            pairs = [(order[i], order[(i - offset) % n]) for i in range(n)]
            got.append(lax.ppermute(own, "ctx", pairs) if offset else own)
        return got

    def join_tokens(self, got):
        n, m = lax.axis_size("ctx"), lax.axis_size("fsdp")
        offsets, width = ring_offsets(n), got[0].shape[1]

        def kernel(place_ref, *refs):
            place = place_ref[0]
            mine = jnp.where(place % 2 == 0, place // 2, n - 1 - place // 2)
            held = refs[-1]
            for k, offset in enumerate(offsets):
                at = lax.rem(mine + offset + n, n)
                owner = jnp.where(at < n // 2, 2 * at, 2 * (n - 1 - at) + 1)
                held[:, lanes_at(owner, width)] = refs[k][...]
            refs[n][...] = spread_lanes(held[...], n, m)

        whole = jax.ShapeDtypeStruct((self.rows, n * width), got[0].dtype)
        scratch = [pltpu.VMEM(whole.shape, whole.dtype)]
        return place_call(kernel, lax.axis_index("ctx"), got, [whole], scratch)[0]

    def forward(self, u, w_gate_up, w_down):
        n, m = lax.axis_size("ctx"), lax.axis_size("fsdp")
        got = {}

        place = lax.axis_index("ctx")
        out_ctx = lax.all_gather(self.w_out, "ctx", axis=0, tiled=True)
        cut = self.cut_qkv
        sent_qkv = [cut[0], *[send_one(cut, k) for k in (1, 2)]]
        sent_qkv += [send_one(cut, k, u) for k in range(3, n)]

        def early(step, arrived):
            if step == 1:
                arrived, sent, self.marks = lax.optimization_barrier(
                    (arrived, sent_qkv, self.marks)
                )
                got["own"] = take_columns(sent)
                got["far"] = far(got["own"])
                got["cut"] = cut_columns(after(w_gate_up, got["own"]), 2, place, n)
            if step == 2:
                arrived, got["far"], got["out"], got["cut"] = lax.optimization_barrier(
                    (arrived, got["far"], out_ctx, got["cut"])
                )
                got["near"] = [near(got["own"]), near(got["far"])]
            return arrived

        blocks = ring_gather(u, early)
        blocks, got["near"] = lax.optimization_barrier((blocks, got["near"]))
        self.qkv_cols = in_order([got["own"], got["near"][0], got["far"], got["near"][1]])
        out_all = lax.all_gather(got["out"], "fsdp", axis=0, tiled=True)
        down_rows = gather_groups(after(w_down, *blocks))
        cut, blocks = lax.optimization_barrier((got["cut"], blocks))
        first = [send_one(cut, k) for k in (1, 2)]
        self.u_all, qkv = joined_dot(blocks, self.qkv_cols)
        qkv, first = lax.optimization_barrier((qkv, first))
        second = [send_one(cut, k, qkv) for k in (3, 4)]
        self.o, self.lse, self.q, self.k, self.v = attend(qkv, self.heads, self.marks)
        o, second = lax.optimization_barrier((self.o, second))
        sent_o = self.to_tokens(o)
        sent = [cut[0], *first, *second, *[send_one(cut, k, o) for k in range(5, n)]]
        held = out_all.reshape(m, n, -1, D)
        held = lax.dynamic_slice_in_dim(held, lax.axis_index("ctx"), 1, 1)
        self.out_rows = held.reshape(-1, D)
        y = jnp.dot(self.join_tokens(sent_o), out_all, preferred_element_type=F32)
        y, *sent[:5] = lax.optimization_barrier((y, *sent[:5]))
        return (y, sent, down_rows)

    def backward(self, dy, dy_blocks, grad_gate_up, grad_down):
        got = {}

        dy_all, d_out = joined_dot(dy_blocks, self.out_rows, nt=True, dtype=BF16)
        n, place = lax.axis_size("ctx"), lax.axis_index("ctx")
        cut = cut_rows(after(grad_gate_up, dy_all), place, n)
        first = [send_one(cut, k) for k in range(1, 4)]
        dq, dk, dv = attend_back(self.q, self.k, self.v, d_out, self.lse, self.heads, self.marks)
        dq, first = lax.optimization_barrier((dq, first))
        second = [send_one(cut, k, dq) for k in range(4, n)]
        d_qkv = jnp.concatenate([dq, dk, dv], axis=1)
        partial = jnp.einsum(
            "tc,dc->td", d_qkv, self.qkv_cols, preferred_element_type=F32
        ).astype(BF16)

        def early(step, arrived):
            if step == 0:
                u_all = after(self.u_all, partial)
                g = jnp.einsum("td,tc->dc", u_all, d_qkv, preferred_element_type=F32)
                got["qkv"] = scatter_groups(g.astype(BF16))
            if step == 1:
                arrived, got["second"] = lax.optimization_barrier((arrived, second))
                o, dy_now = after([self.o, dy_all], arrived)
                g = jnp.einsum("te,td->ed", o, dy_now, preferred_element_type=F32)
                got["out"] = g.astype(BF16)
            if step == 2:
                arrived, got["out"], got["down"] = lax.optimization_barrier(
                    (arrived, got["out"], grad_down)
                )
            return arrived

        du = ring_scatter(partial, self.rows, early)
        sent_qkv = send_rows(got["qkv"])
        du, sent_qkv = lax.optimization_barrier((du, sent_qkv))
        return (
            du,
            lambda tie: take_rows(after(sent_qkv, tie), 3),
            scatter_groups(got["out"]).astype(F32),
            take_rows([cut[0], *first, *got["second"]], 2),
            got["down"].astype(F32),
        )


def rotate(v, inside, sign):
    half = v.shape[-1] // 2
    freq = 10000.0 ** (-jnp.arange(half, dtype=F32) / half)
    angle = inside.astype(F32)[:, None] * freq[None, :]
    cosine = jnp.cos(angle)[:, None, :]
    sine = sign * jnp.sin(angle)[:, None, :]
    first, second = (v[..., :half], v[..., half:])
    return jnp.concatenate(
        [first * cosine - second * sine, second * cosine + first * sine], axis=-1
    )


class TokenAttention:
    def __init__(self, rows, w_qkv, w_out, pair_row, length_row):
        n = lax.axis_size("ctx")
        place = lax.axis_index("ctx")
        self.rows = rows
        owners = jnp.arange(n, dtype=jnp.int32)
        kpos, kdoc, kstart = places(pair_row, length_row, rows, owners)

        def own(v):
            return lax.dynamic_slice_in_dim(v, place * rows, rows)

        self.inside = own(kpos - kstart)
        self.keep = (kpos[None, :] <= own(kpos)[:, None]) & (kdoc[None, :] == own(kdoc)[:, None])
        self.w_qkv, self.w_out = w_qkv, w_out

    def gathered(self, weight):
        return lax.all_gather(weight, ("ctx", "fsdp"), axis=0, tiled=True)

    def scores(self):
        scores = jnp.einsum("qhe,hke->hqk", self.q, self.k, preferred_element_type=F32) * SCALE
        return jnp.where(self.keep[None], scores, -1e30)

    def forward(self, u, w_gate_up, w_down):
        rows, shape = self.rows, (self.rows, HEADS, HEAD_DIM)
        self.u = u
        qkv = jnp.dot(u, self.gathered(self.w_qkv), preferred_element_type=F32)
        self.q = rotate(qkv[:, :D].reshape(shape), self.inside, 1.0).astype(BF16)
        key = rotate(qkv[:, D : 2 * D].reshape(shape), self.inside, 1.0).astype(BF16)
        value = qkv[:, 2 * D :].reshape(shape).astype(BF16)
        self.k = lax.all_gather(key.transpose(1, 0, 2), "ctx", axis=1, tiled=True)
        self.v = lax.all_gather(value.transpose(1, 0, 2), "ctx", axis=1, tiled=True)
        scores = self.scores()
        top = jnp.max(scores, axis=-1, keepdims=True)
        self.lse = top + jnp.log(jnp.sum(jnp.exp(scores - top), axis=-1, keepdims=True))
        probs = jnp.exp(scores - self.lse).astype(BF16)
        attended = jnp.einsum("hqk,hke->qhe", probs, self.v, preferred_element_type=F32)
        self.o = attended.reshape(rows, D).astype(BF16)
        y = jnp.dot(self.o, self.gathered(self.w_out), preferred_element_type=F32)
        return (y, send_columns(w_gate_up, 2), gather_groups(w_down))

    def backward(self, dy, dy_blocks, grad_gate_up, grad_down):
        rows = self.rows
        d_out = jnp.einsum(
            "td,ed->te", dy, self.gathered(self.w_out), preferred_element_type=F32
        )
        d_out = d_out.astype(BF16).reshape(rows, HEADS, HEAD_DIM)
        grad_out = jnp.einsum("te,td->ed", self.o, dy, preferred_element_type=F32)
        again = jnp.exp(self.scores() - self.lse)
        d_probs = jnp.einsum("qhe,hke->hqk", d_out, self.v, preferred_element_type=F32)
        delta = jnp.sum(again * d_probs, axis=-1, keepdims=True)
        ds = (again * (d_probs - delta)).astype(BF16)
        dq = jnp.einsum("hqk,hke->qhe", ds, self.k, preferred_element_type=F32) * SCALE
        dk_all = jnp.einsum("hqk,qhe->hke", ds, self.q, preferred_element_type=F32) * SCALE
        dv_all = jnp.einsum(
            "hqk,qhe->hke", again.astype(BF16), d_out, preferred_element_type=F32
        )

        def shared(v):
            mine = lax.psum_scatter(v.astype(BF16), "ctx", scatter_dimension=1, tiled=True)
            return mine.astype(F32).transpose(1, 0, 2)

        dk, dv = shared(dk_all), shared(dv_all)
        d_qkv = jnp.concatenate(
            [
                rotate(dq, self.inside, -1.0).reshape(rows, D),
                rotate(dk, self.inside, -1.0).reshape(rows, D),
                dv.reshape(rows, D),
            ],
            axis=1,
        ).astype(BF16)
        du = jnp.einsum("tc,dc->td", d_qkv, self.gathered(self.w_qkv), preferred_element_type=F32)
        grad_qkv = jnp.einsum("td,tc->dc", self.u, d_qkv, preferred_element_type=F32)
        grad_qkv = weight_share(grad_qkv, self.w_qkv.shape[0])
        return (
            (du,),
            lambda tie: grad_qkv,
            weight_share(grad_out, self.w_out.shape[0]),
            take_rows(send_rows(grad_gate_up), 2),
            grad_down.astype(F32),
        )


def on_device(
    streams,
    cotangent,
    w_qkv,
    w_out,
    w_gate_up,
    w_down,
    hc_weight,
    hc_static,
    seq_lengths,
    pair_perm,
):
    n = lax.axis_size("ctx")
    group = lax.axis_index("fsdp")
    rows = streams.shape[1]
    pair_row = lax.dynamic_index_in_dim(pair_perm, group, 0, keepdims=False)
    length_row = lax.dynamic_index_in_dim(seq_lengths, group, 0, keepdims=False)
    state, cot = streams[0], cotangent[0]
    wpack0, wpack1 = pack_weight(hc_weight[0]), pack_weight(hc_weight[1])
    static = jnp.pad(hc_static, ((0, 0), (0, 0), (0, 2))).reshape(2, 8 * STREAMS)
    static = jnp.pad(static, ((0, 6), (0, LANES - 8 * STREAMS)))

    by_heads = HEADS % n == 0 and n % 2 == 0 and n > 2 and lax.axis_size("fsdp") == 4
    plan = HeadAttention if by_heads else TokenAttention
    attention = plan(rows, w_qkv, w_out, pair_row, length_row)
    order = (n, lax.axis_size("fsdp"))
    own_order = order if by_heads else None
    u, aux0 = row_call(
        functools.partial(first_kernel, own_order),
        rows,
        [(state, True), (wpack0, False), (static, False)],
        [(D, BF16), (LANES, F32)],
    )
    y, sent_gate_up, down_rows = attention.forward(u, w_gate_up, w_down)
    u2, dy2, aux1 = row_call(
        functools.partial(middle_kernel, order),
        rows,
        [(state, True), (cot, True), (y, True), (aux0, True), (wpack1, False), (static, False)],
        [(D, BF16), (D, BF16), (LANES, F32)],
    )
    got = {}

    def early_u2(step, arrived):
        if step == 0:
            got["own"] = take_columns(sent)
            arrived, got["own"], got["down"] = lax.optimization_barrier(
                (arrived, got["own"], down_rows)
            )
        return arrived

    u2, sent = lax.optimization_barrier((u2, sent_gate_up))
    u2_blocks = ring_gather(u2, early_u2)
    gate_up_cols, down_rows = gather_groups(got["own"]), got["down"]
    width = FF // n
    u2_all, both, hidden = ffn_enter(u2_blocks, gate_up_cols)

    def early_dy2(step, arrived):
        return after(arrived, both) if step == 2 else arrived

    dy2_blocks = ring_gather(after(dy2, *u2_blocks[-2:]), early_dy2)
    y2_partial = jnp.dot(hidden, down_rows, preferred_element_type=F32).astype(BF16)
    y2_partial, dy2_blocks = lax.optimization_barrier((y2_partial, dy2_blocks))

    def early_y2(step, arrived):
        if step == 0:
            got["dy2_all"], got["dgu"] = ffn_back(after(dy2_blocks, arrived), down_rows, both)
        if step == 1:
            dgu = after(got["dgu"], arrived)
            got["du2"] = jnp.einsum(
                "tg,dg->td", dgu, gate_up_cols, preferred_element_type=F32
            ).astype(BF16)
        return arrived

    y2 = ring_scatter(y2_partial, rows, early_y2)

    def early_du2(step, arrived):
        if step == 0:
            left = after(u2_all, got["du2"])
            g = jnp.einsum("td,tg->dg", left, got["dgu"], preferred_element_type=F32)
            got["gate_up"] = g.astype(BF16)
        if step == 1:
            arrived, got["y2"] = lax.optimization_barrier((arrived, tuple(y2)))
        if step == 2:
            arrived, got["gate_up"] = lax.optimization_barrier((arrived, got["gate_up"]))
        return arrived

    du2 = ring_scatter(got["du2"], rows, early_du2)
    y2 = got["y2"] if "y2" in got else y2
    grad_gate_up = scatter_groups(got["gate_up"])
    dmid, dy, hc1 = row_call(
        functools.partial(back_kernel, order),
        rows,
        [
            (state, True), (cot, True), (y, True), *[(v, True) for v in y2],
            *[(v, True) for v in du2], (aux0, True), (aux1, True), (wpack1, False),
            (static, False),
        ],
        [(STREAMS * D, F32), (D, BF16)],
        hc=True,
    )
    left = after(hidden, dy)
    g = jnp.einsum("tf,td->fd", left, got["dy2_all"], preferred_element_type=F32).astype(BF16)
    terms = after(list(y2), g)
    out = row_call(
        out_kernel,
        rows,
        [
            (state, True), (y, True), *[(v, True) for v in terms], (aux0, True), (aux1, True),
            (static, False),
        ],
        [(STREAMS * D, BF16)],
    )[0]
    red0 = row_call(
        red_kernel, rows, [(after(state, out), True), (dmid, True), (y, True)], [(LANES, F32)]
    )[0]
    held = {}

    def early_dy(step, arrived):
        if step == 1:
            arrived, held["down"] = lax.optimization_barrier((arrived, g))
        if step == 2:
            arrived, held["out"] = lax.optimization_barrier((arrived, out))
        if step == 3:
            arrived, held["gate_up"], held["red0"] = lax.optimization_barrier(
                (arrived, grad_gate_up, red0)
            )
        return arrived

    dy_blocks = ring_gather(dy, early_dy)
    out, red0 = held.get("out", out), held.get("red0", red0)
    grad_gate_up = held.get("gate_up", grad_gate_up)
    grad_down = scatter_groups(held.get("down", g))
    du, take_grad_qkv, grad_out, grad_gate_up, grad_down = attention.backward(
        dy, dy_blocks, grad_gate_up, grad_down
    )
    grad_state, hc0 = row_call(
        functools.partial(last_kernel, own_order),
        rows,
        [
            (state, True), (dmid, True), *[(v, True) for v in du], (red0, True), (aux0, True),
            (wpack0, False), (static, False),
        ],
        [(STREAMS * D, BF16)],
        hc=True,
    )
    hc, beside = sum_all(
        jnp.concatenate([hc0, hc1], axis=0),
        (grad_down, grad_gate_up, take_grad_qkv(hc0), grad_out),
    )
    grad_down, grad_gate_up, grad_qkv, grad_out = beside
    hc = hc.reshape(2, 8, D)
    grad_hc_weight = hc[:, 0:6].transpose(0, 2, 1)
    grad_hc_static = hc[:, 6, : 8 * STREAMS].reshape(2, STREAMS, 8)[:, :, 0:6]
    return (
        out[None],
        grad_state[None],
        grad_qkv,
        grad_out,
        grad_gate_up,
        grad_down,
        grad_hc_weight,
        grad_hc_static,
    )


def solution(mesh):
    return jax.shard_map(
        on_device,
        mesh=mesh,
        in_specs=(
            P("fsdp", "ctx", None),
            P("fsdp", "ctx", None),
            P(("ctx", "fsdp"), None),
            P(("ctx", "fsdp"), None),
            P(("ctx", "fsdp"), None),
            P(("ctx", "fsdp"), None),
            P(),
            P(),
            P(),
            P(),
        ),
        out_specs=(
            P("fsdp", "ctx", None),
            P("fsdp", "ctx", None),
            P(("ctx", "fsdp"), None),
            P(("ctx", "fsdp"), None),
            P(("ctx", "fsdp"), None),
            P(("ctx", "fsdp"), None),
            P(),
            P(),
        ),
        check_vma=False,
    )
```

```python
import functools

import jax
import jax.numpy as jnp
from jax import lax
from jax.experimental import pallas as pl
from jax.experimental.pallas import tpu as pltpu
from jax.sharding import PartitionSpec as P

D = 2048
HEADS = 16
HEAD_DIM = 128
FF = 8192
STREAMS = 4
SCALE = HEAD_DIM ** (-0.5)

eps = 1e-05
F32 = jnp.float32
BF16 = jnp.bfloat16
MIB = 1 << 20


def doc_of(position, length_row):
    ends = jnp.cumsum(length_row)
    starts = ends - length_row
    doc = jnp.sum((position[:, None] >= ends[None, :]).astype(jnp.int32), axis=1)
    seq_ids = jnp.arange(length_row.shape[0], dtype=jnp.int32)
    start = jnp.sum(jnp.where(doc[:, None] == seq_ids[None, :], starts[None, :], 0), axis=1)
    return (doc, start)


def places(pair_row, length_row, rows, owners):
    count = pair_row.shape[0]
    half = rows // 2
    ids = jnp.arange(count, dtype=jnp.int32)
    pair = jnp.sum(jnp.where(owners[:, None] == ids[None, :], pair_row[None, :], 0), axis=1)
    block = jnp.stack([pair, 2 * count - 1 - pair], axis=1)
    offset = jnp.arange(half, dtype=jnp.int32)
    position = (block[:, :, None] * half + offset[None, None, :]).reshape(-1)
    doc, start = doc_of(position, length_row)
    return (position, doc, start)


def ring_order(n):
    return list(range(0, n, 2)) + list(range(n - 1, 0, -2)) if n % 2 == 0 else list(range(n))


def ring_perms(n):
    order = ring_order(n)
    ahead = [(order[i], order[(i + 1) % n]) for i in range(n)]
    return (ahead, [(b, a) for a, b in ahead])


def ring_offsets(n):
    offsets = [0]
    for k in range(1, n // 2):
        offsets += [-k, k]
    return offsets + [-(n // 2)]


def ring_owners(n, place):
    order = jnp.array(ring_order(n), dtype=jnp.int32)
    ids = jnp.arange(n, dtype=jnp.int32)
    mine = jnp.sum(jnp.where(order == place, ids, 0))
    at = (mine + jnp.array(ring_offsets(n), dtype=jnp.int32)) % n
    return jnp.sum(jnp.where(at[:, None] == ids[None, :], order[None, :], 0), axis=1)


def ring_gather(block, early=None):
    n = lax.axis_size("ctx")
    ahead, back = ring_perms(n)
    moving = [block, block]
    blocks = [block]
    for step in range(n // 2):
        if 2 * (step + 1) == n:
            half = block.shape[0] // 2
            moving = [moving[0][:half], moving[1][half:]]
        moving = [lax.ppermute(moving[0], "ctx", ahead), lax.ppermute(moving[1], "ctx", back)]
        if early:
            moving = early(step, moving)
        blocks += moving
    return blocks


def add_pair(moving, partial, rows, slots, spans):
    def kernel(one_ref, other_ref, one_own, other_own, one_out, other_out):
        for ref, own, out, (first, last) in (
            (one_ref, one_own, one_out, spans[0]),
            (other_ref, other_own, other_out, spans[1]),
        ):
            if last - first < rows:
                out[...] = own[...]
            here = slice(first, last)
            out[here, :] = (ref[...].astype(F32) + own[here, :].astype(F32)).astype(BF16)

    def whole(shape, at):
        return pl.BlockSpec(shape, lambda i: (at, 0))

    shape = (rows, partial.shape[1])
    return pl.pallas_call(
        kernel,
        grid=(1,),
        in_specs=[whole(v.shape, 0) for v in moving] + [whole(shape, at) for at in slots],
        out_specs=[whole(shape, 0)] * 2,
        out_shape=[jax.ShapeDtypeStruct(shape, BF16)] * 2,
        cost_estimate=cost(moving, [jax.ShapeDtypeStruct(shape, BF16)] * 4),
        compiler_params=room(),
    )(*moving, partial, partial)


def ring_scatter(partial, rows, early=None):
    n = lax.axis_size("ctx")
    ahead, back = ring_perms(n)
    offsets = ring_offsets(n)
    half = n // 2
    mid = rows // 2
    last = offsets.index(-half) * rows
    moving = [partial[last : last + mid], partial[last + mid : last + rows]]
    spans = [(0, mid), (mid, rows)]
    for step in range(half):
        moving = [lax.ppermute(moving[0], "ctx", ahead), lax.ppermute(moving[1], "ctx", back)]
        if early:
            moving = early(step, moving)
        k = half - 1 - step
        if k:
            slots = [offsets.index(k), offsets.index(-k)]
            moving = add_pair(moving, partial, rows, slots, spans)
            spans = [(0, rows), (0, rows)]
    if half == 1:
        moving = [jnp.concatenate(moving, axis=0), jnp.zeros((rows, partial.shape[1]), BF16)]
    return (partial, *moving)


def joined_dot(blocks, weight, nt=False, tile=256, dtype=F32):
    total, depth = sum(v.shape[0] for v in blocks), blocks[0].shape[1]
    columns = weight.shape[0] if nt else weight.shape[1]
    tile = min(tile, columns)
    count = len(blocks)

    def kernel(*refs):
        w_ref, joined, out = refs[count:]

        @pl.when(pl.program_id(0) == 0)
        def _():
            at = 0
            for ref in refs[:count]:
                joined[at : at + ref.shape[0], :] = ref[...]
                at += ref.shape[0]

        dims = (((1,), (1 if nt else 0,)), ((), ()))
        out[...] = lax.dot_general(
            joined[...], w_ref[...], dims, preferred_element_type=F32
        ).astype(dtype)

    once = pl.Buffered(1)
    outs = [
        jax.ShapeDtypeStruct((total, depth), BF16),
        jax.ShapeDtypeStruct((total, columns), dtype),
    ]
    w_spec = (
        pl.BlockSpec((tile, depth), lambda j: (j, 0))
        if nt
        else pl.BlockSpec((depth, tile), lambda j: (0, j))
    )
    return pl.pallas_call(
        kernel,
        grid=(columns // tile,),
        in_specs=[
            pl.BlockSpec(v.shape, lambda j: (0, 0), pipeline_mode=once) for v in blocks
        ]
        + [w_spec],
        out_specs=[
            pl.BlockSpec((total, depth), lambda j: (0, 0), pipeline_mode=once),
            pl.BlockSpec((total, tile), lambda j: (0, j)),
        ],
        out_shape=outs,
        cost_estimate=cost((*blocks, weight), outs, 2 * total * depth * columns),
        compiler_params=room(),
    )(*blocks, weight)


def ffn_specs(blocks, width):
    total, depth = sum(v.shape[0] for v in blocks), blocks[0].shape[1]
    tile = run_of(width, 2)
    once = pl.Buffered(1)
    whole = [pl.BlockSpec(v.shape, lambda j: (0, 0), pipeline_mode=once) for v in blocks]
    joined = pl.BlockSpec((total, depth), lambda j: (0, 0), pipeline_mode=once)
    return (total, depth, tile, whole, joined, lambda c: pl.BlockSpec((total, c), lambda j: (0, j)))


def join_once(refs, joined):
    @pl.when(pl.program_id(0) == 0)
    def _():
        at = 0
        for ref in refs:
            joined[at : at + ref.shape[0], :] = ref[...]
            at += ref.shape[0]


def ffn_enter(blocks, weight):
    width = weight.shape[1] // 2
    total, depth, tile, whole, joined_spec, cut = ffn_specs(blocks, width)
    count = len(blocks)

    def kernel(*refs):
        w_ref, joined, both_ref, hidden_ref = refs[count:]
        join_once(refs[:count], joined)
        both = jnp.dot(joined[...], w_ref[...], preferred_element_type=F32)
        gate, up = both[:, :tile], both[:, tile:]
        both_ref[...] = both
        hidden_ref[...] = (gate * jax.nn.sigmoid(gate) * up).astype(BF16)

    outs = [
        jax.ShapeDtypeStruct((total, depth), BF16),
        jax.ShapeDtypeStruct((total, 2 * width), F32),
        jax.ShapeDtypeStruct((total, width), BF16),
    ]
    return pl.pallas_call(
        kernel,
        grid=(width // tile,),
        in_specs=whole + [pl.BlockSpec((depth, 2 * tile), lambda j: (0, j))],
        out_specs=[joined_spec, cut(2 * tile), cut(tile)],
        out_shape=outs,
        cost_estimate=cost((*blocks, weight), outs, 4 * total * depth * width),
        compiler_params=room(),
    )(*blocks, weight)


def ffn_back(blocks, weight, both):
    width = weight.shape[0]
    total, depth, tile, whole, joined_spec, cut = ffn_specs(blocks, width)
    count = len(blocks)

    def kernel(*refs):
        w_ref, both_ref, joined, grad_ref = refs[count:]
        join_once(refs[:count], joined)
        d_hidden = lax.dot_general(
            joined[...], w_ref[...], (((1,), (1,)), ((), ())), preferred_element_type=F32
        )
        d_hidden = d_hidden.astype(BF16).astype(F32)
        gate, up = both_ref[:, :tile], both_ref[:, tile:]
        open_gate = jax.nn.sigmoid(gate)
        part = d_hidden * open_gate
        grad_ref[:, :tile] = (part * up * (1.0 + gate * (1.0 - open_gate))).astype(BF16)
        grad_ref[:, tile:] = (part * gate).astype(BF16)

    outs = [
        jax.ShapeDtypeStruct((total, depth), BF16),
        jax.ShapeDtypeStruct((total, 2 * width), BF16),
    ]
    return pl.pallas_call(
        kernel,
        grid=(width // tile,),
        in_specs=whole + [pl.BlockSpec((tile, depth), lambda j: (j, 0)), cut(2 * tile)],
        out_specs=[joined_spec, cut(2 * tile)],
        out_shape=outs,
        cost_estimate=cost((*blocks, weight, both), outs, 2 * total * depth * width),
        compiler_params=room(),
    )(*blocks, weight, both)


def after(value, *others):
    return lax.optimization_barrier((value, *others))[0]


def cost(ins, outs, flops=0, exps=0):
    moved = sum(v.size * v.dtype.itemsize for v in (*ins, *outs))
    return pl.CostEstimate(flops=flops, bytes_accessed=moved, transcendentals=exps)


def room():
    return pltpu.CompilerParams(vmem_limit_bytes=60 * MIB)


def place_call(kernel, place, ins, outs, scratch=()):
    vmem = pl.BlockSpec(memory_space=pltpu.VMEM)
    return pl.pallas_call(
        kernel,
        in_specs=[pl.BlockSpec(memory_space=pltpu.SMEM)] + [vmem] * len(ins),
        out_specs=[vmem] * len(outs),
        out_shape=outs,
        scratch_shapes=scratch,
        cost_estimate=cost(ins, outs),
        compiler_params=room(),
    )(place.reshape(1), *ins)


def shifted(place_ref, k, n):
    return lax.rem(place_ref[0] + (k + n), n)


def lanes_at(index, width):
    return pl.ds(pl.multiple_of(index * width, width), width)


def run_of(width, parts):
    return min(256, max(128, width // 4)) if parts == 2 else width


def cut_columns(weight, parts, place, n):
    rows = weight.shape[0]
    width = weight.shape[1] // parts // n
    run = run_of(width, parts)

    def kernel(place_ref, w_ref, *outs):
        for k in range(n):
            dest = shifted(place_ref, k, n)
            for at in range(width // run):
                for p in range(parts):
                    to = (at * parts + p) * run
                    start = pl.multiple_of((p * n + dest) * width + at * run, run)
                    outs[k][:, to : to + run] = w_ref[:, pl.ds(start, run)]

    piece = jax.ShapeDtypeStruct((rows, parts * width), weight.dtype)
    return place_call(kernel, place, [weight], [piece] * n)


def cut_rows(v, place, n):
    rows = v.shape[0] // n

    def kernel(place_ref, v_ref, *outs):
        for k in range(n):
            outs[k][...] = v_ref[lanes_at(shifted(place_ref, k, n), rows), :]

    piece = jax.ShapeDtypeStruct((rows, v.shape[1]), v.dtype)
    return place_call(kernel, place, [v], [piece] * n)


def join_rows(pieces, place, n):
    rows, width = pieces[0].shape

    def kernel(place_ref, *refs):
        for k in range(n):
            refs[n][lanes_at(shifted(place_ref, -k, n), rows), :] = refs[k][...]

    whole = jax.ShapeDtypeStruct((n * rows, width), pieces[0].dtype)
    return place_call(kernel, place, pieces, [whole])[0]


def join_columns(pieces, parts, place, dtype):
    n = len(pieces)
    rows, width = pieces[0].shape[0], pieces[0].shape[1] // parts
    run = run_of(width, parts)

    def kernel(place_ref, *refs):
        for k in range(n):
            source = shifted(place_ref, -k, n)
            for at in range(width // run):
                for p in range(parts):
                    cut = refs[k][:, (at * parts + p) * run : (at * parts + p + 1) * run]
                    start = pl.multiple_of((p * n + source) * width + at * run, run)
                    refs[n][:, pl.ds(start, run)] = cut.astype(dtype)

    whole = jax.ShapeDtypeStruct((rows, parts * n * width), dtype)
    return place_call(kernel, place, pieces, [whole])[0]


def send_one(pieces, k, *ties):
    n = len(pieces)
    return lax.ppermute(after(pieces[k], *ties), "ctx", [(i, (i + k) % n) for i in range(n)])


def send_on(pieces):
    got = [pieces[0]]
    for k in range(1, len(pieces)):
        got.append(send_one(pieces, k, *got[max(k - 4, 0) : max(k - 3, 0)]))
    return got


def send_columns(weight, parts):
    n = lax.axis_size("ctx")
    rows = weight.shape[0]
    width = weight.shape[1] // parts // n
    if n <= 8:
        return send_on(cut_columns(weight, parts, lax.axis_index("ctx"), n))
    cut = weight.reshape(rows, parts, n, -1, run_of(width, parts)).transpose(2, 0, 3, 1, 4)
    return [lax.all_to_all(cut.reshape(n, rows, parts * width), "ctx", 0, 0, tiled=True)]


def take_columns(sent):
    if len(sent) == 1:
        return sent[0].reshape(-1, sent[0].shape[-1])
    return join_rows(sent, lax.axis_index("ctx"), len(sent))


def send_rows(mine):
    n = lax.axis_size("ctx")
    if n <= 8:
        return send_on(cut_rows(mine, lax.axis_index("ctx"), n))
    return [lax.all_to_all(mine.reshape(n, -1, mine.shape[1]), "ctx", 0, 0, tiled=True)]


def take_rows(sent, parts):
    if len(sent) > 1:
        return join_columns(sent, parts, lax.axis_index("ctx"), F32)
    n, rows, columns = sent[0].shape
    got = sent[0].reshape(n, rows, -1, parts, run_of(columns // parts, parts))
    return got.transpose(1, 3, 0, 2, 4).reshape(rows, -1).astype(F32)


def gather_groups(v):
    return lax.all_gather(v, "fsdp", axis=0, tiled=True)


def scatter_groups(v):
    return lax.psum_scatter(v, "fsdp", scatter_dimension=0, tiled=True)


def far(v):
    return lax.ppermute(v, "fsdp", [(i, i ^ 2) for i in range(4)])


def near(v):
    return lax.ppermute(v, "fsdp", [(i, i ^ 1) for i in range(4)])


def in_order(held):
    me = lax.axis_index("fsdp")
    out = jnp.zeros((4,) + held[0].shape, held[0].dtype)
    for k, h in enumerate(held):
        out = lax.dynamic_update_slice_in_dim(out, h[None], me ^ k, 0)
    return out.reshape(4 * held[0].shape[0], held[0].shape[1])


def cut_groups(v):
    me = lax.axis_index("fsdp")
    rows = v.shape[0] // 4
    return [lax.dynamic_slice_in_dim(v, (me ^ k) * rows, rows, 0) for k in range(4)]


def add_low(got, own):
    return (got.astype(F32) + own.astype(F32)).astype(BF16)


def weight_share(gradient, shard_rows):
    partial_rows = lax.psum_scatter(
        gradient.astype(BF16), "ctx", scatter_dimension=0, tiled=True
    )
    return lax.psum_scatter(partial_rows, "fsdp", scatter_dimension=0, tiled=True).astype(F32)


def spread_lanes(v, n, m):
    w = D // (n * m)
    cuts = [v[:, (c * m + f) * w : (c * m + f + 1) * w] for f in range(m) for c in range(n)]
    return jnp.concatenate(cuts, axis=1)


def unspread_lanes(v, n, m):
    return spread_lanes(v, m, n)


def sum_all(v, beside):
    beside, made = list(beside), []
    for axis in ("ctx", "fsdp"):
        n = lax.axis_size(axis)
        if n & (n - 1):
            v = lax.psum(v, axis)
            continue
        step = 1
        while step < n:
            got = lax.ppermute(v, axis, [(i, i ^ step) for i in range(n)])
            if beside:
                got, now = lax.optimization_barrier((got, beside.pop(0)))
                made.append(now)
            v = v + got
            step *= 2
    return (v, made + beside)


LANES = 128
HC_ROWS = 32


def lanes_of(rows):
    return lax.broadcasted_iota(jnp.int32, (rows, LANES), 1)


def put(held, lane, at, column):
    return jnp.where(lane == at, column, held)


def mean_of(v):
    return jnp.sum(v, axis=1, keepdims=True) * (1.0 / D)


def stream_parts(ref):
    return [ref[:, i * D : (i + 1) * D].astype(F32) for i in range(STREAMS)]


def mixed(parts, coef, branch):
    outs = []
    for j in range(STREAMS):
        total = coef[:, 8 * j + 5 : 8 * j + 6] * branch
        for i in range(STREAMS):
            total = total + coef[:, 8 * i + 1 + j : 8 * i + 2 + j] * parts[i]
        outs.append(total)
    return outs


def branch_grad(parts, coef):
    return sum(coef[:, 8 * j + 5 : 8 * j + 6] * parts[j] for j in range(STREAMS))


def layer_in(parts, coef):
    return sum(coef[:, 8 * i : 8 * i + 1] * parts[i] for i in range(STREAMS))


def enter(parts, wpack, static):
    rows = parts[0].shape[0]
    lane = lanes_of(rows)
    aux = jnp.zeros((rows, LANES), F32)
    pieces = ([], [], [])
    for i in range(STREAMS):
        mean = mean_of(parts[i])
        cent = parts[i] - mean
        rstd = lax.rsqrt(mean_of(cent * cent) + eps)
        left = cent * rstd
        for piece in pieces:
            piece.append(left.astype(BF16))
            left = left - piece[-1].astype(F32)
        aux = put(aux, lane, 8 * i + 6, mean)
        aux = put(aux, lane, 8 * i + 7, rstd)
    dims = (((1,), (1,)), ((), ()))
    proj = sum(
        lax.dot_general(jnp.concatenate(p, axis=0), wpack, dims, preferred_element_type=F32)
        for p in pieces[::-1]
    )
    proj = proj + pltpu.roll(proj, LANES - 32, 1) + pltpu.roll(proj, LANES - 64, 1)
    for i in range(STREAMS):
        own = jnp.where(lane < 6, proj[i * rows : (i + 1) * rows], 0.0)
        aux += own if i == 0 else pltpu.roll(own, 8 * i, 1)
    coef = static + jnp.tanh(aux)
    x = layer_in(parts, coef)
    mean = mean_of(x)
    cent = x - mean
    rstd = lax.rsqrt(mean_of(cent * cent) + eps)
    aux = put(aux, lane, 32, mean)
    aux = put(aux, lane, 33, rstd)
    return (aux, coef, cent * rstd)


def leave_grads(parts, grads, branch):
    rows = parts[0].shape[0]
    lane = lanes_of(rows)
    red = jnp.zeros((rows, LANES), F32)
    for j in range(STREAMS):
        red = put(red, lane, 8 * j + 5, jnp.sum(grads[j] * branch, axis=1, keepdims=True))
        for i in range(STREAMS):
            red = put(
                red, lane, 8 * i + 1 + j, jnp.sum(parts[i] * grads[j], axis=1, keepdims=True)
            )
    return red


def enter_back(parts, grads, aux, coef, red, du, wpack, normed_ref, dz_ref, stat_ref, step):
    rows = parts[0].shape[0]
    lane = lanes_of(rows)
    x = layer_in(parts, coef)
    rx = aux[:, 33:34]
    nx = (x - aux[:, 32:33]) * rx
    dx = rx * (du - mean_of(du) - nx * mean_of(du * nx))
    for i in range(STREAMS):
        red = put(red, lane, 8 * i, jnp.sum(parts[i] * dx, axis=1, keepdims=True))
    used = (lane < 8 * STREAMS) & (lane % 8 < 6)
    slope = jnp.tanh(aux)
    dz = jnp.where(used, red * (1.0 - slope * slope), 0.0)
    stat_ref[0:1, :] += jnp.sum(red, axis=0, keepdims=True)
    dz_ref[pl.ds(step * rows, rows), :] = dz
    both = dz * aux
    packed = []
    for i in range(STREAMS):
        own = dz if i == 0 else pltpu.roll(dz, LANES - 8 * i, 1)
        own = jnp.where(lane < 6, own, 0.0)
        top = own.astype(BF16).astype(F32)
        packed.append((top + pltpu.roll(top, 32, 1) + pltpu.roll(own - top, 96, 1)).astype(BF16))
    dn_all = lax.dot_general(
        jnp.concatenate(packed, axis=0), wpack, (((1,), (0,)), ((), ())), preferred_element_type=F32
    )
    outs = []
    total_rows = dz_ref.shape[0]
    for i in range(STREAMS):
        mean, rstd = aux[:, 8 * i + 6 : 8 * i + 7], aux[:, 8 * i + 7 : 8 * i + 8]
        normed = (parts[i] - mean) * rstd
        normed_ref[pl.ds(i * total_rows + step * rows, rows), :] = normed.astype(BF16)
        dn = dn_all[i * rows : (i + 1) * rows]
        own = (lane >= 8 * i) & (lane < 8 * i + 6)
        along = jnp.sum(jnp.where(own, both, 0.0), axis=1, keepdims=True) * (1.0 / D)
        total = coef[:, 8 * i : 8 * i + 1] * dx + rstd * (dn - mean_of(dn) - normed * along)
        for j in range(STREAMS):
            total = total + coef[:, 8 * i + 1 + j : 8 * i + 2 + j] * grads[j]
        outs.append(total)
    return outs


def finish_hc(normed_ref, dz_ref, stat_ref, hc_ref):
    across = dz_ref[...].T
    left = jnp.concatenate([across[8 * i : 8 * i + 8] for i in range(STREAMS)], axis=1)
    top = left.astype(BF16)
    low = (left - top.astype(F32)).astype(BF16)
    both = lax.dot_general(
        jnp.concatenate([top, low], axis=0),
        normed_ref[...],
        (((1,), (0,)), ((), ())),
        preferred_element_type=F32,
    )
    hc_ref[...] = both[0:8] + both[8:16]
    hc_ref[6:7, 0:LANES] = stat_ref[0:1, :]


def sum_of(refs):
    return sum(ref[...].astype(F32) for ref in refs)


def first_kernel(order, s_ref, w_ref, static_ref, u_ref, aux_ref):
    aux, _, u = enter(stream_parts(s_ref), w_ref[...], static_ref[0:1, :])
    u = u.astype(BF16)
    u_ref[...] = spread_lanes(u, *order) if order else u
    aux_ref[...] = aux


def middle_kernel(order, s_ref, c_ref, y_ref, aux0_ref, w_ref, static_ref, u_ref, dy_ref, aux_ref):
    coef0 = static_ref[0:1, :] + jnp.tanh(aux0_ref[...])
    mid = mixed(stream_parts(s_ref), coef0, y_ref[...])
    aux, coef, u = enter(mid, w_ref[...], static_ref[1:2, :])
    u_ref[...] = spread_lanes(u.astype(BF16), *order)
    aux_ref[...] = aux
    dy_ref[...] = branch_grad(stream_parts(c_ref), coef).astype(BF16)


def out_kernel(
    s_ref, y_ref, y2a_ref, y2b_ref, y2c_ref, aux0_ref, aux1_ref, static_ref, out_ref
):
    coef0 = static_ref[0:1, :] + jnp.tanh(aux0_ref[...])
    coef1 = static_ref[1:2, :] + jnp.tanh(aux1_ref[...])
    mid = mixed(stream_parts(s_ref), coef0, y_ref[...])
    y2 = sum_of((y2a_ref, y2b_ref, y2c_ref))
    for j, total in enumerate(mixed(mid, coef1, y2)):
        out_ref[:, j * D : (j + 1) * D] = total.astype(BF16)


def back_kernel(
    order, s_ref, c_ref, y_ref, y2a_ref, y2b_ref, y2c_ref, dua_ref, dub_ref, duc_ref, aux0_ref,
    aux1_ref, w_ref, static_ref, dmid_ref, dy_ref, hc_ref, normed_ref, dz_ref, stat_ref,
):
    step = pl.program_id(0)

    @pl.when(step == 0)
    def _():
        stat_ref[...] = jnp.zeros_like(stat_ref)

    coef0 = static_ref[0:1, :] + jnp.tanh(aux0_ref[...])
    aux1 = aux1_ref[...]
    coef1 = static_ref[1:2, :] + jnp.tanh(aux1)
    mid = mixed(stream_parts(s_ref), coef0, y_ref[...])
    du = unspread_lanes(sum_of((dua_ref, dub_ref, duc_ref)), *order)
    grads = stream_parts(c_ref)
    red = leave_grads(mid, grads, sum_of((y2a_ref, y2b_ref, y2c_ref)))
    dmid = enter_back(
        mid, grads, aux1, coef1, red, du, w_ref[...],
        normed_ref, dz_ref, stat_ref, step,
    )
    for j in range(STREAMS):
        dmid_ref[:, j * D : (j + 1) * D] = dmid[j]
    dy_ref[...] = branch_grad(dmid, coef0).astype(BF16)

    @pl.when(step == pl.num_programs(0) - 1)
    def _():
        finish_hc(normed_ref, dz_ref, stat_ref, hc_ref)


def red_kernel(s_ref, dmid_ref, y_ref, red_ref):
    red_ref[...] = leave_grads(stream_parts(s_ref), stream_parts(dmid_ref), y_ref[...])


def last_kernel(
    order, s_ref, dmid_ref, *refs
):
    du_refs = refs[:-9]
    red_ref, aux0_ref, w_ref, static_ref, ds_ref, hc_ref, normed_ref, dz_ref, stat_ref = refs[-9:]
    step = pl.program_id(0)

    @pl.when(step == 0)
    def _():
        stat_ref[...] = jnp.zeros_like(stat_ref)

    aux0 = aux0_ref[...]
    coef0 = static_ref[0:1, :] + jnp.tanh(aux0)
    parts, grads = stream_parts(s_ref), stream_parts(dmid_ref)
    du = sum_of(du_refs)
    if order:
        du = unspread_lanes(du, *order)
    ds = enter_back(
        parts, grads, aux0, coef0, red_ref[...], du, w_ref[...],
        normed_ref, dz_ref, stat_ref, step,
    )
    for j in range(STREAMS):
        ds_ref[:, j * D : (j + 1) * D] = ds[j].astype(BF16)

    @pl.when(step == pl.num_programs(0) - 1)
    def _():
        finish_hc(normed_ref, dz_ref, stat_ref, hc_ref)


def row_call(kernel, rows, ins, outs, hc=False):
    tile = HC_ROWS if hc else min(rows, 2 * HC_ROWS)

    def cut(columns):
        return pl.BlockSpec((tile, columns), lambda i: (i, 0))

    def whole(shape):
        return pl.BlockSpec(shape, lambda i: (0, 0))

    in_specs = [cut(a.shape[1]) if by_rows else whole(a.shape) for a, by_rows in ins]
    out_specs = [cut(columns) for columns, _ in outs]
    out_shape = [jax.ShapeDtypeStruct((rows, columns), dtype) for columns, dtype in outs]
    scratch = []
    if hc:
        out_specs.append(whole((8, D)))
        out_shape.append(jax.ShapeDtypeStruct((8, D), F32))
        scratch = [
            pltpu.VMEM((STREAMS * rows, D), BF16),
            pltpu.VMEM((rows, LANES), F32),
            pltpu.VMEM((8, LANES), F32),
        ]
    return pl.pallas_call(
        kernel,
        grid=(rows // tile,),
        in_specs=in_specs,
        out_specs=out_specs,
        out_shape=out_shape,
        scratch_shapes=scratch,
        cost_estimate=cost([a for a, _ in ins], out_shape, 100 * rows * STREAMS * D),
        compiler_params=room(),
    )(*[a for a, _ in ins])


def pack_weight(weight):
    across = jnp.pad(weight.T, ((0, 26), (0, 0)))
    top = lax.reduce_precision(across, 8, 7)
    mid = lax.reduce_precision(across - top, 8, 7)
    return jnp.concatenate([top, mid, across - top - mid, top], axis=0).astype(BF16)


Q_ROWS = 512


def turn(v, cosine, sine):
    return v * cosine + pltpu.roll(v, HEAD_DIM // 2, 1) * sine


def attend_kernel(
    q_ref, k_ref, v_ref, cos_ref, sin_ref, qpos_ref, qstart_ref, kpos_ref,
    o_ref, lse_ref, qr_ref, kr_ref, vb_ref,
):
    at = pl.program_id(1)

    @pl.when(at == 0)
    def _():
        kr_ref[...] = turn(k_ref[...], cos_ref[...], sin_ref[...]).astype(BF16)
        vb_ref[...] = v_ref[...].astype(BF16)

    here = pl.ds(at * Q_ROWS, Q_ROWS)
    query = turn(q_ref[...], cos_ref[here, :], sin_ref[here, :]).astype(BF16)
    qr_ref[...] = query
    scores = (
        lax.dot_general(query, kr_ref[...], (((1,), (1,)), ((), ())), preferred_element_type=F32)
        * SCALE
    )
    kpos = kpos_ref[0:1, :]
    keep = (kpos <= qpos_ref[...]) & (kpos >= qstart_ref[...])
    scores = jnp.where(keep, scores, -1e30)
    top = jnp.max(scores, axis=1, keepdims=True)
    grown = jnp.exp(scores - top)
    total = jnp.sum(grown, axis=1, keepdims=True)
    out = jnp.dot((grown / total).astype(BF16), vb_ref[...], preferred_element_type=F32)
    o_ref[...] = out.astype(BF16)
    lse_ref[...] = jnp.broadcast_to(top + jnp.log(total), lse_ref.shape)


def attend_back_kernel(
    q_ref, k_ref, v_ref, do_ref, lse_ref, cos_ref, sin_ref, qpos_ref, qstart_ref, kpos_ref,
    dq_ref, dk_ref, dv_ref, dk_sum, dv_sum,
):
    at = pl.program_id(1)

    @pl.when(at == 0)
    def _():
        dk_sum[...] = jnp.zeros_like(dk_sum)
        dv_sum[...] = jnp.zeros_like(dv_sum)

    here = pl.ds(at * Q_ROWS, Q_ROWS)
    query, keys, d_out = q_ref[...], k_ref[...], do_ref[...]
    nt = (((1,), (1,)), ((), ()))
    tn = (((0,), (0,)), ((), ()))
    scores = lax.dot_general(query, keys, nt, preferred_element_type=F32) * SCALE
    kpos = kpos_ref[0:1, :]
    keep = (kpos <= qpos_ref[...]) & (kpos >= qstart_ref[...])
    probs = jnp.where(keep, jnp.exp(scores - lse_ref[:, 0:1]), 0.0)
    d_probs = lax.dot_general(d_out, v_ref[...], nt, preferred_element_type=F32)
    delta = jnp.sum(probs * d_probs, axis=1, keepdims=True)
    ds = (probs * (d_probs - delta)).astype(BF16)
    dq = jnp.dot(ds, keys, preferred_element_type=F32) * SCALE
    dq_ref[...] = turn(dq, cos_ref[here, :], -sin_ref[here, :]).astype(BF16)
    dk_sum[...] += lax.dot_general(ds, query, tn, preferred_element_type=F32)
    dv_sum[...] += lax.dot_general(probs.astype(BF16), d_out, tn, preferred_element_type=F32)

    @pl.when(at == pl.num_programs(1) - 1)
    def _():
        dk_ref[...] = turn(dk_sum[...] * SCALE, cos_ref[...], -sin_ref[...]).astype(BF16)
        dv_ref[...] = dv_sum[...].astype(BF16)


def attention_specs(total):
    by_query = pl.BlockSpec((Q_ROWS, HEAD_DIM), lambda h, i: (i, h))
    by_head = pl.BlockSpec((total, HEAD_DIM), lambda h, i: (0, h))
    table = pl.BlockSpec((total, HEAD_DIM), lambda h, i: (0, 0))
    row = pl.BlockSpec((Q_ROWS, 1), lambda h, i: (i, 0))
    keys = pl.BlockSpec((8, total), lambda h, i: (0, 0))
    return (by_query, by_head, [table, table, row, row, keys])


def attend(qkv, heads, marks):
    total = qkv.shape[0]
    by_query, by_head, shared = attention_specs(total)

    def of(kind):
        return pl.BlockSpec((total, HEAD_DIM), lambda h, i: (0, kind * heads + h))

    low = jax.ShapeDtypeStruct((total, heads * HEAD_DIM), BF16)
    wide = jax.ShapeDtypeStruct((total, heads * HEAD_DIM), F32)
    return pl.pallas_call(
        attend_kernel,
        grid=(heads, total // Q_ROWS),
        in_specs=[by_query, of(1), of(2)] + shared,
        out_specs=[by_query, by_query, by_query, by_head, by_head],
        out_shape=[low, wide, low, low, low],
        cost_estimate=cost([qkv], [low] * 4, 4 * heads * total**2 * HEAD_DIM, heads * total**2),
        compiler_params=room(),
    )(qkv, qkv, qkv, *marks)


def attend_back(query, keys, values, d_out, lse, heads, marks):
    total = query.shape[0]
    by_query, by_head, shared = attention_specs(total)
    low = jax.ShapeDtypeStruct((total, heads * HEAD_DIM), BF16)
    return pl.pallas_call(
        attend_back_kernel,
        grid=(heads, total // Q_ROWS),
        in_specs=[by_query, by_head, by_head, by_query, by_query] + shared,
        out_specs=[by_query, by_head, by_head],
        out_shape=[low, low, low],
        scratch_shapes=[pltpu.VMEM((total, HEAD_DIM), F32)] * 2,
        cost_estimate=cost([lse], [low] * 7, 10 * heads * total**2 * HEAD_DIM, heads * total**2),
        compiler_params=room(),
    )(query, keys, values, d_out, lse, *marks)


def angles(inside):
    half = HEAD_DIM // 2
    freq = 10000.0 ** (-jnp.arange(half, dtype=F32) / half)
    angle = inside.astype(F32)[:, None] * freq[None, :]
    cosine, sine = jnp.cos(angle), jnp.sin(angle)
    return (jnp.concatenate([cosine, cosine], axis=1), jnp.concatenate([-sine, sine], axis=1))


class HeadAttention:
    def __init__(self, rows, w_qkv, w_out, pair_row, length_row):
        n = lax.axis_size("ctx")
        self.group = lax.axis_index("fsdp")
        self.rows, self.heads = rows, HEADS // n
        owners = ring_owners(n, lax.axis_index("ctx"))
        position, _, start = places(pair_row, length_row, rows, owners)
        cosine, sine = angles(position - start)
        kpos = jnp.broadcast_to(position[None, :], (8, position.shape[0]))
        self.marks = (cosine, sine, position[:, None], start[:, None], kpos)
        self.cut_qkv = cut_columns(w_qkv, 3, lax.axis_index("ctx"), n)
        self.w_out = w_out

    def to_tokens(self, heads_out):
        n = lax.axis_size("ctx")
        order, offsets = ring_order(n), ring_offsets(n)
        got = []
        for offset in offsets:
            at = offsets.index(-offset if 2 * offset != -n else offset)
            own = heads_out[at * self.rows : (at + 1) * self.rows]
            pairs = [(order[i], order[(i - offset) % n]) for i in range(n)]
            got.append(lax.ppermute(own, "ctx", pairs) if offset else own)
        return got

    def join_tokens(self, got):
        n, m = lax.axis_size("ctx"), lax.axis_size("fsdp")
        offsets, width = ring_offsets(n), got[0].shape[1]

        def kernel(place_ref, *refs):
            place = place_ref[0]
            mine = jnp.where(place % 2 == 0, place // 2, n - 1 - place // 2)
            held = refs[-1]
            for k, offset in enumerate(offsets):
                at = lax.rem(mine + offset + n, n)
                owner = jnp.where(at < n // 2, 2 * at, 2 * (n - 1 - at) + 1)
                held[:, lanes_at(owner, width)] = refs[k][...]
            refs[n][...] = spread_lanes(held[...], n, m)

        whole = jax.ShapeDtypeStruct((self.rows, n * width), got[0].dtype)
        scratch = [pltpu.VMEM(whole.shape, whole.dtype)]
        return place_call(kernel, lax.axis_index("ctx"), got, [whole], scratch)[0]

    def forward(self, u, w_gate_up, w_down):
        n, m = lax.axis_size("ctx"), lax.axis_size("fsdp")
        got = {}

        place = lax.axis_index("ctx")
        out_ctx = lax.all_gather(self.w_out, "ctx", axis=0, tiled=True)
        cut = self.cut_qkv
        sent_qkv = [cut[0], *[send_one(cut, k) for k in (1, 2)]]
        sent_qkv += [send_one(cut, k, u) for k in range(3, n)]

        def early(step, arrived):
            if step == 1:
                arrived, sent, self.marks = lax.optimization_barrier(
                    (arrived, sent_qkv, self.marks)
                )
                got["own"] = take_columns(sent)
                got["far"] = far(got["own"])
                got["cut"] = cut_columns(after(w_gate_up, got["own"]), 2, place, n)
            if step == 2:
                arrived, got["far"], got["out"], got["cut"] = lax.optimization_barrier(
                    (arrived, got["far"], out_ctx, got["cut"])
                )
                got["near"] = [near(got["own"]), near(got["far"])]
            return arrived

        blocks = ring_gather(u, early)
        blocks, got["near"] = lax.optimization_barrier((blocks, got["near"]))
        self.qkv_cols = in_order([got["own"], got["near"][0], got["far"], got["near"][1]])
        out_all = lax.all_gather(got["out"], "fsdp", axis=0, tiled=True)
        down_rows = gather_groups(after(w_down, *blocks))
        cut, blocks = lax.optimization_barrier((got["cut"], blocks))
        first = [send_one(cut, k) for k in (1, 2)]
        self.u_all, qkv = joined_dot(blocks, self.qkv_cols)
        qkv, first = lax.optimization_barrier((qkv, first))
        second = [send_one(cut, k, qkv) for k in (3, 4)]
        self.o, self.lse, self.q, self.k, self.v = attend(qkv, self.heads, self.marks)
        o, second = lax.optimization_barrier((self.o, second))
        sent_o = self.to_tokens(o)
        sent = [cut[0], *first, *second, *[send_one(cut, k, o) for k in range(5, n)]]
        held = out_all.reshape(m, n, -1, D)
        held = lax.dynamic_slice_in_dim(held, lax.axis_index("ctx"), 1, 1)
        self.out_rows = held.reshape(-1, D)
        y = jnp.dot(self.join_tokens(sent_o), out_all, preferred_element_type=F32)
        y, *sent[:5] = lax.optimization_barrier((y, *sent[:5]))
        return (y, sent, down_rows)

    def backward(self, dy, dy_blocks, grad_gate_up, grad_down):
        got = {}

        dy_all, d_out = joined_dot(dy_blocks, self.out_rows, nt=True, dtype=BF16)
        n, place = lax.axis_size("ctx"), lax.axis_index("ctx")
        cut = cut_rows(after(grad_gate_up, dy_all), place, n)
        first = [send_one(cut, k) for k in range(1, 4)]
        dq, dk, dv = attend_back(self.q, self.k, self.v, d_out, self.lse, self.heads, self.marks)
        dq, first = lax.optimization_barrier((dq, first))
        second = [send_one(cut, k, dq) for k in range(4, n)]
        d_qkv = jnp.concatenate([dq, dk, dv], axis=1)
        partial = jnp.einsum(
            "tc,dc->td", d_qkv, self.qkv_cols, preferred_element_type=F32
        ).astype(BF16)

        def early(step, arrived):
            if step == 0:
                u_all = after(self.u_all, arrived)
                g = jnp.einsum("td,tc->dc", u_all, d_qkv, preferred_element_type=F32)
                got["qkv"] = g.astype(BF16)
            if step == 1:
                arrived, got["qkv"] = lax.optimization_barrier((arrived, got["qkv"]))
                got["qkv"] = scatter_groups(got["qkv"])
                arrived, got["second"] = lax.optimization_barrier((arrived, second))
                o, dy_now = after([self.o, dy_all], arrived)
                g = jnp.einsum("te,td->ed", o, dy_now, preferred_element_type=F32)
                got["out"] = g.astype(BF16)
            if step == 2:
                arrived, got["out"], got["down"] = lax.optimization_barrier(
                    (arrived, got["out"], grad_down)
                )
            return arrived

        du = ring_scatter(partial, self.rows, early)
        sent_qkv = send_rows(got["qkv"])
        du, sent_qkv = lax.optimization_barrier((du, sent_qkv))
        return (
            du,
            lambda tie: take_rows(after(sent_qkv, tie), 3),
            scatter_groups(got["out"]).astype(F32),
            take_rows([cut[0], *first, *got["second"]], 2),
            got["down"].astype(F32),
        )


def rotate(v, inside, sign):
    half = v.shape[-1] // 2
    freq = 10000.0 ** (-jnp.arange(half, dtype=F32) / half)
    angle = inside.astype(F32)[:, None] * freq[None, :]
    cosine = jnp.cos(angle)[:, None, :]
    sine = sign * jnp.sin(angle)[:, None, :]
    first, second = (v[..., :half], v[..., half:])
    return jnp.concatenate(
        [first * cosine - second * sine, second * cosine + first * sine], axis=-1
    )


class TokenAttention:
    def __init__(self, rows, w_qkv, w_out, pair_row, length_row):
        n = lax.axis_size("ctx")
        place = lax.axis_index("ctx")
        self.rows = rows
        owners = jnp.arange(n, dtype=jnp.int32)
        kpos, kdoc, kstart = places(pair_row, length_row, rows, owners)

        def own(v):
            return lax.dynamic_slice_in_dim(v, place * rows, rows)

        self.inside = own(kpos - kstart)
        self.keep = (kpos[None, :] <= own(kpos)[:, None]) & (kdoc[None, :] == own(kdoc)[:, None])
        self.w_qkv, self.w_out = w_qkv, w_out

    def gathered(self, weight):
        return lax.all_gather(weight, ("ctx", "fsdp"), axis=0, tiled=True)

    def scores(self):
        scores = jnp.einsum("qhe,hke->hqk", self.q, self.k, preferred_element_type=F32) * SCALE
        return jnp.where(self.keep[None], scores, -1e30)

    def forward(self, u, w_gate_up, w_down):
        rows, shape = self.rows, (self.rows, HEADS, HEAD_DIM)
        self.u = u
        qkv = jnp.dot(u, self.gathered(self.w_qkv), preferred_element_type=F32)
        self.q = rotate(qkv[:, :D].reshape(shape), self.inside, 1.0).astype(BF16)
        key = rotate(qkv[:, D : 2 * D].reshape(shape), self.inside, 1.0).astype(BF16)
        value = qkv[:, 2 * D :].reshape(shape).astype(BF16)
        self.k = lax.all_gather(key.transpose(1, 0, 2), "ctx", axis=1, tiled=True)
        self.v = lax.all_gather(value.transpose(1, 0, 2), "ctx", axis=1, tiled=True)
        scores = self.scores()
        top = jnp.max(scores, axis=-1, keepdims=True)
        self.lse = top + jnp.log(jnp.sum(jnp.exp(scores - top), axis=-1, keepdims=True))
        probs = jnp.exp(scores - self.lse).astype(BF16)
        attended = jnp.einsum("hqk,hke->qhe", probs, self.v, preferred_element_type=F32)
        self.o = attended.reshape(rows, D).astype(BF16)
        y = jnp.dot(self.o, self.gathered(self.w_out), preferred_element_type=F32)
        return (y, send_columns(w_gate_up, 2), gather_groups(w_down))

    def backward(self, dy, dy_blocks, grad_gate_up, grad_down):
        rows = self.rows
        d_out = jnp.einsum(
            "td,ed->te", dy, self.gathered(self.w_out), preferred_element_type=F32
        )
        d_out = d_out.astype(BF16).reshape(rows, HEADS, HEAD_DIM)
        grad_out = jnp.einsum("te,td->ed", self.o, dy, preferred_element_type=F32)
        again = jnp.exp(self.scores() - self.lse)
        d_probs = jnp.einsum("qhe,hke->hqk", d_out, self.v, preferred_element_type=F32)
        delta = jnp.sum(again * d_probs, axis=-1, keepdims=True)
        ds = (again * (d_probs - delta)).astype(BF16)
        dq = jnp.einsum("hqk,hke->qhe", ds, self.k, preferred_element_type=F32) * SCALE
        dk_all = jnp.einsum("hqk,qhe->hke", ds, self.q, preferred_element_type=F32) * SCALE
        dv_all = jnp.einsum(
            "hqk,qhe->hke", again.astype(BF16), d_out, preferred_element_type=F32
        )

        def shared(v):
            mine = lax.psum_scatter(v.astype(BF16), "ctx", scatter_dimension=1, tiled=True)
            return mine.astype(F32).transpose(1, 0, 2)

        dk, dv = shared(dk_all), shared(dv_all)
        d_qkv = jnp.concatenate(
            [
                rotate(dq, self.inside, -1.0).reshape(rows, D),
                rotate(dk, self.inside, -1.0).reshape(rows, D),
                dv.reshape(rows, D),
            ],
            axis=1,
        ).astype(BF16)
        du = jnp.einsum("tc,dc->td", d_qkv, self.gathered(self.w_qkv), preferred_element_type=F32)
        grad_qkv = jnp.einsum("td,tc->dc", self.u, d_qkv, preferred_element_type=F32)
        grad_qkv = weight_share(grad_qkv, self.w_qkv.shape[0])
        return (
            (du,),
            lambda tie: grad_qkv,
            weight_share(grad_out, self.w_out.shape[0]),
            take_rows(send_rows(grad_gate_up), 2),
            grad_down.astype(F32),
        )


def on_device(
    streams,
    cotangent,
    w_qkv,
    w_out,
    w_gate_up,
    w_down,
    hc_weight,
    hc_static,
    seq_lengths,
    pair_perm,
):
    n = lax.axis_size("ctx")
    group = lax.axis_index("fsdp")
    rows = streams.shape[1]
    pair_row = lax.dynamic_index_in_dim(pair_perm, group, 0, keepdims=False)
    length_row = lax.dynamic_index_in_dim(seq_lengths, group, 0, keepdims=False)
    state, cot = streams[0], cotangent[0]
    wpack0, wpack1 = pack_weight(hc_weight[0]), pack_weight(hc_weight[1])
    static = jnp.pad(hc_static, ((0, 0), (0, 0), (0, 2))).reshape(2, 8 * STREAMS)
    static = jnp.pad(static, ((0, 6), (0, LANES - 8 * STREAMS)))

    by_heads = HEADS % n == 0 and n % 2 == 0 and n > 2 and lax.axis_size("fsdp") == 4
    plan = HeadAttention if by_heads else TokenAttention
    attention = plan(rows, w_qkv, w_out, pair_row, length_row)
    order = (n, lax.axis_size("fsdp"))
    own_order = order if by_heads else None
    u, aux0 = row_call(
        functools.partial(first_kernel, own_order),
        rows,
        [(state, True), (wpack0, False), (static, False)],
        [(D, BF16), (LANES, F32)],
    )
    y, sent_gate_up, down_rows = attention.forward(u, w_gate_up, w_down)
    u2, dy2, aux1 = row_call(
        functools.partial(middle_kernel, order),
        rows,
        [(state, True), (cot, True), (y, True), (aux0, True), (wpack1, False), (static, False)],
        [(D, BF16), (D, BF16), (LANES, F32)],
    )
    got = {}

    def early_u2(step, arrived):
        if step == 0:
            got["own"] = take_columns(sent)
            arrived, got["own"], got["down"] = lax.optimization_barrier(
                (arrived, got["own"], down_rows)
            )
        return arrived

    u2, sent = lax.optimization_barrier((u2, sent_gate_up))
    u2_blocks = ring_gather(u2, early_u2)
    gate_up_cols, down_rows = gather_groups(got["own"]), got["down"]
    width = FF // n
    u2_all, both, hidden = ffn_enter(u2_blocks, gate_up_cols)

    def early_dy2(step, arrived):
        return after(arrived, both) if step == 2 else arrived

    dy2_blocks = ring_gather(after(dy2, *u2_blocks[-2:]), early_dy2)
    y2_partial = jnp.dot(hidden, down_rows, preferred_element_type=F32).astype(BF16)
    y2_partial, dy2_blocks = lax.optimization_barrier((y2_partial, dy2_blocks))

    def early_y2(step, arrived):
        if step == 0:
            got["dy2_all"], got["dgu"] = ffn_back(after(dy2_blocks, arrived), down_rows, both)
        if step == 1:
            dgu = after(got["dgu"], arrived)
            got["du2"] = jnp.einsum(
                "tg,dg->td", dgu, gate_up_cols, preferred_element_type=F32
            ).astype(BF16)
        return arrived

    y2 = ring_scatter(y2_partial, rows, early_y2)

    def early_du2(step, arrived):
        if step == 0:
            left = after(u2_all, got["du2"])
            g = jnp.einsum("td,tg->dg", left, got["dgu"], preferred_element_type=F32)
            got["gate_up"] = g.astype(BF16)
        if step == 1:
            arrived, got["y2"] = lax.optimization_barrier((arrived, tuple(y2)))
        if step == 2:
            arrived, got["gate_up"] = lax.optimization_barrier((arrived, got["gate_up"]))
        return arrived

    du2 = ring_scatter(got["du2"], rows, early_du2)
    y2 = got["y2"] if "y2" in got else y2
    grad_gate_up = scatter_groups(got["gate_up"])
    dmid, dy, hc1 = row_call(
        functools.partial(back_kernel, order),
        rows,
        [
            (state, True), (cot, True), (y, True), *[(v, True) for v in y2],
            *[(v, True) for v in du2], (aux0, True), (aux1, True), (wpack1, False),
            (static, False),
        ],
        [(STREAMS * D, F32), (D, BF16)],
        hc=True,
    )
    left = after(hidden, dy)
    g = jnp.einsum("tf,td->fd", left, got["dy2_all"], preferred_element_type=F32).astype(BF16)
    terms = after(list(y2), g)
    out = row_call(
        out_kernel,
        rows,
        [
            (state, True), (y, True), *[(v, True) for v in terms], (aux0, True), (aux1, True),
            (static, False),
        ],
        [(STREAMS * D, BF16)],
    )[0]
    red0 = row_call(
        red_kernel, rows, [(after(state, out), True), (dmid, True), (y, True)], [(LANES, F32)]
    )[0]
    held = {}

    def early_dy(step, arrived):
        if step == 1:
            arrived, held["down"] = lax.optimization_barrier((arrived, g))
        if step == 2:
            arrived, held["out"] = lax.optimization_barrier((arrived, out))
        if step == 3:
            arrived, held["gate_up"], held["red0"] = lax.optimization_barrier(
                (arrived, grad_gate_up, red0)
            )
        return arrived

    dy_blocks = ring_gather(dy, early_dy)
    out, red0 = held.get("out", out), held.get("red0", red0)
    grad_gate_up = held.get("gate_up", grad_gate_up)
    grad_down = scatter_groups(held.get("down", g))
    du, take_grad_qkv, grad_out, grad_gate_up, grad_down = attention.backward(
        dy, dy_blocks, grad_gate_up, grad_down
    )
    grad_state, hc0 = row_call(
        functools.partial(last_kernel, own_order),
        rows,
        [
            (state, True), (dmid, True), *[(v, True) for v in du], (red0, True), (aux0, True),
            (wpack0, False), (static, False),
        ],
        [(STREAMS * D, BF16)],
        hc=True,
    )
    hc, beside = sum_all(
        jnp.concatenate([hc0, hc1], axis=0),
        (grad_down, grad_gate_up, take_grad_qkv(hc0), grad_out),
    )
    grad_down, grad_gate_up, grad_qkv, grad_out = beside
    hc = hc.reshape(2, 8, D)
    grad_hc_weight = hc[:, 0:6].transpose(0, 2, 1)
    grad_hc_static = hc[:, 6, : 8 * STREAMS].reshape(2, STREAMS, 8)[:, :, 0:6]
    return (
        out[None],
        grad_state[None],
        grad_qkv,
        grad_out,
        grad_gate_up,
        grad_down,
        grad_hc_weight,
        grad_hc_static,
    )


def solution(mesh):
    return jax.shard_map(
        on_device,
        mesh=mesh,
        in_specs=(
            P("fsdp", "ctx", None),
            P("fsdp", "ctx", None),
            P(("ctx", "fsdp"), None),
            P(("ctx", "fsdp"), None),
            P(("ctx", "fsdp"), None),
            P(("ctx", "fsdp"), None),
            P(),
            P(),
            P(),
            P(),
        ),
        out_specs=(
            P("fsdp", "ctx", None),
            P("fsdp", "ctx", None),
            P(("ctx", "fsdp"), None),
            P(("ctx", "fsdp"), None),
            P(("ctx", "fsdp"), None),
            P(("ctx", "fsdp"), None),
            P(),
            P(),
        ),
        check_vma=False,
    )
```
